32 devices in a mesh: groups: 2 (over y), section: 4 (over z), fsdp: 4 (over x, core).
Axes of the slice: x: 2, y: 2, z: 4, core: 2. Of those that a mesh axis runs over, the one named last changes fastest.
Arguments:
- sent_act: bfloat16 [4, 1024, 4096], P('section', 'groups', 'fsdp'), parts along dimension 1, may hold values from -6 to 6
- sent_grad: bfloat16 [4, 1024, 4096], P('section', 'groups', 'fsdp'), parts along dimension 1, may hold values from -6 to 6
- stash_in: bfloat16 [4, 2, 1024, 4096], P('section', None, 'groups', 'fsdp'), parts along dimension 2, may hold values from -6 to 6
- stash_pre: bfloat16 [4, 2, 1024, 4096], P('section', None, 'groups', 'fsdp'), parts along dimension 2, may hold values from -6 to 6
- layer_weight: bfloat16 [4, 4096, 4096], P('section', None, 'fsdp'), may hold values from -0.125 to 0.125
- layer_bias: float32 [4, 4096], P('section', 'fsdp'), may hold values from -3 to 3
- seg_table: bfloat16 [4784, 4096], P('section', 'fsdp'), may hold values from -6 to 6
- seg_index: int32 [1024, 32], P('groups'), parts along dimension 0, may hold values from 0 to 4783
- seg_amp: float32 [1024, 32], P('groups'), parts along dimension 0, may hold values from -1.2 to 1.2
- field_angle: float32 [1024, 2], P('groups'), parts along dimension 0, may hold values from -1 to 1
- angle_weight: float32 [2, 4096], P(None, 'fsdp'), may hold values from -3 to 3
- target: bfloat16 [1024, 4096], P('groups', 'fsdp'), parts along dimension 0, may hold values from -6 to 6
- sched: int32 [4], P('section'), may hold values from 0 to 1
Outputs:
- fwd_out: bfloat16 [4, 1024, 4096], P('section', 'groups', 'fsdp'), parts along dimension 1
- grad_in: bfloat16 [4, 1024, 4096], P('section', 'groups', 'fsdp'), parts along dimension 1
- grad_w: bfloat16 [4, 8192, 4096], P('section', 'groups', 'fsdp'), parts along dimension 1
- grad_bias: float32 [4, 8192], P('section', ('groups', 'fsdp')), parts along dimension 1
The draws below stay inside these ranges and needn't reach their ends.
There are 2 independent parts, one for each index of `groups`. The reference program is written for one: setup_inputs(seed, part) draws one part's arguments, and reference() takes and returns one part's arrays. A program takes and returns all parts, laid end to end along the dimension named above; an argument that names none is the same for every part. Nothing has to cross between parts.
All inputs are finite; a program needn't handle non-finite values.
Results may differ from the reference program's by a relative error of at most 0.017.
Values may be sent and summed in bfloat16 or wider, within the bound.
No kernel may reach another device: no remote copies, remote signals or barrier semaphores. Data moves between devices by JAX's collectives and lax.ppermute only.
A program may use at most 128 MiB of HBM per device.

```python
import jax
import jax.numpy as jnp
from jax import lax

D = 4096
NSEG = 4784
KACT = 32
MB = 512
NSTASH = 2
N_SECTION = 4
N_FSDP = 4


def draw_sched(key, part):
    offset = jax.random.randint(key, (), 0, NSTASH)
    return jnp.mod(jnp.arange(N_SECTION, dtype=jnp.int32) + offset, NSTASH).astype(jnp.int32)


def draw_sent_grad(key, part):
    noise_key = jax.random.fold_in(key, 11)
    column_key = jax.random.fold_in(key, 12)
    noise = jax.random.normal(noise_key, (N_SECTION, MB, D), jnp.float32)
    column = 0.5 * jax.random.normal(column_key, (N_SECTION, 1, D), jnp.float32)
    return jnp.clip(noise + column, -6.0, 6.0).astype(jnp.bfloat16)


def with_ends(entries, stream_key, least, top_value):
    longest = entries.shape.index(max(entries.shape))
    spots = []
    for shift in (0, 1):
        where = [jax.random.randint(jax.random.fold_in(stream_key, axis), (), 0, length) for axis, length in enumerate(entries.shape)]
        where[longest] = (where[longest] + shift) % entries.shape[longest]
        spots.append(tuple(where))
    return entries.at[spots[0]].set(least).at[spots[1]].set(top_value)


def strengthened(array, own_key, source, target, parts, factor):
    owner, partner = [(jnp.arange(array.shape[dim]) // (array.shape[dim] // parts)).reshape([-1 if axis == dim else 1 for axis in range(array.ndim)]) for dim in (source, target)]
    chosen = jax.random.permutation(own_key, parts)[partner]
    strong = (owner == chosen) | (owner == (partner + parts // 2) % parts)
    return jnp.where(strong, factor * array, array)


def block_levels(key, extent, shards, smallest, high):
    def one(position, blocks):
        steps = jax.random.uniform(jax.random.fold_in(jax.random.fold_in(key, 6), position), (blocks,), jnp.float32, smallest / len(shards), high / len(shards))
        return jnp.repeat(jnp.exp(steps), extent[position] // blocks).reshape((-1,) + (1,) * (len(extent) - position - 1))

    factor_of = one(*shards[0])
    for cut in shards[1:]:
        factor_of = factor_of * one(*cut)
    return factor_of


def bell_draw(key, dims, scale, reach, pieces=(), kind=jnp.bfloat16):
    values = scale * jax.random.normal(key, dims, jnp.float32)
    if pieces:
        values = values * block_levels(key, dims, pieces, -0.22, 0.18)
    return jnp.clip(values, -reach, reach).astype(kind)


def noise_with(rng, extent, scale, bound, shards, heavy, kind=jnp.bfloat16):
    array = scale * jax.random.normal(rng, extent, jnp.float32)
    if shards:
        array = array * block_levels(rng, extent, shards, -0.22, 0.18)
    return jnp.clip(strengthened(array, jax.random.fold_in(rng, 3), *heavy), -bound, bound).astype(kind)


def setup_inputs(seed: int = 0, part: int = 0) -> dict:
    splits = jax.random.split(jax.random.key(seed), 14)
    part_splits = jax.random.split(jax.random.fold_in(splits[13], part), 14)
    return {
        "sent_act": bell_draw(part_splits[0], (N_SECTION, MB, D), 1.0, 6.0, ((0, 4), (2, 4))),
        "sent_grad": draw_sent_grad(jax.random.fold_in(jax.random.fold_in(splits[13], part), 71), part),
        "stash_in": bell_draw(part_splits[2], (N_SECTION, NSTASH, MB, D), 1.0, 6.0, ((0, 4), (3, 4))),
        "stash_pre": bell_draw(part_splits[3], (N_SECTION, NSTASH, MB, D), 1.0, 6.0, ((0, 4), (3, 4))),
        "layer_weight": noise_with(splits[4], (N_SECTION, D, D), D ** -0.5, 0.125, ((0, 4), (2, 4)), (2, 1, 4, 2.0)),
        "layer_bias": bell_draw(splits[5], (N_SECTION, D), 0.5, 3.0, ((0, 4), (1, 4)), jnp.float32),
        "seg_table": bell_draw(splits[6], (NSEG, D), 1.0, 6.0, ((0, 4), (1, 4))),
        "seg_index": with_ends(jax.random.randint(part_splits[7], (MB, KACT), 0, NSEG), jax.random.fold_in(part_splits[7], 1), 0, NSEG - 1).astype(jnp.int32),
        "seg_amp": bell_draw(part_splits[8], (MB, KACT), 0.2, 1.2, (), jnp.float32),
        "field_angle": jnp.clip(jax.random.uniform(part_splits[9], (MB, 2), jnp.float32, -1.0, 1.0), -1.0, 1.0),
        "angle_weight": bell_draw(splits[10], (2, D), 0.5, 3.0, ((1, 4),), jnp.float32),
        "target": bell_draw(part_splits[11], (MB, D), 1.0, 6.0, ((1, 4),)),
        "sched": draw_sched(jax.random.fold_in(splits[13], 71), part),
    }


def gelu_back(stashed_pre, target_rows, cotangent_in, is_last):
    stashed_f32 = stashed_pre.astype(jnp.float32)
    stashed_act, pullback = jax.vjp(jax.nn.gelu, stashed_f32)
    if is_last:
        cotangent = stashed_act - target_rows.astype(jnp.float32)
    else:
        cotangent = cotangent_in.astype(jnp.float32)
    return pullback(cotangent)[0].astype(jnp.bfloat16)

def reference(sent_act, sent_grad, stash_in, stash_pre, layer_weight, layer_bias, seg_table, seg_index, seg_amp, field_angle, angle_weight, target, sched):
    embedded = jnp.zeros((MB, D), jnp.float32)
    for column in range(KACT):
        picked = jnp.take(seg_table, seg_index[:, column], axis=0).astype(jnp.float32)
        embedded = embedded + seg_amp[:, column:column + 1] * picked
    angular = jnp.dot(field_angle, angle_weight, precision=lax.Precision.HIGHEST)
    first_input = (embedded + angular).astype(jnp.bfloat16)
    width = D // N_FSDP
    outputs, input_grads, weight_grads, bias_grads = ([], [], [], [])
    for section_num in range(N_SECTION):
        layer_input = first_input if section_num == 0 else sent_act[section_num - 1]
        preact = jnp.dot(layer_input, layer_weight[section_num], preferred_element_type=jnp.float32) + layer_bias[section_num]
        outputs.append(jax.nn.gelu(preact).astype(jnp.bfloat16))
        stash_slot = sched[section_num]
        stashed_in = stash_in[section_num][stash_slot]
        stashed_pre = stash_pre[section_num][stash_slot]
        following = sent_grad[min(section_num + 1, N_SECTION - 1)]
        pre_grad = gelu_back(stashed_pre, target, following, section_num == N_SECTION - 1)
        weight_grads.append(jnp.dot(stashed_in.T, pre_grad, preferred_element_type=jnp.float32).astype(jnp.bfloat16))
        bias_grads.append(lax.optimization_barrier(jnp.sum(pre_grad.astype(jnp.float32), axis=0)))
        summed = jnp.zeros((MB, D), jnp.float32)
        for shard_num in range(N_FSDP):
            lower = shard_num * width
            input_part = jnp.dot(pre_grad[:, lower:lower + width], layer_weight[section_num][:, lower:lower + width].T, preferred_element_type=jnp.float32).astype(jnp.bfloat16)
            summed = summed + input_part.astype(jnp.float32)
        input_grads.append(summed.astype(jnp.bfloat16))
    return (jnp.stack(outputs), jnp.stack(input_grads), jnp.stack(weight_grads), jnp.stack(bias_grads))
```

```python
import functools

import jax
import jax.numpy as jnp
from jax import lax
from jax.experimental import pallas as pl
from jax.experimental.pallas import tpu as pltpu
from jax.sharding import PartitionSpec as P

F32 = jnp.float32
BF16 = jnp.bfloat16
LANES = 128
GROUP = 8
CORES = 2


def over(axis, shard, pairs):
    return lax.ppermute(shard, axis, pairs)


def swap_cores(shard):
    count = lax.axis_size("fsdp")
    return over("fsdp", shard, [(i, i ^ 1) for i in range(count)])


def to_chip(shard, by):
    count = lax.axis_size("fsdp")
    return over("fsdp", shard, [(i, (i + CORES * by) % count) for i in range(count)])


def lookup_kernel(place, idx, amp, fa, aw, table, out, code, low_part, high, low, spread, upper, lower, edge):
    rows = table.shape[0]
    high_count = spread.shape[1] // LANES
    groups, lanes = idx.shape
    per_sample = lanes // GROUP
    whole = rows // LANES * LANES
    rest = rows - whole

    @pl.when(pl.program_id(0) == 0)
    def build():
        local_row = idx[...] - place[0]
        inside = (local_row >= 0) & (local_row < rows)
        sample = lax.broadcasted_iota(jnp.int32, idx.shape, 1) // per_sample
        code[...] = jnp.where(inside, (local_row // LANES) * GROUP + sample, -1)
        low_part[...] = local_row % LANES
        high[...] = amp[...].astype(BF16).astype(F32)
        low[...] = amp[...] - high[...]
        row_id = lax.broadcasted_iota(jnp.int32, (high_count * GROUP, lanes), 0)
        lane_id = lax.broadcasted_iota(jnp.int32, (LANES, lanes), 0)

        def one(group, unused):
            here = pl.ds(group, 1)
            matched = code[here, :] == row_id
            left_high = jnp.where(matched, high[here, :], 0.0).astype(BF16)
            left_low = jnp.where(matched, low[here, :], 0.0).astype(BF16)
            right = jnp.where(low_part[here, :] == lane_id, 1.0, 0.0).astype(BF16)
            dims = (((1,), (1,)), ((), ()))
            summed = lax.dot_general(left_high, right, dims, preferred_element_type=F32)
            summed += lax.dot_general(left_low, right, dims, preferred_element_type=F32)
            for k in range(high_count):
                spread[pl.ds(pl.multiple_of(group * GROUP, GROUP), GROUP), k * LANES:(k + 1) * LANES] = (
                    summed[k * GROUP:(k + 1) * GROUP, :]
                )
            return unused

        lax.fori_loop(0, groups, one, 0, unroll=4)
        values = spread[...]
        upper[...] = values.astype(BF16)
        lower[...] = (values - upper[...].astype(F32)).astype(BF16)

    total = jnp.zeros(out.shape, F32)
    if whole:
        total += jnp.dot(upper[:, :whole], table[:whole, :], preferred_element_type=F32)
        total += jnp.dot(lower[:, :whole], table[:whole, :], preferred_element_type=F32)
    if rest:
        edge[...] = jnp.zeros(edge.shape, BF16)
        edge[:rest, :] = table[whole:, :]
        total += jnp.dot(upper[:, whole:], edge[...], preferred_element_type=F32)
        total += jnp.dot(lower[:, whole:], edge[...], preferred_element_type=F32)
    angular = fa[:, 0:1] * aw[0:1, :] + fa[:, 1:2] * aw[1:2, :]
    out[...] = total + jnp.where(place[1] == 1, angular, 0.0)


def lookup_sum(table, seg_index, seg_amp, field_angle, angle_weight, section):
    rows, width = table.shape
    samples, active = seg_index.shape
    groups, lanes = samples // GROUP, GROUP * active
    high_count = -(-rows // LANES)
    block = min(width, 256)
    place = jnp.stack([section * rows, (section == 0).astype(jnp.int32)]).astype(jnp.int32)
    small = pl.BlockSpec((groups, lanes), lambda n, place: (0, 0))
    return pl.pallas_call(
        lookup_kernel,
        grid_spec=pltpu.PrefetchScalarGridSpec(
            num_scalar_prefetch=1,
            grid=(width // block,),
            in_specs=[
                small,
                small,
                pl.BlockSpec((samples, 2), lambda n, place: (0, 0)),
                pl.BlockSpec((2, block), lambda n, place: (0, n)),
                pl.BlockSpec((rows, block), lambda n, place: (0, n)),
            ],
            out_specs=pl.BlockSpec((samples, block), lambda n, place: (0, n)),
            scratch_shapes=[
                pltpu.VMEM((groups, lanes), jnp.int32),
                pltpu.VMEM((groups, lanes), jnp.int32),
                pltpu.VMEM((groups, lanes), F32),
                pltpu.VMEM((groups, lanes), F32),
                pltpu.VMEM((samples, high_count * LANES), F32),
                pltpu.VMEM((samples, high_count * LANES), BF16),
                pltpu.VMEM((samples, high_count * LANES), BF16),
                pltpu.VMEM((LANES, block), BF16),
            ],
        ),
        out_shape=jax.ShapeDtypeStruct((samples, width), F32),
        compiler_params=pltpu.CompilerParams(vmem_limit_bytes=24 << 20),
        cost_estimate=pl.CostEstimate(
            flops=4 * samples * rows * width, bytes_accessed=2 * rows * width + 4 * samples * width, transcendentals=0
        ),
        name="lookup_sum",
    )(
        place,
        seg_index.reshape(groups, lanes),
        seg_amp.reshape(groups, lanes),
        field_angle,
        angle_weight,
        table,
    )


def terms_kernel(ids, grad, first, second, first_out, second_out):
    dims = (((1,), (1,)), ((), ()))
    first_out[...] = lax.dot_general(grad[...], first[...], dims, preferred_element_type=F32).astype(BF16)
    second_out[...] = lax.dot_general(grad[...], second[...], dims, preferred_element_type=F32).astype(BF16)


def terms(grad, weight, ids):
    rows, width = grad.shape
    block = min(width, 512)
    steps = width // block
    shape = jax.ShapeDtypeStruct((rows, width), BF16)
    out_spec = pl.BlockSpec((rows, block), lambda n, ids: (0, n))
    return pl.pallas_call(
        terms_kernel,
        grid_spec=pltpu.PrefetchScalarGridSpec(
            num_scalar_prefetch=1,
            grid=(steps,),
            in_specs=[
                pl.BlockSpec((rows, width), lambda n, ids: (0, 0)),
                pl.BlockSpec((block, width), lambda n, ids: (ids[0] * steps + n, 0)),
                pl.BlockSpec((block, width), lambda n, ids: (ids[1] * steps + n, 0)),
            ],
            out_specs=[out_spec, out_spec],
        ),
        out_shape=[shape, shape],
        compiler_params=pltpu.CompilerParams(vmem_limit_bytes=20 << 20),
        cost_estimate=pl.CostEstimate(
            flops=4 * rows * width * width, bytes_accessed=4 * width * width + 6 * rows * width, transcendentals=0
        ),
        name="input_terms",
    )(ids, grad, weight, weight)


def forward_kernel(finish, ids, a, b, first, second, carry, out):
    total = carry[...] + jnp.dot(a[...], first[...], preferred_element_type=F32)
    total += jnp.dot(b[...], second[...], preferred_element_type=F32)
    if finish:
        total = jax.nn.gelu(total)
    out[...] = total.astype(out.dtype)


def forward_step(a, b, weight, ids, carry, finish):
    rows, width = a.shape
    block = min(width, 512)
    piece = pl.BlockSpec((rows, width), lambda n, ids: (0, 0))
    return pl.pallas_call(
        functools.partial(forward_kernel, finish),
        grid_spec=pltpu.PrefetchScalarGridSpec(
            num_scalar_prefetch=1,
            grid=(width // block,),
            in_specs=[
                piece,
                piece,
                pl.BlockSpec((width, block), lambda n, ids: (ids[0], n)),
                pl.BlockSpec((width, block), lambda n, ids: (ids[1], n)),
                pl.BlockSpec((carry.shape[0], block), lambda n, ids: (0, n)),
            ],
            out_specs=pl.BlockSpec((rows, block), lambda n, ids: (0, n)),
        ),
        out_shape=jax.ShapeDtypeStruct((rows, width), BF16 if finish else F32),
        compiler_params=pltpu.CompilerParams(vmem_limit_bytes=24 << 20),
        cost_estimate=pl.CostEstimate(
            flops=4 * rows * width * width, bytes_accessed=4 * width * width + 8 * rows * width, transcendentals=0
        ),
        name="forward_step",
    )(ids, a, b, weight, weight, carry)


def chained_sum(partial, section, chunks):
    sections = lax.axis_size("section")
    size = partial.shape[0] // chunks
    arrived = None
    landed = []
    for wave in range(chunks + sections - 2):
        piece = jnp.clip(wave - (sections - 1 - section), 0, chunks - 1)
        own = lax.dynamic_slice_in_dim(partial, piece * size, size, 0)
        if arrived is not None:
            own = own + arrived.astype(F32)
        pairs = [(s, s - 1) for s in range(1, sections) if 0 <= wave - (sections - 1 - s) < chunks]
        arrived = over("section", own.astype(BF16), pairs)
        if wave >= sections - 2:
            landed.append(arrived)
    return landed


def local(
    sent_act,
    sent_grad,
    stash_in,
    stash_pre,
    layer_weight,
    layer_bias,
    seg_table,
    seg_index,
    seg_amp,
    field_angle,
    angle_weight,
    target,
    sched,
):
    section = lax.axis_index("section")
    sections = lax.axis_size("section")
    me = lax.axis_index("fsdp")
    count = lax.axis_size("fsdp")
    chips = count // CORES
    rows = sent_act.shape[1]
    halves = 2
    half = rows // halves
    weight = layer_weight[0]

    def blocks(by):
        base = lax.rem(me // CORES + by, chips) * CORES
        mine = base + lax.rem(me, CORES)
        return mine, mine + 1 - 2 * lax.rem(me, CORES)

    def pair_ids(first, second):
        return jnp.stack([first, second]).astype(jnp.int32)

    slot = sched[0]
    stashed_in = lax.dynamic_index_in_dim(stash_in[0], slot, 0, keepdims=False)
    stashed_pre = lax.dynamic_index_in_dim(stash_pre[0], slot, 0, keepdims=False)
    stashed_full = lax.all_gather(stashed_in, "fsdp", axis=1, tiled=True)

    down = [(s, s - 1) for s in range(1, sections)]
    up = [(s, s + 1) for s in range(sections - 1)]
    from_next = [over("section", sent_grad[0, h * half:(h + 1) * half], down) for h in range(halves)]
    from_before = over("section", sent_act[0], up)

    partial = lookup_sum(seg_table, seg_index, seg_amp, field_angle, angle_weight, section)

    stashed_act, pullback = jax.vjp(jax.nn.gelu, stashed_pre.astype(F32))
    slope = pullback(jnp.ones_like(stashed_act))[0]
    missed = stashed_act - target.astype(F32)
    slope, missed = lax.optimization_barrier((slope, missed))

    grads, returned = [], []
    for h in range(halves):
        span = slice(h * half, (h + 1) * half)
        cotangent = jnp.where(section == sections - 1, missed[span], from_next[h].astype(F32))
        grad = (cotangent * slope[span]).astype(BF16)
        grads.append(grad)
        received = []
        for by in range(1, chips):
            mine, other = blocks(by)
            to_other, kept = terms(grad, weight, pair_ids(other, mine))
            both = (kept.astype(F32) + swap_cores(to_other).astype(F32)).astype(BF16)
            received.append(to_chip(both, by))
        returned.append(received)
    pre_grad = jnp.concatenate(grads, axis=0)
    grad_bias = jnp.sum(pre_grad.astype(F32), axis=0)
    mine, other = blocks(0)
    to_other, kept = terms(pre_grad, weight, pair_ids(other, mine))
    near = kept.astype(F32) + swap_cores(to_other).astype(F32)
    far = jnp.concatenate([sum(part.astype(F32) for part in received) for received in returned], axis=0)
    grad_in = (near + far).astype(BF16)

    landed = jnp.concatenate(chained_sum(partial, section, 4), axis=0)
    first_input = (partial + landed.astype(F32)).astype(BF16)
    layer_input = jnp.where(section == 0, first_input, from_before)
    bias = layer_bias
    total = forward_step(layer_input, swap_cores(layer_input), weight, pair_ids(mine, other), bias, False)
    outs = []
    for h in range(halves):
        span = slice(h * half, (h + 1) * half)
        carry = total[span]
        for by in range(1, chips):
            arrived = to_chip(layer_input[span], chips - by)
            mine, other = blocks(by)
            carry = forward_step(
                arrived, swap_cores(arrived), weight, pair_ids(mine, other), carry, by == chips - 1
            )
        outs.append(carry)
    fwd_out = jnp.concatenate(outs, axis=0)

    grad_w = lax.dot_general(
        stashed_full, pre_grad, (((0,), (0,)), ((), ())), preferred_element_type=F32
    ).astype(BF16)
    return (fwd_out[None], grad_in[None], grad_w[None], grad_bias[None])


def solution(mesh):
    return jax.shard_map(
        local,
        mesh=mesh,
        in_specs=(
            P("section", "groups", "fsdp"),
            P("section", "groups", "fsdp"),
            P("section", None, "groups", "fsdp"),
            P("section", None, "groups", "fsdp"),
            P("section", None, "fsdp"),
            P("section", "fsdp"),
            P("section", "fsdp"),
            P("groups", None),
            P("groups", None),
            P("groups", None),
            P(None, "fsdp"),
            P("groups", "fsdp"),
            P("section"),
        ),
        out_specs=(
            P("section", "groups", "fsdp"),
            P("section", "groups", "fsdp"),
            P("section", "groups", "fsdp"),
            P("section", ("groups", "fsdp")),
        ),
        check_vma=False,
    )
```

```python
import functools

import jax
import jax.numpy as jnp
from jax import lax
from jax.experimental import pallas as pl
from jax.experimental.pallas import tpu as pltpu
from jax.sharding import PartitionSpec as P

F32 = jnp.float32
BF16 = jnp.bfloat16
LANES = 128
GROUP = 8
CORES = 2


def over(axis, shard, pairs):
    return lax.ppermute(shard, axis, pairs)


def swap_cores(shard):
    count = lax.axis_size("fsdp")
    return over("fsdp", shard, [(i, i ^ 1) for i in range(count)])


def to_chip(shard, by):
    count = lax.axis_size("fsdp")
    return over("fsdp", shard, [(i, (i + CORES * by) % count) for i in range(count)])


FREE = pl.CostEstimate(flops=0, bytes_accessed=0, transcendentals=0)
ANYWHERE = pl.BlockSpec(memory_space=pl.ANY)


def params(mib):
    return pltpu.CompilerParams(vmem_limit_bytes=mib << 20)


def amplitude_kernel(rows, place, idx, amp, upper, lower, code, low_part, high, low, spread):
    high_count = spread.shape[1] // LANES
    groups, lanes = idx.shape
    per_sample = lanes // GROUP
    local_row = idx[...] - place[0]
    inside = (local_row >= 0) & (local_row < rows)
    sample = lax.broadcasted_iota(jnp.int32, idx.shape, 1) // per_sample
    code[...] = jnp.where(inside, (local_row // LANES) * GROUP + sample, -1)
    low_part[...] = local_row % LANES
    high[...] = amp[...].astype(BF16).astype(F32)
    low[...] = amp[...] - high[...]
    row_id = lax.broadcasted_iota(jnp.int32, (high_count * GROUP, lanes), 0)
    lane_id = lax.broadcasted_iota(jnp.int32, (LANES, lanes), 0)

    def one(group, unused):
        here = pl.ds(group, 1)
        matched = code[here, :] == row_id
        left_high = jnp.where(matched, high[here, :], 0.0).astype(BF16)
        left_low = jnp.where(matched, low[here, :], 0.0).astype(BF16)
        right = jnp.where(low_part[here, :] == lane_id, 1.0, 0.0).astype(BF16)
        dims = (((1,), (1,)), ((), ()))
        summed = lax.dot_general(left_high, right, dims, preferred_element_type=F32)
        summed += lax.dot_general(left_low, right, dims, preferred_element_type=F32)
        for k in range(high_count):
            spread[pl.ds(pl.multiple_of(group * GROUP, GROUP), GROUP), k * LANES:(k + 1) * LANES] = (
                summed[k * GROUP:(k + 1) * GROUP, :]
            )
        return unused

    lax.fori_loop(0, groups, one, 0, unroll=4)
    values = spread[...]
    upper[...] = values.astype(BF16)
    lower[...] = (values - upper[...].astype(F32)).astype(BF16)


def amplitudes(rows, seg_index, seg_amp, place):
    samples, active = seg_index.shape
    groups, lanes = samples // GROUP, GROUP * active
    columns = -(-rows // LANES) * LANES
    small = pl.BlockSpec((groups, lanes), lambda n, place: (0, 0))
    wide = pl.BlockSpec((samples, columns), lambda n, place: (0, 0))
    return pl.pallas_call(
        functools.partial(amplitude_kernel, rows),
        grid_spec=pltpu.PrefetchScalarGridSpec(
            num_scalar_prefetch=1,
            grid=(1,),
            in_specs=[small, small],
            out_specs=[wide, wide],
            scratch_shapes=[
                pltpu.VMEM((groups, lanes), jnp.int32),
                pltpu.VMEM((groups, lanes), jnp.int32),
                pltpu.VMEM((groups, lanes), F32),
                pltpu.VMEM((groups, lanes), F32),
                pltpu.VMEM((samples, columns), F32),
            ],
        ),
        out_shape=[jax.ShapeDtypeStruct((samples, columns), BF16)] * 2,
        compiler_params=params(20),
        cost_estimate=FREE,
        name="amplitudes",
    )(place, seg_index.reshape(groups, lanes), seg_amp.reshape(groups, lanes))


def lookup_kernel(place, upper, lower, fa, aw, table, held_back, after, later, out, passed, edge):
    rows = table.shape[0]
    whole = rows // LANES * LANES
    rest = rows - whole
    total = jnp.zeros(out.shape, F32)
    if whole:
        total += jnp.dot(upper[:, :whole], table[:whole, :], preferred_element_type=F32)
        total += jnp.dot(lower[:, :whole], table[:whole, :], preferred_element_type=F32)
    if rest:
        edge[...] = jnp.zeros(edge.shape, BF16)
        edge[:rest, :] = table[whole:, :]
        total += jnp.dot(upper[:, whole:], edge[...], preferred_element_type=F32)
        total += jnp.dot(lower[:, whole:], edge[...], preferred_element_type=F32)
    angular = fa[:, 0:1] * aw[0:1, :] + fa[:, 1:2] * aw[1:2, :]
    out[...] = total + jnp.where(place[1] == 1, angular, 0.0)
    passed[...] = held_back[...]


def lookup_sum(table, split, field_angle, angle_weight, place, gradient, half, after, later):
    rows, width = table.shape
    samples, columns = split[0].shape
    block = min(width, 256)
    return pl.pallas_call(
        lookup_kernel,
        grid_spec=pltpu.PrefetchScalarGridSpec(
            num_scalar_prefetch=1,
            grid=(width // block,),
            in_specs=[
                pl.BlockSpec((samples, columns), lambda n, place: (0, 0)),
                pl.BlockSpec((samples, columns), lambda n, place: (0, 0)),
                pl.BlockSpec((samples, 2), lambda n, place: (0, 0)),
                pl.BlockSpec((2, block), lambda n, place: (0, n)),
                pl.BlockSpec((rows, block), lambda n, place: (0, n)),
                pl.BlockSpec((half, block), lambda n, place: (1, n)),
                ANYWHERE,
                ANYWHERE,
            ],
            out_specs=[
                pl.BlockSpec((samples, block), lambda n, place: (0, n)),
                pl.BlockSpec((half, block), lambda n, place: (0, n)),
            ],
            scratch_shapes=[pltpu.VMEM((LANES, block), BF16)],
        ),
        out_shape=[jax.ShapeDtypeStruct((samples, width), F32), jax.ShapeDtypeStruct((half, width), BF16)],
        compiler_params=params(20),
        cost_estimate=FREE,
        name="lookup_sum",
    )(place, *split, field_angle, angle_weight, table, gradient, after, later)


NT = (((1,), (1,)), ((), ()))


def first_terms_kernel(last, ids, came, slope, missed, first, second, before, after, grad, first_out, second_out):
    @pl.when(pl.program_id(0) == 0)
    def differentiate():
        cotangent = jnp.where(last[0] == 1, missed[...], came[...].astype(F32))
        grad[...] = (cotangent * slope[...]).astype(BF16)

    first_out[...] = lax.dot_general(grad[...], first[...], NT, preferred_element_type=F32).astype(BF16)
    second_out[...] = lax.dot_general(grad[...], second[...], NT, preferred_element_type=F32).astype(BF16)


def first_terms(came, slope, missed, weight, last, ids, h, before, after):
    rows, width = came.shape
    block = min(width, 512)
    steps = width // block
    shape = jax.ShapeDtypeStruct((rows, width), BF16)
    whole = pl.BlockSpec((rows, width), lambda n, last, ids: (0, 0))
    span = pl.BlockSpec((rows, width), lambda n, last, ids: (h, 0))
    out_spec = pl.BlockSpec((rows, block), lambda n, last, ids: (0, n))
    return pl.pallas_call(
        first_terms_kernel,
        grid_spec=pltpu.PrefetchScalarGridSpec(
            num_scalar_prefetch=2,
            grid=(steps,),
            in_specs=[
                whole,
                span,
                span,
                pl.BlockSpec((block, width), lambda n, last, ids: (ids[0] * steps + n, 0)),
                pl.BlockSpec((block, width), lambda n, last, ids: (ids[1] * steps + n, 0)),
                ANYWHERE,
                ANYWHERE,
            ],
            out_specs=[span, out_spec, out_spec],
        ),
        out_shape=[jax.ShapeDtypeStruct(slope.shape, BF16), shape, shape],
        input_output_aliases={7: 0} if h else {},
        compiler_params=params(24),
        cost_estimate=FREE,
        name="gradient_terms",
    )(last, ids, came, slope, missed, weight, weight, before, after)


def terms_kernel(ids, grad, first, second, first_out, second_out):
    first_out[...] = lax.dot_general(grad[...], first[...], NT, preferred_element_type=F32).astype(BF16)
    second_out[...] = lax.dot_general(grad[...], second[...], NT, preferred_element_type=F32).astype(BF16)


def terms(grad, weight, ids, rows, h):
    width = grad.shape[1]
    block = min(width, 512)
    steps = width // block
    shape = jax.ShapeDtypeStruct((rows, width), BF16)
    out_spec = pl.BlockSpec((rows, block), lambda n, ids: (0, n))
    return pl.pallas_call(
        terms_kernel,
        grid_spec=pltpu.PrefetchScalarGridSpec(
            num_scalar_prefetch=1,
            grid=(steps,),
            in_specs=[
                pl.BlockSpec((rows, width), lambda n, ids: (h, 0)),
                pl.BlockSpec((block, width), lambda n, ids: (ids[0] * steps + n, 0)),
                pl.BlockSpec((block, width), lambda n, ids: (ids[1] * steps + n, 0)),
            ],
            out_specs=[out_spec, out_spec],
        ),
        out_shape=[shape, shape],
        compiler_params=params(20),
        cost_estimate=FREE,
        name="input_terms",
    )(ids, grad, weight, weight)


def merge_kernel(first, came, partial, *refs):
    *landed, out = refs
    size = landed[0].shape[0]
    for k, piece in enumerate(landed):
        span = slice(k * size, (k + 1) * size)
        summed = (partial[span, :] + piece[...].astype(F32)).astype(BF16)
        out[span, :] = jnp.where(first[0] == 1, summed, came[span, :])


def merge(first, came, partial, landed, half, h):
    width = came.shape[1]
    size = landed[0].shape[0]
    span = pl.BlockSpec((half, width), lambda n, first: (h, 0))
    piece = pl.BlockSpec((size, width), lambda n, first: (0, 0))
    return pl.pallas_call(
        merge_kernel,
        grid_spec=pltpu.PrefetchScalarGridSpec(
            num_scalar_prefetch=1,
            grid=(1,),
            in_specs=[span, span] + [piece] * len(landed),
            out_specs=pl.BlockSpec((half, width), lambda n, first: (0, 0)),
        ),
        out_shape=jax.ShapeDtypeStruct((half, width), BF16),
        compiler_params=params(20),
        cost_estimate=FREE,
        name="layer_input",
    )(first, came, partial, *landed)


def forward_kernel(finish, ids, a, b, first, second, carry, before, after, out):
    total = carry[...] + jnp.dot(a[...], first[...], preferred_element_type=F32)
    total += jnp.dot(b[...], second[...], preferred_element_type=F32)
    if finish:
        total = jax.nn.gelu(total)
    out[...] = total.astype(out.dtype)


def forward_step(a, b, weight, ids, carry, rows, h, finish, before, after):
    half, width = a.shape
    block = min(width, 512)
    piece = pl.BlockSpec((half, width), lambda n, ids: (0, 0))
    out_rows, place = (rows, h) if finish else (half, 0)
    return pl.pallas_call(
        functools.partial(forward_kernel, finish),
        grid_spec=pltpu.PrefetchScalarGridSpec(
            num_scalar_prefetch=1,
            grid=(width // block,),
            in_specs=[
                piece,
                piece,
                pl.BlockSpec((width, block), lambda n, ids: (ids[0], n)),
                pl.BlockSpec((width, block), lambda n, ids: (ids[1], n)),
                pl.BlockSpec((carry.shape[0], block), lambda n, ids: (0, n)),
                ANYWHERE,
                ANYWHERE,
            ],
            out_specs=pl.BlockSpec((half, block), lambda n, ids: (place, n)),
        ),
        out_shape=jax.ShapeDtypeStruct((out_rows, width), BF16 if finish else F32),
        input_output_aliases={6: 0} if finish and h else {},
        compiler_params=params(24),
        cost_estimate=FREE,
        name="forward_step",
    )(ids, a, b, weight, weight, carry, before, after)


def chained_sum(partial, section, chunks):
    sections = lax.axis_size("section")
    size = partial.shape[0] // chunks
    arrived = None
    landed = []
    for wave in range(chunks + sections - 2):
        piece = jnp.clip(wave - (sections - 1 - section), 0, chunks - 1)
        own = lax.dynamic_slice_in_dim(partial, piece * size, size, 0)
        if arrived is not None:
            own = own + arrived.astype(F32)
        pairs = [(s, s - 1) for s in range(1, sections) if 0 <= wave - (sections - 1 - s) < chunks]
        arrived = over("section", own.astype(BF16), pairs)
        if wave >= sections - 2:
            landed.append(arrived)
    return landed


def local(
    sent_act,
    sent_grad,
    stash_in,
    stash_pre,
    layer_weight,
    layer_bias,
    seg_table,
    seg_index,
    seg_amp,
    field_angle,
    angle_weight,
    target,
    sched,
):
    section = lax.axis_index("section")
    sections = lax.axis_size("section")
    me = lax.axis_index("fsdp")
    count = lax.axis_size("fsdp")
    chips = count // CORES
    rows = sent_act.shape[1]
    halves = 2
    half = rows // halves
    weight = layer_weight[0]

    def blocks(by):
        base = lax.rem(me // CORES + by, chips) * CORES
        mine = base + lax.rem(me, CORES)
        return mine, mine + 1 - 2 * lax.rem(me, CORES)

    def pair_ids(first, second):
        return jnp.stack([first, second]).astype(jnp.int32)

    is_first = (section == 0).astype(jnp.int32)
    is_last = (section == sections - 1).astype(jnp.int32)[None]
    place = jnp.stack([section * seg_table.shape[0], is_first]).astype(jnp.int32)
    slot = sched[0]
    stashed_in = lax.dynamic_index_in_dim(stash_in[0], slot, 0, keepdims=False)
    stashed_pre = lax.dynamic_index_in_dim(stash_pre[0], slot, 0, keepdims=False)
    stashed_full = lax.all_gather(stashed_in, "fsdp", axis=1, tiled=True)

    down = [(s, s - 1) for s in range(1, sections)]
    up = [(s, s + 1) for s in range(sections - 1)]
    from_before = over("section", sent_act[0], up)
    early = over("section", sent_grad[0, :half], down)

    split = amplitudes(seg_table.shape[0], seg_index, seg_amp, place)
    stashed_act, pullback = jax.vjp(jax.nn.gelu, stashed_pre.astype(F32))
    slope = pullback(jnp.ones_like(stashed_act))[0]
    missed = stashed_act - target.astype(F32)
    slope, missed = lax.optimization_barrier((slope, missed))

    partial, held_back = lookup_sum(
        seg_table, split, field_angle, angle_weight, place, sent_grad[0], half, early, slope
    )
    late = over("section", held_back, down)

    pre_grad = place
    returned = []
    for h, came in enumerate((early, late)):
        received = []
        for by in range(1, chips):
            mine, other = blocks(by)
            ids = pair_ids(other, mine)
            if by == 1:
                pre_grad, to_other, kept = first_terms(
                    came, slope, missed, weight, is_last, ids, h, pre_grad, from_before if h else place
                )
            else:
                to_other, kept = terms(pre_grad, weight, ids, half, h)
            both = (kept.astype(F32) + swap_cores(to_other).astype(F32)).astype(BF16)
            received.append(to_chip(both, by))
        returned.append(received)
    grad_bias = jnp.sum(pre_grad.astype(F32), axis=0)
    mine, other = blocks(0)
    to_other, kept = terms(pre_grad, weight, pair_ids(other, mine), rows, 0)
    near = kept.astype(F32) + swap_cores(to_other).astype(F32)
    far = jnp.concatenate([sum(part.astype(F32) for part in received) for received in returned], axis=0)
    grad_in = (near + far).astype(BF16)

    chunks = 4
    landed = chained_sum(partial, section, chunks)
    inputs = []
    for h in range(halves):
        pieces = landed[h * chunks // halves:(h + 1) * chunks // halves]
        inputs.append(merge(is_first[None], from_before, partial, pieces, half, h))
    grad_w = lax.dot_general(
        stashed_full, pre_grad, (((0,), (0,)), ((), ())), preferred_element_type=F32
    ).astype(BF16)
    fwd_out = place
    for h in range(halves):
        mine, other = blocks(0)
        carry = forward_step(
            inputs[h], swap_cores(inputs[h]), weight, pair_ids(mine, other), layer_bias, rows, h, False, place, place
        )
        for by in range(1, chips):
            arrived = to_chip(inputs[h], chips - by)
            mine, other = blocks(by)
            carry = forward_step(
                arrived,
                swap_cores(arrived),
                weight,
                pair_ids(mine, other),
                carry,
                rows,
                h,
                by == chips - 1,
                fwd_out,
                grad_w if h else grad_in,
            )
        fwd_out = carry
    return (fwd_out[None], grad_in[None], grad_w[None], grad_bias[None])


def solution(mesh):
    return jax.shard_map(
        local,
        mesh=mesh,
        in_specs=(
            P("section", "groups", "fsdp"),
            P("section", "groups", "fsdp"),
            P("section", None, "groups", "fsdp"),
            P("section", None, "groups", "fsdp"),
            P("section", None, "fsdp"),
            P("section", "fsdp"),
            P("section", "fsdp"),
            P("groups", None),
            P("groups", None),
            P("groups", None),
            P(None, "fsdp"),
            P("groups", "fsdp"),
            P("section"),
        ),
        out_specs=(
            P("section", "groups", "fsdp"),
            P("section", "groups", "fsdp"),
            P("section", "groups", "fsdp"),
            P("section", ("groups", "fsdp")),
        ),
        check_vma=False,
    )
```

```python
import functools

import jax
import jax.numpy as jnp
from jax import lax
from jax.experimental import pallas as pl
from jax.experimental.pallas import tpu as pltpu
from jax.sharding import PartitionSpec as P

F32 = jnp.float32
BF16 = jnp.bfloat16
LANES = 128
GROUP = 8
CORES = 2


def over(axis, shard, pairs):
    return lax.ppermute(shard, axis, pairs)


def swap_cores(shard):
    count = lax.axis_size("fsdp")
    return over("fsdp", shard, [(i, i ^ 1) for i in range(count)])


def to_chip(shard, by):
    count = lax.axis_size("fsdp")
    return over("fsdp", shard, [(i, (i + CORES * by) % count) for i in range(count)])


FREE = pl.CostEstimate(flops=0, bytes_accessed=0, transcendentals=0)
ANYWHERE = pl.BlockSpec(memory_space=pl.ANY)


def params():
    return pltpu.CompilerParams(vmem_limit_bytes=57 << 20)


def amplitude_kernel(rows, place, idx, amp, upper, lower, code, low_part, high, low, spread):
    high_count = spread.shape[1] // LANES
    groups, lanes = idx.shape
    per_sample = lanes // GROUP
    local_row = idx[...] - place[0]
    inside = (local_row >= 0) & (local_row < rows)
    sample = lax.broadcasted_iota(jnp.int32, idx.shape, 1) // per_sample
    code[...] = jnp.where(inside, (local_row // LANES) * GROUP + sample, -1)
    low_part[...] = local_row % LANES
    high[...] = amp[...].astype(BF16).astype(F32)
    low[...] = amp[...] - high[...]
    row_id = lax.broadcasted_iota(jnp.int32, (high_count * GROUP, lanes), 0)
    lane_id = lax.broadcasted_iota(jnp.int32, (LANES, lanes), 0)

    def one(group, unused):
        here = pl.ds(group, 1)
        matched = code[here, :] == row_id
        left_high = jnp.where(matched, high[here, :], 0.0).astype(BF16)
        left_low = jnp.where(matched, low[here, :], 0.0).astype(BF16)
        right = jnp.where(low_part[here, :] == lane_id, 1.0, 0.0).astype(BF16)
        dims = (((1,), (1,)), ((), ()))
        summed = lax.dot_general(left_high, right, dims, preferred_element_type=F32)
        summed += lax.dot_general(left_low, right, dims, preferred_element_type=F32)
        for k in range(high_count):
            spread[pl.ds(pl.multiple_of(group * GROUP, GROUP), GROUP), k * LANES:(k + 1) * LANES] = (
                summed[k * GROUP:(k + 1) * GROUP, :]
            )
        return unused

    lax.fori_loop(0, groups, one, 0, unroll=4)
    values = spread[...]
    upper[...] = values.astype(BF16)
    lower[...] = (values - upper[...].astype(F32)).astype(BF16)


def amplitudes(rows, seg_index, seg_amp, place):
    samples, active = seg_index.shape
    groups, lanes = samples // GROUP, GROUP * active
    columns = -(-rows // LANES) * LANES
    small = pl.BlockSpec((groups, lanes), lambda n, place: (0, 0))
    wide = pl.BlockSpec((samples, columns), lambda n, place: (0, 0))
    return pl.pallas_call(
        functools.partial(amplitude_kernel, rows),
        grid_spec=pltpu.PrefetchScalarGridSpec(
            num_scalar_prefetch=1,
            grid=(1,),
            in_specs=[small, small],
            out_specs=[wide, wide],
            scratch_shapes=[
                pltpu.VMEM((groups, lanes), jnp.int32),
                pltpu.VMEM((groups, lanes), jnp.int32),
                pltpu.VMEM((groups, lanes), F32),
                pltpu.VMEM((groups, lanes), F32),
                pltpu.VMEM((samples, columns), F32),
            ],
        ),
        out_shape=[jax.ShapeDtypeStruct((samples, columns), BF16)] * 2,
        compiler_params=params(),
        cost_estimate=FREE,
        name="amplitudes",
    )(place, seg_index.reshape(groups, lanes), seg_amp.reshape(groups, lanes))


def lookup_kernel(place, upper, lower, fa, aw, table, *refs):
    out, rounded, edge = refs[-3:]
    rows = table.shape[0]
    whole = rows // LANES * LANES
    rest = rows - whole
    total = jnp.zeros(out.shape, F32)
    if whole:
        total += jnp.dot(upper[:, :whole], table[:whole, :], preferred_element_type=F32)
        total += jnp.dot(lower[:, :whole], table[:whole, :], preferred_element_type=F32)
    if rest:
        edge[...] = jnp.zeros(edge.shape, BF16)
        edge[:rest, :] = table[whole:, :]
        total += jnp.dot(upper[:, whole:], edge[...], preferred_element_type=F32)
        total += jnp.dot(lower[:, whole:], edge[...], preferred_element_type=F32)
    angular = fa[:, 0:1] * aw[0:1, :] + fa[:, 1:2] * aw[1:2, :]
    total += jnp.where(place[1] == 1, angular, 0.0)
    out[...] = total
    rounded[...] = total.astype(BF16)


def lookup_sum(table, split, field_angle, angle_weight, place, half, h, after):
    rows, width = table.shape
    columns = split[0].shape[1]
    block = min(width, 256)
    span = pl.BlockSpec((half, columns), lambda n, place: (h, 0))
    out_spec = pl.BlockSpec((half, block), lambda n, place: (0, n))
    return pl.pallas_call(
        lookup_kernel,
        grid_spec=pltpu.PrefetchScalarGridSpec(
            num_scalar_prefetch=1,
            grid=(width // block,),
            in_specs=[
                span,
                span,
                pl.BlockSpec((half, 2), lambda n, place: (h, 0)),
                pl.BlockSpec((2, block), lambda n, place: (0, n)),
                pl.BlockSpec((rows, block), lambda n, place: (0, n)),
            ]
            + [ANYWHERE] * len(after),
            out_specs=[out_spec, out_spec],
            scratch_shapes=[pltpu.VMEM((LANES, block), BF16)],
        ),
        out_shape=[jax.ShapeDtypeStruct((half, width), F32), jax.ShapeDtypeStruct((half, width), BF16)],
        compiler_params=params(),
        cost_estimate=FREE,
        name="lookup_sum",
    )(place, *split, field_angle, angle_weight, table, *after)


NT = (((1,), (1,)), ((), ()))


def first_terms_kernel(where, ids, came, pre, target, first, second, after, grad, first_out, second_out):
    @pl.when(pl.program_id(0) == 0)
    def differentiate():
        act, pullback = jax.vjp(jax.nn.gelu, pre[0, 0].astype(F32))
        slope = pullback(jnp.ones_like(act))[0]
        cotangent = jnp.where(where[1] == 1, act - target[...].astype(F32), came[...].astype(F32))
        grad[...] = (cotangent * slope).astype(BF16)

    first_out[...] = lax.dot_general(grad[...], first[...], NT, preferred_element_type=F32).astype(BF16)
    second_out[...] = lax.dot_general(grad[...], second[...], NT, preferred_element_type=F32).astype(BF16)


def first_terms(came, stash_pre, target, weight, where, ids, after):
    rows, width = came.shape
    block = min(width, 256)
    steps = width // block
    shape = jax.ShapeDtypeStruct((rows, width), BF16)
    whole = pl.BlockSpec((rows, width), lambda n, where, ids: (0, 0))
    out_spec = pl.BlockSpec((rows, block), lambda n, where, ids: (0, n))
    return pl.pallas_call(
        first_terms_kernel,
        grid_spec=pltpu.PrefetchScalarGridSpec(
            num_scalar_prefetch=2,
            grid=(steps,),
            in_specs=[
                whole,
                pl.BlockSpec((1, 1, rows, width), lambda n, where, ids: (0, where[0], 0, 0)),
                whole,
                pl.BlockSpec((block, width), lambda n, where, ids: (ids[0] * steps + n, 0)),
                pl.BlockSpec((block, width), lambda n, where, ids: (ids[1] * steps + n, 0)),
                ANYWHERE,
            ],
            out_specs=[whole, out_spec, out_spec],
        ),
        out_shape=[shape, shape, shape],
        compiler_params=params(),
        cost_estimate=FREE,
        name="gradient_terms",
    )(where, ids, came, stash_pre, target, weight, weight, after)


def terms_kernel(ids, grad, first, second, after, first_out, second_out):
    first_out[...] = lax.dot_general(grad[...], first[...], NT, preferred_element_type=F32).astype(BF16)
    second_out[...] = lax.dot_general(grad[...], second[...], NT, preferred_element_type=F32).astype(BF16)


def terms(grad, weight, ids, after):
    rows, width = grad.shape
    block = min(width, 512)
    steps = width // block
    shape = jax.ShapeDtypeStruct((rows, width), BF16)
    out_spec = pl.BlockSpec((rows, block), lambda n, ids: (0, n))
    return pl.pallas_call(
        terms_kernel,
        grid_spec=pltpu.PrefetchScalarGridSpec(
            num_scalar_prefetch=1,
            grid=(steps,),
            in_specs=[
                pl.BlockSpec((rows, width), lambda n, ids: (0, 0)),
                pl.BlockSpec((block, width), lambda n, ids: (ids[0] * steps + n, 0)),
                pl.BlockSpec((block, width), lambda n, ids: (ids[1] * steps + n, 0)),
                ANYWHERE,
            ],
            out_specs=[out_spec, out_spec],
        ),
        out_shape=[shape, shape],
        compiler_params=params(),
        cost_estimate=FREE,
        name="input_terms",
    )(ids, grad, weight, weight, after)


def weight_grad_kernel(stashed, grad, after, later, out):
    dims = (((0,), (0,)), ((), ()))
    out[...] = lax.dot_general(stashed[...], grad[...], dims, preferred_element_type=F32).astype(BF16)


def weight_grad(stashed, grad, after, later):
    rows, features = stashed.shape
    width = grad.shape[1]
    block = 512
    return pl.pallas_call(
        weight_grad_kernel,
        grid=(features // block,),
        in_specs=[
            pl.BlockSpec((rows, block), lambda n: (0, n)),
            pl.BlockSpec((rows, width), lambda n: (0, 0)),
            ANYWHERE,
            ANYWHERE,
        ],
        out_specs=pl.BlockSpec((block, width), lambda n: (n, 0)),
        out_shape=jax.ShapeDtypeStruct((features, width), BF16),
        compiler_params=params(),
        cost_estimate=FREE,
        name="weight_grad",
    )(stashed, grad, after, later)


def merge_kernel(first, came, partial, after, later, *refs):
    *landed, out = refs
    total = partial[...]
    for piece in landed:
        total += piece[...].astype(F32)
    out[...] = jnp.where(first[0] == 1, total.astype(BF16), came[...])


def merge(first, came, partial, landed, h, after, later):
    half, width = partial.shape
    piece = pl.BlockSpec((half, width), lambda n, first: (0, 0))
    return pl.pallas_call(
        merge_kernel,
        grid_spec=pltpu.PrefetchScalarGridSpec(
            num_scalar_prefetch=1,
            grid=(1,),
            in_specs=[pl.BlockSpec((half, width), lambda n, first: (h, 0)), piece, ANYWHERE, ANYWHERE] + [piece] * len(landed),
            out_specs=piece,
        ),
        out_shape=jax.ShapeDtypeStruct((half, width), BF16),
        compiler_params=params(),
        cost_estimate=FREE,
        name="layer_input",
    )(first, came, partial, after, later, *landed)


def forward_kernel(finish, ids, a, b, first, second, carry, before, after, out):
    total = carry[...] + jnp.dot(a[...], first[...], preferred_element_type=F32)
    total += jnp.dot(b[...], second[...], preferred_element_type=F32)
    if finish:
        total = jax.nn.gelu(total)
    out[...] = total.astype(out.dtype)


def forward_step(a, b, weight, ids, carry, rows, h, finish, before, after):
    half, width = a.shape
    block = min(width, 512)
    piece = pl.BlockSpec((half, width), lambda n, ids: (0, 0))
    out_rows, place = (rows, h) if finish else (half, 0)
    return pl.pallas_call(
        functools.partial(forward_kernel, finish),
        grid_spec=pltpu.PrefetchScalarGridSpec(
            num_scalar_prefetch=1,
            grid=(width // block,),
            in_specs=[
                piece,
                piece,
                pl.BlockSpec((width, block), lambda n, ids: (ids[0], n)),
                pl.BlockSpec((width, block), lambda n, ids: (ids[1], n)),
                pl.BlockSpec((carry.shape[0], block), lambda n, ids: (0, n)),
                ANYWHERE,
                ANYWHERE,
            ],
            out_specs=pl.BlockSpec((half, block), lambda n, ids: (place, n)),
        ),
        out_shape=jax.ShapeDtypeStruct((out_rows, width), BF16 if finish else F32),
        input_output_aliases={6: 0} if finish and h else {},
        compiler_params=params(),
        cost_estimate=FREE,
        name="forward_step",
    )(ids, a, b, weight, weight, carry, before, after)


def tree_sum(partial, rounded):
    sections = lax.axis_size("section")
    landed = []
    stride = 1
    while stride < sections:
        arrived = over("section", rounded, [(s, s - stride) for s in range(stride, sections, 2 * stride)])
        landed.append(arrived)
        stride *= 2
        if stride < sections:
            rounded = (partial + sum(piece.astype(F32) for piece in landed)).astype(BF16)
    return landed, rounded


def local(
    sent_act,
    sent_grad,
    stash_in,
    stash_pre,
    layer_weight,
    layer_bias,
    seg_table,
    seg_index,
    seg_amp,
    field_angle,
    angle_weight,
    target,
    sched,
):
    section = lax.axis_index("section")
    sections = lax.axis_size("section")
    me = lax.axis_index("fsdp")
    count = lax.axis_size("fsdp")
    chips = count // CORES
    rows = sent_act.shape[1]
    halves = 2
    half = rows // halves
    weight = layer_weight[0]

    def blocks(by):
        base = lax.rem(me // CORES + by, chips) * CORES
        mine = base + lax.rem(me, CORES)
        return mine, mine + 1 - 2 * lax.rem(me, CORES)

    def pair_ids(first, second):
        return jnp.stack([first, second]).astype(jnp.int32)

    is_first = (section == 0).astype(jnp.int32)
    is_last = (section == sections - 1).astype(jnp.int32)
    place = jnp.stack([section * seg_table.shape[0], is_first]).astype(jnp.int32)
    where = jnp.stack([sched[0], is_last]).astype(jnp.int32)
    stashed_in = lax.dynamic_index_in_dim(stash_in[0], sched[0], 0, keepdims=False)
    stashed_full = lax.all_gather(stashed_in, "fsdp", axis=1, tiled=True)

    from_before = over("section", sent_act[0], [(s, s + 1) for s in range(sections - 1)])
    from_next = over("section", sent_grad[0], [(s, s - 1) for s in range(1, sections)])

    split = amplitudes(seg_table.shape[0], seg_index, seg_amp, place)
    sums = []
    for h in range(halves):
        after = (rounded, from_next, from_before) if h else ()
        partial, rounded = lookup_sum(seg_table, split, field_angle, angle_weight, place, half, h, after)
        sums.append((partial, *tree_sum(partial, rounded)))

    received = []
    for by in range(1, chips):
        mine, other = blocks(by)
        ids = pair_ids(other, mine)
        if by == 1:
            pre_grad, to_other, kept = first_terms(from_next, stash_pre, target, weight, where, ids, rounded)
        else:
            to_other, kept = terms(pre_grad, weight, ids, ids)
        both = (kept.astype(F32) + swap_cores(to_other).astype(F32)).astype(BF16)
        received.append(to_chip(both, by))
    grad_bias = jnp.sum(pre_grad.astype(F32), axis=0)
    mine, other = blocks(0)
    to_other, kept = terms(pre_grad, weight, pair_ids(other, mine), both)
    near = kept.astype(F32) + swap_cores(to_other).astype(F32)
    grad_in = (near + sum(part.astype(F32) for part in received)).astype(BF16)
    grad_w = weight_grad(stashed_full, pre_grad, kept, sums[0][2])

    inputs, carries, after = [], [], grad_w
    mine, other = blocks(0)
    for h, (partial, landed, unused) in enumerate(sums):
        inputs.append(merge(is_first[None], from_before, partial, landed, h, after, grad_in if h else place))
        after = forward_step(
            inputs[h], swap_cores(inputs[h]), weight, pair_ids(mine, other), layer_bias, rows, h, False, place, place
        )
        carries.append(after)
    fwd_out = place
    for h, carry in enumerate(carries):
        for by in range(1, chips):
            arrived = to_chip(inputs[h], chips - by)
            mine, other = blocks(by)
            if h:
                arrived, fwd_out = lax.optimization_barrier((arrived, fwd_out))
            carry = forward_step(
                arrived,
                swap_cores(arrived),
                weight,
                pair_ids(mine, other),
                carry,
                rows,
                h,
                by == chips - 1,
                fwd_out,
                place if h else carries[-1],
            )
        fwd_out = carry
    return (fwd_out[None], grad_in[None], grad_w[None], grad_bias[None])


def solution(mesh):
    return jax.shard_map(
        local,
        mesh=mesh,
        in_specs=(
            P("section", "groups", "fsdp"),
            P("section", "groups", "fsdp"),
            P("section", None, "groups", "fsdp"),
            P("section", None, "groups", "fsdp"),
            P("section", None, "fsdp"),
            P("section", "fsdp"),
            P("section", "fsdp"),
            P("groups", None),
            P("groups", None),
            P("groups", None),
            P(None, "fsdp"),
            P("groups", "fsdp"),
            P("section"),
        ),
        out_specs=(
            P("section", "groups", "fsdp"),
            P("section", "groups", "fsdp"),
            P("section", "groups", "fsdp"),
            P("section", ("groups", "fsdp")),
        ),
        check_vma=False,
    )
```

```python
import functools

import jax
import jax.numpy as jnp
from jax import lax
from jax.experimental import pallas as pl
from jax.experimental.pallas import tpu as pltpu
from jax.sharding import PartitionSpec as P

F32 = jnp.float32
BF16 = jnp.bfloat16
LANES = 128
GROUP = 8
CORES = 2


def over(axis, shard, pairs):
    return lax.ppermute(shard, axis, pairs)


def swap_cores(shard):
    count = lax.axis_size("fsdp")
    return over("fsdp", shard, [(i, i ^ 1) for i in range(count)])


def to_chip(shard, by):
    count = lax.axis_size("fsdp")
    return over("fsdp", shard, [(i, (i + CORES * by) % count) for i in range(count)])


def costs(micros):
    return pl.CostEstimate(flops=int(micros * 1.1e9), bytes_accessed=0, transcendentals=0)


ANYWHERE = pl.BlockSpec(memory_space=pl.ANY)


def params():
    return pltpu.CompilerParams(vmem_limit_bytes=24 << 20)


def lookup_kernel(place, idx, amp, fa, aw, table, out, rounded, code, low_part, high, low, spread, upper, lower, edge):
    rows = table.shape[0]
    whole = rows // LANES * LANES
    rest = rows - whole
    high_count = spread.shape[1] // LANES
    groups, lanes = idx.shape
    per_sample = lanes // GROUP

    @pl.when(pl.program_id(0) == 0)
    def build():
        local_row = idx[...] - place[0]
        inside = (local_row >= 0) & (local_row < rows)
        sample = lax.broadcasted_iota(jnp.int32, idx.shape, 1) // per_sample
        code[...] = jnp.where(inside, (local_row // LANES) * GROUP + sample, -1)
        low_part[...] = local_row % LANES
        high[...] = amp[...].astype(BF16).astype(F32)
        low[...] = amp[...] - high[...]
        row_id = lax.broadcasted_iota(jnp.int32, (high_count * GROUP, lanes), 0)
        lane_id = lax.broadcasted_iota(jnp.int32, (LANES, lanes), 0)

        def one(group, unused):
            here = pl.ds(group, 1)
            matched = code[here, :] == row_id
            left_high = jnp.where(matched, high[here, :], 0.0).astype(BF16)
            left_low = jnp.where(matched, low[here, :], 0.0).astype(BF16)
            right = jnp.where(low_part[here, :] == lane_id, 1.0, 0.0).astype(BF16)
            summed = lax.dot_general(left_high, right, NT, preferred_element_type=F32)
            summed += lax.dot_general(left_low, right, NT, preferred_element_type=F32)
            for k in range(high_count):
                spread[pl.ds(pl.multiple_of(group * GROUP, GROUP), GROUP), k * LANES:(k + 1) * LANES] = (
                    summed[k * GROUP:(k + 1) * GROUP, :]
                )
            return unused

        lax.fori_loop(0, groups, one, 0, unroll=4)
        values = spread[...]
        upper[...] = values.astype(BF16)
        lower[...] = (values - upper[...].astype(F32)).astype(BF16)

    total = jnp.zeros(out.shape, F32)
    if whole:
        total += jnp.dot(upper[:, :whole], table[:whole, :], preferred_element_type=F32)
        total += jnp.dot(lower[:, :whole], table[:whole, :], preferred_element_type=F32)
    if rest:
        edge[...] = jnp.zeros(edge.shape, BF16)
        edge[:rest, :] = table[whole:, :]
        total += jnp.dot(upper[:, whole:], edge[...], preferred_element_type=F32)
        total += jnp.dot(lower[:, whole:], edge[...], preferred_element_type=F32)
    angular = fa[:, 0:1] * aw[0:1, :] + fa[:, 1:2] * aw[1:2, :]
    total += jnp.where(place[1] == 1, angular, 0.0)
    out[...] = total
    rounded[...] = total.astype(BF16)


def lookup_sum(table, seg_index, seg_amp, field_angle, angle_weight, place):
    rows, width = table.shape
    samples, active = seg_index.shape
    groups, lanes = samples // GROUP, GROUP * active
    columns = -(-rows // LANES) * LANES
    block = min(width, 256)
    small = pl.BlockSpec((groups, lanes), lambda n, place: (0, 0))
    out_spec = pl.BlockSpec((samples, block), lambda n, place: (0, n))
    return pl.pallas_call(
        lookup_kernel,
        grid_spec=pltpu.PrefetchScalarGridSpec(
            num_scalar_prefetch=1,
            grid=(width // block,),
            in_specs=[
                small,
                small,
                pl.BlockSpec((samples, 2), lambda n, place: (0, 0)),
                pl.BlockSpec((2, block), lambda n, place: (0, n)),
                pl.BlockSpec((rows, block), lambda n, place: (0, n)),
            ],
            out_specs=[out_spec, out_spec],
            scratch_shapes=[
                pltpu.VMEM((groups, lanes), jnp.int32),
                pltpu.VMEM((groups, lanes), jnp.int32),
                pltpu.VMEM((groups, lanes), F32),
                pltpu.VMEM((groups, lanes), F32),
                pltpu.VMEM((samples, columns), F32),
                pltpu.VMEM((samples, columns), BF16),
                pltpu.VMEM((samples, columns), BF16),
                pltpu.VMEM((LANES, block), BF16),
            ],
        ),
        out_shape=[jax.ShapeDtypeStruct((samples, width), F32), jax.ShapeDtypeStruct((samples, width), BF16)],
        compiler_params=params(),
        cost_estimate=costs(11),
        name="lookup_sum",
    )(place, seg_index.reshape(groups, lanes), seg_amp.reshape(groups, lanes), field_angle, angle_weight, table)


NT = (((1,), (1,)), ((), ()))


def first_terms_kernel(where, ids, came, pre, target, first, second, after, later, grad, upper_out, lower_out, second_out):
    piece = 32

    @pl.when(pl.program_id(0) == 0)
    def differentiate():
        def one(k, unused):
            span = pl.ds(pl.multiple_of(k * piece, piece), piece)
            act, pullback = jax.vjp(jax.nn.gelu, pre[0, 0, span, :].astype(F32))
            slope = pullback(jnp.ones_like(act))[0]
            missed = act - target[span, :].astype(F32)
            cotangent = jnp.where(where[1] == 1, missed, came[span, :].astype(F32))
            grad[span, :] = (cotangent * slope).astype(BF16)
            return unused

        lax.fori_loop(0, grad.shape[0] // piece, one, 0)

    half = upper_out.shape[0]
    going = lax.dot_general(grad[...], first[...], NT, preferred_element_type=F32).astype(BF16)
    upper_out[...] = going[:half]
    lower_out[...] = going[half:]
    second_out[...] = lax.dot_general(grad[...], second[...], NT, preferred_element_type=F32).astype(BF16)


def first_terms(came, stash_pre, target, weight, where, ids, after, later):
    rows, width = came.shape
    block = min(width, 256)
    steps = width // block
    shape = jax.ShapeDtypeStruct((rows, width), BF16)
    whole = pl.BlockSpec((rows, width), lambda n, where, ids: (0, 0))
    out_spec = pl.BlockSpec((rows, block), lambda n, where, ids: (0, n))
    half_spec = pl.BlockSpec((rows // 2, block), lambda n, where, ids: (0, n))
    half_shape = jax.ShapeDtypeStruct((rows // 2, width), BF16)
    return pl.pallas_call(
        first_terms_kernel,
        grid_spec=pltpu.PrefetchScalarGridSpec(
            num_scalar_prefetch=2,
            grid=(steps,),
            in_specs=[
                whole,
                pl.BlockSpec((1, 1, rows, width), lambda n, where, ids: (0, where[0], 0, 0)),
                whole,
                pl.BlockSpec((block, width), lambda n, where, ids: (ids[0] * steps + n, 0)),
                pl.BlockSpec((block, width), lambda n, where, ids: (ids[1] * steps + n, 0)),
                ANYWHERE,
                ANYWHERE,
            ],
            out_specs=[whole, half_spec, half_spec, out_spec],
        ),
        out_shape=[shape, half_shape, half_shape, shape],
        compiler_params=params(),
        cost_estimate=costs(0),
        name="gradient_terms",
    )(where, ids, came, stash_pre, target, weight, weight, after, later)


def terms_kernel(ids, grad, first, second, after, later, first_out, second_out):
    first_out[...] = lax.dot_general(grad[...], first[...], NT, preferred_element_type=F32).astype(BF16)
    second_out[...] = lax.dot_general(grad[...], second[...], NT, preferred_element_type=F32).astype(BF16)


def terms(grad, weight, ids, after, later):
    rows, width = grad.shape
    block = min(width, 512)
    steps = width // block
    shape = jax.ShapeDtypeStruct((rows, width), BF16)
    out_spec = pl.BlockSpec((rows, block), lambda n, ids: (0, n))
    return pl.pallas_call(
        terms_kernel,
        grid_spec=pltpu.PrefetchScalarGridSpec(
            num_scalar_prefetch=1,
            grid=(steps,),
            in_specs=[
                pl.BlockSpec((rows, width), lambda n, ids: (0, 0)),
                pl.BlockSpec((block, width), lambda n, ids: (ids[0] * steps + n, 0)),
                pl.BlockSpec((block, width), lambda n, ids: (ids[1] * steps + n, 0)),
                ANYWHERE,
                ANYWHERE,
            ],
            out_specs=[out_spec, out_spec],
        ),
        out_shape=[shape, shape],
        compiler_params=params(),
        cost_estimate=costs(0),
        name="input_terms",
    )(ids, grad, weight, weight, after, later)


def merge_kernel(first, came, partial, near, far, out):
    total = partial[...] + near[...].astype(F32) + far[...].astype(F32)
    out[...] = jnp.where(first[0] == 1, total.astype(BF16), came[...])


def merge(first, came, partial, near, far, h):
    half, width = far.shape
    span = pl.BlockSpec((half, width), lambda n, first: (h, 0))
    whole = pl.BlockSpec((half, width), lambda n, first: (0, 0))
    return pl.pallas_call(
        merge_kernel,
        grid_spec=pltpu.PrefetchScalarGridSpec(
            num_scalar_prefetch=1,
            grid=(1,),
            in_specs=[span, span, span, whole],
            out_specs=whole,
        ),
        out_shape=jax.ShapeDtypeStruct((half, width), BF16),
        compiler_params=params(),
        cost_estimate=costs(0),
        name="layer_input",
    )(first, came, partial, near, far)


def forward_kernel(finish, ids, a, b, first, second, carry, before, after, out):
    total = carry[...] + jnp.dot(a[...], first[...], preferred_element_type=F32)
    total += jnp.dot(b[...], second[...], preferred_element_type=F32)
    if finish:
        total = jax.nn.gelu(total)
    out[...] = total.astype(out.dtype)


def forward_step(a, b, weight, ids, carry, rows, h, finish, before, after):
    half, width = a.shape
    block = min(width, 512)
    piece = pl.BlockSpec((half, width), lambda n, ids: (0, 0))
    out_rows, place = (rows, h) if finish else (half, 0)
    return pl.pallas_call(
        functools.partial(forward_kernel, finish),
        grid_spec=pltpu.PrefetchScalarGridSpec(
            num_scalar_prefetch=1,
            grid=(width // block,),
            in_specs=[
                piece,
                piece,
                pl.BlockSpec((width, block), lambda n, ids: (ids[0], n)),
                pl.BlockSpec((width, block), lambda n, ids: (ids[1], n)),
                pl.BlockSpec((carry.shape[0], block), lambda n, ids: (0, n)),
                ANYWHERE,
                ANYWHERE,
            ],
            out_specs=pl.BlockSpec((half, block), lambda n, ids: (place, n)),
        ),
        out_shape=jax.ShapeDtypeStruct((out_rows, width), BF16 if finish else F32),
        input_output_aliases={6: 0} if finish and h else {},
        compiler_params=params(),
        cost_estimate=costs(0),
        name="forward_step",
    )(ids, a, b, weight, weight, carry, before, after)


def from_pair(shard):
    pairs = [[i, i + CORES] for i in range(CORES)]
    both = lax.all_gather(shard, "fsdp", axis=0, axis_index_groups=pairs)
    place = 1 - lax.axis_index("fsdp") // CORES
    return lax.dynamic_index_in_dim(both, place, 0, keepdims=False)


def step_down(shard, stride):
    sections = lax.axis_size("section")
    return over("section", shard, [(s, s - stride) for s in range(stride, sections, 2 * stride)])


def local(
    sent_act,
    sent_grad,
    stash_in,
    stash_pre,
    layer_weight,
    layer_bias,
    seg_table,
    seg_index,
    seg_amp,
    field_angle,
    angle_weight,
    target,
    sched,
):
    section = lax.axis_index("section")
    sections = lax.axis_size("section")
    me = lax.axis_index("fsdp")
    count = lax.axis_size("fsdp")
    chips = count // CORES
    rows = sent_act.shape[1]
    halves = 2
    half = rows // halves
    weight = layer_weight[0]

    def blocks(by):
        base = lax.rem(me // CORES + by, chips) * CORES
        mine = base + lax.rem(me, CORES)
        return mine, mine + 1 - 2 * lax.rem(me, CORES)

    def pair_ids(first, second):
        return jnp.stack([first, second]).astype(jnp.int32)

    is_first = (section == 0).astype(jnp.int32)
    is_last = (section == sections - 1).astype(jnp.int32)
    place = jnp.stack([section * seg_table.shape[0], is_first]).astype(jnp.int32)
    where = jnp.stack([sched[0], is_last]).astype(jnp.int32)
    stashed_in = lax.dynamic_index_in_dim(stash_in[0], sched[0], 0, keepdims=False)
    stashed_full = lax.all_gather(stashed_in, "fsdp", axis=1, tiled=True)

    from_before = over("section", sent_act[0], [(s, s + 1) for s in range(sections - 1)])
    from_next = over("section", sent_grad[0], [(s, s - 1) for s in range(1, sections)])
    partial, rounded = lookup_sum(seg_table, seg_index, seg_amp, field_angle, angle_weight, place)

    received = []
    for by in range(1, chips):
        mine, other = blocks(by)
        ids = pair_ids(other, mine)
        if by == 1:
            pre_grad, *to_other, kept = first_terms(
                from_next, stash_pre, target, weight, where, ids, rounded, from_before
            )
        else:
            to_other, kept = terms(pre_grad, weight, ids, ids, ids)
            to_other = [to_other]
        came = jnp.concatenate([swap_cores(piece) for piece in to_other], axis=0)
        both = (kept.astype(F32) + came.astype(F32)).astype(BF16)
        if by == 1:
            near, token = lax.optimization_barrier((step_down(rounded, 1), both))
        received.append(from_pair(both) if chips == 2 else to_chip(both, by))
    grad_bias = jnp.sum(pre_grad.astype(F32), axis=0)

    stride = 2
    while 2 * stride < sections:
        near = near.astype(F32) + step_down((partial + near.astype(F32)).astype(BF16), stride).astype(F32)
        stride *= 2
    leaving = partial + near.astype(F32)
    leaving = [leaving[h * half:(h + 1) * half].astype(BF16) for h in range(halves)]
    last = [step_down(piece, stride) for piece in leaving]

    grad_w = lax.dot_general(
        stashed_full, pre_grad, (((0,), (0,)), ((), ())), preferred_element_type=F32
    ).astype(BF16)
    last[0], grad_w = lax.optimization_barrier((last[0], grad_w))
    inputs, carries = [], []
    mine, other = blocks(0)
    for h in range(halves):
        inputs.append(merge(is_first[None], from_before, partial, near, last[h], h))
        if h == 0:
            to_other, kept = terms(pre_grad, weight, pair_ids(other, mine), inputs[0], token)
            last[1], to_other = lax.optimization_barrier((last[1], to_other))
        carry = forward_step(
            inputs[h], swap_cores(inputs[h]), weight, pair_ids(mine, other), layer_bias, rows, h, False, place, place
        )
        carries.append(carry)
    beside = kept.astype(F32) + swap_cores(to_other).astype(F32)
    grad_in = (beside + sum(part.astype(F32) for part in received)).astype(BF16)
    fwd_out = place
    for h, carry in enumerate(carries):
        for by in range(1, chips):
            arrived = to_chip(inputs[h], chips - by)
            mine, other = blocks(by)
            if h:
                arrived, fwd_out, grad_in = lax.optimization_barrier((arrived, fwd_out, grad_in))
            carry = forward_step(
                arrived,
                swap_cores(arrived),
                weight,
                pair_ids(mine, other),
                carry,
                rows,
                h,
                by == chips - 1,
                fwd_out,
                place if h else carries[-1],
            )
        fwd_out = carry
    return (fwd_out[None], grad_in[None], grad_w[None], grad_bias[None])


def solution(mesh):
    return jax.shard_map(
        local,
        mesh=mesh,
        in_specs=(
            P("section", "groups", "fsdp"),
            P("section", "groups", "fsdp"),
            P("section", None, "groups", "fsdp"),
            P("section", None, "groups", "fsdp"),
            P("section", None, "fsdp"),
            P("section", "fsdp"),
            P("section", "fsdp"),
            P("groups", None),
            P("groups", None),
            P("groups", None),
            P(None, "fsdp"),
            P("groups", "fsdp"),
            P("section"),
        ),
        out_specs=(
            P("section", "groups", "fsdp"),
            P("section", "groups", "fsdp"),
            P("section", "groups", "fsdp"),
            P("section", ("groups", "fsdp")),
        ),
        check_vma=False,
    )
```

```python
import functools

import jax
import jax.numpy as jnp
from jax import lax
from jax.experimental import pallas as pl
from jax.experimental.pallas import tpu as pltpu
from jax.sharding import PartitionSpec as P

F32 = jnp.float32
BF16 = jnp.bfloat16
LANES = 128
GROUP = 8
CORES = 2
ROW, FIRST, SLOT, LAST, BLOCKS = range(5)


def over(axis, shard, pairs):
    return lax.ppermute(shard, axis, pairs)


def swap_cores(shard):
    count = lax.axis_size("fsdp")
    return over("fsdp", shard, [(i, i ^ 1) for i in range(count)])


def to_chip(shard, by):
    count = lax.axis_size("fsdp")
    return over("fsdp", shard, [(i, (i + CORES * by) % count) for i in range(count)])


def costs(micros):
    return pl.CostEstimate(flops=int(micros * 1.1e9), bytes_accessed=0, transcendentals=0)


ANYWHERE = pl.BlockSpec(memory_space=pl.ANY)


def params():
    return pltpu.CompilerParams(vmem_limit_bytes=57 << 20)


def lookup_kernel(info, idx, amp, fa, aw, table, out, code, low_part, high, low, spread, split, edge):
    rows = table.shape[0]
    samples = out.shape[0]
    whole = rows // LANES * LANES
    rest = rows - whole
    high_count = spread.shape[1] // LANES
    groups, lanes = idx.shape
    per_sample = lanes // GROUP

    @pl.when(pl.program_id(0) == 0)
    def build():
        local_row = idx[...] - info[ROW]
        inside = (local_row >= 0) & (local_row < rows)
        sample = lax.broadcasted_iota(jnp.int32, idx.shape, 1) // per_sample
        code[...] = jnp.where(inside, (local_row // LANES) * GROUP + sample, -1)
        low_part[...] = local_row % LANES
        high[...] = amp[...].astype(BF16).astype(F32)
        low[...] = amp[...] - high[...]
        row_id = lax.broadcasted_iota(jnp.int32, (high_count * GROUP, lanes), 0)
        lane_id = lax.broadcasted_iota(jnp.int32, (LANES, lanes), 0)

        def one(group, unused):
            here = pl.ds(group, 1)
            matched = code[here, :] == row_id
            left_high = jnp.where(matched, high[here, :], 0.0).astype(BF16)
            left_low = jnp.where(matched, low[here, :], 0.0).astype(BF16)
            right = jnp.where(low_part[here, :] == lane_id, 1.0, 0.0).astype(BF16)
            left = jnp.concatenate([left_high, left_low], axis=0)
            summed = lax.dot_general(left, right, NT, preferred_element_type=F32)
            summed = summed[:high_count * GROUP] + summed[high_count * GROUP:]
            for k in range(high_count):
                spread[pl.ds(pl.multiple_of(group * GROUP, GROUP), GROUP), k * LANES:(k + 1) * LANES] = (
                    summed[k * GROUP:(k + 1) * GROUP, :]
                )
            return unused

        lax.fori_loop(0, groups, one, 0, unroll=8)
        values = spread[...]
        upper = values.astype(BF16)
        split[:samples, :] = upper
        split[samples:, :] = (values - upper.astype(F32)).astype(BF16)

    total = jnp.zeros((2 * samples, out.shape[1]), F32)
    if whole:
        total += jnp.dot(split[:, :whole], table[:whole, :], preferred_element_type=F32)
    if rest:
        edge[...] = jnp.zeros(edge.shape, BF16)
        edge[:rest, :] = table[whole:, :]
        total += jnp.dot(split[:, whole:], edge[...], preferred_element_type=F32)
    angular = fa[:, 0:1] * aw[0:1, :] + fa[:, 1:2] * aw[1:2, :]
    summed = total[:samples] + total[samples:] + jnp.where(info[FIRST] == 1, angular, 0.0)
    out[...] = summed.astype(BF16)


def lookup_sum(table, seg_index, seg_amp, field_angle, angle_weight, info):
    rows, width = table.shape
    samples, active = seg_index.shape
    groups, lanes = samples // GROUP, GROUP * active
    columns = -(-rows // LANES) * LANES
    block = min(width, 256)
    small = pl.BlockSpec((groups, lanes), lambda n, info: (0, 0))
    return pl.pallas_call(
        lookup_kernel,
        grid_spec=pltpu.PrefetchScalarGridSpec(
            num_scalar_prefetch=1,
            grid=(width // block,),
            in_specs=[
                small,
                small,
                pl.BlockSpec((samples, 2), lambda n, info: (0, 0)),
                pl.BlockSpec((2, block), lambda n, info: (0, n)),
                pl.BlockSpec((rows, block), lambda n, info: (0, n)),
            ],
            out_specs=pl.BlockSpec((samples, block), lambda n, info: (0, n)),
            scratch_shapes=[
                pltpu.VMEM((groups, lanes), jnp.int32),
                pltpu.VMEM((groups, lanes), jnp.int32),
                pltpu.VMEM((groups, lanes), F32),
                pltpu.VMEM((groups, lanes), F32),
                pltpu.VMEM((samples, columns), F32),
                pltpu.VMEM((2 * samples, columns), BF16),
                pltpu.VMEM((LANES, block), BF16),
            ],
        ),
        out_shape=jax.ShapeDtypeStruct((samples, width), BF16),
        compiler_params=params(),
        cost_estimate=costs(11),
        name="lookup_sum",
    )(info, seg_index.reshape(groups, lanes), seg_amp.reshape(groups, lanes), field_angle, angle_weight, table)


NT = (((1,), (1,)), ((), ()))


def cuts(rows):
    return [rows // 8 * 3, rows - rows // 8 * 3]


def first_terms_kernel(info, came, pre, target, first, second, after, later, grad, *outs):
    piece = 32

    @pl.when(pl.program_id(0) == 0)
    def differentiate():
        def one(k, unused):
            span = pl.ds(pl.multiple_of(k * piece, piece), piece)
            act, pullback = jax.vjp(jax.nn.gelu, pre[0, 0, span, :].astype(F32))
            slope = pullback(jnp.ones_like(act))[0]
            missed = act - target[span, :].astype(F32)
            cotangent = jnp.where(info[LAST] == 1, missed, came[span, :].astype(F32))
            grad[span, :] = (cotangent * slope).astype(BF16)
            return unused

        lax.fori_loop(0, grad.shape[0] // piece, one, 0)

    cut = outs[0].shape[0]
    for block, (upper, lower) in zip((first, second), (outs[:2], outs[2:])):
        term = lax.dot_general(grad[...], block[...], NT, preferred_element_type=F32).astype(BF16)
        upper[...] = term[:cut]
        lower[...] = term[cut:]


def first_terms(came, stash_pre, target, weight, info, at, after, later):
    rows, width = came.shape
    block = min(width, 256)
    steps = width // block
    pieces = cuts(rows) * 2
    shapes = [jax.ShapeDtypeStruct((piece, width), BF16) for piece in pieces]
    whole = pl.BlockSpec((rows, width), lambda n, info: (0, 0))
    out_specs = [pl.BlockSpec((piece, block), lambda n, info: (0, n)) for piece in pieces]
    return pl.pallas_call(
        first_terms_kernel,
        grid_spec=pltpu.PrefetchScalarGridSpec(
            num_scalar_prefetch=1,
            grid=(steps,),
            in_specs=[
                whole,
                pl.BlockSpec((1, 1, rows, width), lambda n, info: (0, info[SLOT], 0, 0)),
                whole,
                pl.BlockSpec((block, width), lambda n, info: (info[at + 1] * steps + n, 0)),
                pl.BlockSpec((block, width), lambda n, info: (info[at] * steps + n, 0)),
                ANYWHERE,
                ANYWHERE,
            ],
            out_specs=[whole] + out_specs,
        ),
        out_shape=[jax.ShapeDtypeStruct((rows, width), BF16)] + shapes,
        compiler_params=params(),
        cost_estimate=costs(0),
        name="gradient_terms",
    )(info, came, stash_pre, target, weight, weight, after, later)


def terms_kernel(info, grad, first, second, after, later, first_out, second_out):
    first_out[...] = lax.dot_general(grad[...], first[...], NT, preferred_element_type=F32).astype(BF16)
    second_out[...] = lax.dot_general(grad[...], second[...], NT, preferred_element_type=F32).astype(BF16)


def terms(grad, weight, info, at, after, later):
    rows, width = grad.shape
    block = min(width, 256)
    steps = width // block
    shape = jax.ShapeDtypeStruct((rows, width), BF16)
    out_spec = pl.BlockSpec((rows, block), lambda n, info: (0, n))
    return pl.pallas_call(
        terms_kernel,
        grid_spec=pltpu.PrefetchScalarGridSpec(
            num_scalar_prefetch=1,
            grid=(steps,),
            in_specs=[
                pl.BlockSpec((rows, width), lambda n, info: (0, 0)),
                pl.BlockSpec((block, width), lambda n, info: (info[at + 1] * steps + n, 0)),
                pl.BlockSpec((block, width), lambda n, info: (info[at] * steps + n, 0)),
                ANYWHERE,
                ANYWHERE,
            ],
            out_specs=[out_spec, out_spec],
        ),
        out_shape=[shape, shape],
        compiler_params=params(),
        cost_estimate=costs(0),
        name="input_terms",
    )(info, grad, weight, weight, after, later)


def forward_kernel(finish, info, a, b, first, second, carry, before, after, out):
    total = carry[...] + jnp.dot(a[...], first[...], preferred_element_type=F32)
    total += jnp.dot(b[...], second[...], preferred_element_type=F32)
    if finish:
        total = jax.nn.gelu(total)
    out[...] = total.astype(out.dtype)


def forward_step(a, b, weight, info, at, carry, rows, h, finish, before, after):
    half, width = a.shape
    block = min(width, 256)
    piece = pl.BlockSpec((half, width), lambda n, info: (0, 0))
    out_rows, place = (rows, h) if finish else (half, 0)
    return pl.pallas_call(
        functools.partial(forward_kernel, finish),
        grid_spec=pltpu.PrefetchScalarGridSpec(
            num_scalar_prefetch=1,
            grid=(width // block,),
            in_specs=[
                piece,
                piece,
                pl.BlockSpec((width, block), lambda n, info: (info[at], n)),
                pl.BlockSpec((width, block), lambda n, info: (info[at + 1], n)),
                pl.BlockSpec((carry.shape[0], block), lambda n, info: (0, n)),
                ANYWHERE,
                ANYWHERE,
            ],
            out_specs=pl.BlockSpec((half, block), lambda n, info: (place, n)),
        ),
        out_shape=jax.ShapeDtypeStruct((out_rows, width), BF16 if finish else F32),
        input_output_aliases={6: 0} if finish and h else {},
        compiler_params=params(),
        cost_estimate=costs(0),
        name="forward_step",
    )(info, a, b, weight, weight, carry, before, after)


def step_down(shard, stride):
    sections = lax.axis_size("section")
    return over("section", shard, [(s, s - stride) for s in range(stride, sections, 2 * stride)])


def local(
    sent_act,
    sent_grad,
    stash_in,
    stash_pre,
    layer_weight,
    layer_bias,
    seg_table,
    seg_index,
    seg_amp,
    field_angle,
    angle_weight,
    target,
    sched,
):
    section = lax.axis_index("section")
    sections = lax.axis_size("section")
    me = lax.axis_index("fsdp")
    count = lax.axis_size("fsdp")
    chips = count // CORES
    rows = sent_act.shape[1]
    halves = 2
    half = rows // halves
    weight = layer_weight[0]

    numbers = [section * seg_table.shape[0], section == 0, sched[0], section == sections - 1]
    for by in range(chips):
        base = lax.rem(me // CORES + by, chips) * CORES
        core = lax.rem(me, CORES)
        numbers += [base + core, base + 1 - core]
    info = jnp.stack([jnp.asarray(number, jnp.int32) for number in numbers])
    is_first = section == 0
    stashed_in = lax.dynamic_index_in_dim(stash_in[0], sched[0], 0, keepdims=False)
    stashed_full = lax.all_gather(stashed_in, "fsdp", axis=1, tiled=True)

    from_before = over("section", sent_act[0], [(s, s + 1) for s in range(sections - 1)])
    from_next = over("section", sent_grad[0], [(s, s - 1) for s in range(1, sections)])
    rounded = lookup_sum(seg_table, seg_index, seg_amp, field_angle, angle_weight, info)

    received = []
    for by in range(1, chips):
        at = BLOCKS + 2 * by
        if by == 1:
            pre_grad, *terms_out = first_terms(
                from_next, stash_pre, target, weight, info, at, rounded, from_before
            )
            to_other, kept = terms_out[:2], terms_out[2:]
        else:
            to_other, kept = [
                [term[:cuts(rows)[0]], term[cuts(rows)[0]:]]
                for term in terms(pre_grad, weight, info, at, info, info)
            ]
        received.append([
            to_chip((mine.astype(F32) + swap_cores(other).astype(F32)).astype(BF16), by)
            for mine, other in zip(kept, to_other)
        ])
    grad_bias = jnp.sum(pre_grad.astype(F32), axis=0)

    near = step_down(rounded, 1)
    near, received[0][0] = lax.optimization_barrier((near, received[0][0]))
    total = (rounded.astype(F32) + near.astype(F32)).astype(BF16)
    stride = 2
    while 2 * stride < sections:
        total = (total.astype(F32) + step_down(total, stride).astype(F32)).astype(BF16)
        stride *= 2
    leaving = [total[h * half:(h + 1) * half] for h in range(halves)]
    grad_w = lax.dot_general(
        stashed_full, pre_grad, (((0,), (0,)), ((), ())), preferred_element_type=F32
    ).astype(BF16)
    last = [step_down(leaving[0], stride)]
    leaving[1], grad_w = lax.optimization_barrier((leaving[1], grad_w))
    last.append(step_down(leaving[1], stride))
    last[0], received[0][1], grad_w = lax.optimization_barrier((last[0], received[0][1], grad_w))

    inputs, carries = [], []
    for h in range(halves):
        first_input = (leaving[h].astype(F32) + last[h].astype(F32)).astype(BF16)
        inputs.append(jnp.where(is_first, first_input, from_before[h * half:(h + 1) * half]))
        carry = forward_step(
            inputs[h], swap_cores(inputs[h]), weight, info, BLOCKS, layer_bias, rows, h, False, info, info
        )
        if h == 0:
            to_other, kept = terms(pre_grad, weight, info, BLOCKS, inputs[0], info)
            last[1], to_other, carry = lax.optimization_barrier((last[1], to_other, carry))
        carries.append(carry)
    beside = kept.astype(F32) + swap_cores(to_other).astype(F32)
    far = [sum(part[h].astype(F32) for part in received) for h in range(2)]
    grad_in = (beside + jnp.concatenate(far, axis=0)).astype(BF16)
    fwd_out = info
    for h, carry in enumerate(carries):
        for by in range(1, chips):
            arrived = to_chip(inputs[h], chips - by)
            if h:
                arrived, fwd_out, grad_in = lax.optimization_barrier((arrived, fwd_out, grad_in))
            carry = forward_step(
                arrived,
                swap_cores(arrived),
                weight,
                info,
                BLOCKS + 2 * by,
                carry,
                rows,
                h,
                by == chips - 1,
                fwd_out,
                info if h else carries[-1],
            )
        fwd_out = carry
    return (fwd_out[None], grad_in[None], grad_w[None], grad_bias[None])


def solution(mesh):
    return jax.shard_map(
        local,
        mesh=mesh,
        in_specs=(
            P("section", "groups", "fsdp"),
            P("section", "groups", "fsdp"),
            P("section", None, "groups", "fsdp"),
            P("section", None, "groups", "fsdp"),
            P("section", None, "fsdp"),
            P("section", "fsdp"),
            P("section", "fsdp"),
            P("groups", None),
            P("groups", None),
            P("groups", None),
            P(None, "fsdp"),
            P("groups", "fsdp"),
            P("section"),
        ),
        out_specs=(
            P("section", "groups", "fsdp"),
            P("section", "groups", "fsdp"),
            P("section", "groups", "fsdp"),
            P("section", ("groups", "fsdp")),
        ),
        check_vma=False,
    )
```

```python
import functools

import jax
import jax.numpy as jnp
from jax import lax
from jax.experimental import pallas as pl
from jax.experimental.pallas import tpu as pltpu
from jax.sharding import PartitionSpec as P

F32 = jnp.float32
BF16 = jnp.bfloat16
LANES = 128
GROUP = 8
CORES = 2
ROW, FIRST, SLOT, LAST, BLOCKS = range(5)


def over(axis, shard, pairs):
    return lax.ppermute(shard, axis, pairs)


def swap_cores(shard):
    count = lax.axis_size("fsdp")
    return over("fsdp", shard, [(i, i ^ 1) for i in range(count)])


def to_chip(shard, by):
    count = lax.axis_size("fsdp")
    return over("fsdp", shard, [(i, (i + CORES * by) % count) for i in range(count)])


def costs(flops, moved):
    return pl.CostEstimate(flops=flops, bytes_accessed=moved, transcendentals=0)


ANYWHERE = pl.BlockSpec(memory_space=pl.ANY)


def params():
    return pltpu.CompilerParams(vmem_limit_bytes=20 << 20)


def lookup_kernel(info, idx, amp, fa, aw, table, out, code, low_part, high, low, spread, split, edge):
    rows = table.shape[0]
    whole = rows // LANES * LANES
    rest = rows - whole
    high_count = spread.shape[1] // LANES
    groups, lanes = idx.shape
    per_sample = lanes // GROUP

    @pl.when(pl.program_id(0) == 0)
    def build():
        local_row = idx[...] - info[ROW]
        inside = (local_row >= 0) & (local_row < rows)
        sample = lax.broadcasted_iota(jnp.int32, idx.shape, 1) // per_sample
        code[...] = jnp.where(inside, (local_row // LANES) * GROUP + sample, -1)
        low_part[...] = local_row % LANES
        high[...] = amp[...].astype(BF16).astype(F32)
        low[...] = amp[...] - high[...]
        row_id = lax.broadcasted_iota(jnp.int32, (high_count * GROUP, lanes), 0)
        lane_id = lax.broadcasted_iota(jnp.int32, (LANES, lanes), 0)

        def one(group, unused):
            here = pl.ds(group, 1)
            matched = code[here, :] == row_id
            left_high = jnp.where(matched, high[here, :], 0.0).astype(BF16)
            left_low = jnp.where(matched, low[here, :], 0.0).astype(BF16)
            right = jnp.where(low_part[here, :] == lane_id, 1.0, 0.0).astype(BF16)
            left = jnp.concatenate([left_high, left_low], axis=0)
            summed = lax.dot_general(left, right, NT, preferred_element_type=F32)
            summed = summed[:high_count * GROUP] + summed[high_count * GROUP:]
            for k in range(high_count):
                spread[pl.ds(pl.multiple_of(group * GROUP, GROUP), GROUP), k * LANES:(k + 1) * LANES] = (
                    summed[k * GROUP:(k + 1) * GROUP, :]
                )
            return unused

        lax.fori_loop(0, groups, one, 0, unroll=8)
        split[...] = spread[...].astype(BF16)

    angular = fa[:, 0:1] * aw[0:1, :] + fa[:, 1:2] * aw[1:2, :]
    total = jnp.where(info[FIRST] == 1, angular, 0.0)
    if whole:
        total += jnp.dot(split[:, :whole], table[:whole, :], preferred_element_type=F32)
    if rest:
        edge[...] = jnp.zeros(edge.shape, BF16)
        edge[:rest, :] = table[whole:, :]
        total += jnp.dot(split[:, whole:], edge[...], preferred_element_type=F32)
    out[...] = total.astype(BF16)


def lookup_sum(table, seg_index, seg_amp, field_angle, angle_weight, info):
    rows, width = table.shape
    samples, active = seg_index.shape
    groups, lanes = samples // GROUP, GROUP * active
    columns = -(-rows // LANES) * LANES
    block = min(width, 256)
    small = pl.BlockSpec((groups, lanes), lambda n, info: (0, 0))
    return pl.pallas_call(
        lookup_kernel,
        grid_spec=pltpu.PrefetchScalarGridSpec(
            num_scalar_prefetch=1,
            grid=(width // block,),
            in_specs=[
                small,
                small,
                pl.BlockSpec((samples, 2), lambda n, info: (0, 0)),
                pl.BlockSpec((2, block), lambda n, info: (0, n)),
                pl.BlockSpec((rows, block), lambda n, info: (0, n)),
            ],
            out_specs=pl.BlockSpec((samples, block), lambda n, info: (0, n)),
            scratch_shapes=[
                pltpu.VMEM((groups, lanes), jnp.int32),
                pltpu.VMEM((groups, lanes), jnp.int32),
                pltpu.VMEM((groups, lanes), F32),
                pltpu.VMEM((groups, lanes), F32),
                pltpu.VMEM((samples, columns), F32),
                pltpu.VMEM((samples, columns), BF16),
                pltpu.VMEM((LANES, block), BF16),
            ],
        ),
        out_shape=jax.ShapeDtypeStruct((samples, width), BF16),
        compiler_params=params(),
        cost_estimate=costs(10 * samples * rows * width, 2 * rows * width),
        name="lookup_sum",
    )(info, seg_index.reshape(groups, lanes), seg_amp.reshape(groups, lanes), field_angle, angle_weight, table)


NT = (((1,), (1,)), ((), ()))


def cuts(rows):
    return [rows // 8 * 3, rows - rows // 8 * 3]


def first_terms_kernel(info, came, pre, target, first, second, after, later, grad, *outs):
    piece = 32

    @pl.when(pl.program_id(0) == 0)
    def differentiate():
        def one(k, unused):
            span = pl.ds(pl.multiple_of(k * piece, piece), piece)
            act, pullback = jax.vjp(jax.nn.gelu, pre[0, 0, span, :].astype(F32))
            slope = pullback(jnp.ones_like(act))[0]
            missed = act - target[span, :].astype(F32)
            cotangent = jnp.where(info[LAST] == 1, missed, came[span, :].astype(F32))
            grad[span, :] = (cotangent * slope).astype(BF16)
            return unused

        lax.fori_loop(0, grad.shape[0] // piece, one, 0)

    cut = outs[0].shape[0]
    for block, (upper, lower) in zip((first, second), (outs[:2], outs[2:])):
        term = lax.dot_general(grad[...], block[...], NT, preferred_element_type=F32).astype(BF16)
        upper[...] = term[:cut]
        lower[...] = term[cut:]


def first_terms(came, stash_pre, target, weight, info, at, after, later):
    rows, width = came.shape
    block = min(width, 256)
    steps = width // block
    pieces = cuts(rows) * 2
    shapes = [jax.ShapeDtypeStruct((piece, width), BF16) for piece in pieces]
    whole = pl.BlockSpec((rows, width), lambda n, info: (0, 0))
    out_specs = [pl.BlockSpec((piece, block), lambda n, info: (0, n)) for piece in pieces]
    return pl.pallas_call(
        first_terms_kernel,
        grid_spec=pltpu.PrefetchScalarGridSpec(
            num_scalar_prefetch=1,
            grid=(steps,),
            in_specs=[
                whole,
                pl.BlockSpec((1, 1, rows, width), lambda n, info: (0, info[SLOT], 0, 0)),
                whole,
                pl.BlockSpec((block, width), lambda n, info: (info[at + 1] * steps + n, 0)),
                pl.BlockSpec((block, width), lambda n, info: (info[at] * steps + n, 0)),
                ANYWHERE,
                ANYWHERE,
            ],
            out_specs=[whole] + out_specs,
        ),
        out_shape=[jax.ShapeDtypeStruct((rows, width), BF16)] + shapes,
        compiler_params=params(),
        cost_estimate=costs(4 * rows * width * width, 4 * width * width + 6 * rows * width),
        name="gradient_terms",
    )(info, came, stash_pre, target, weight, weight, after, later)


def terms_kernel(info, grad, first, second, after, later, first_out, second_out):
    first_out[...] = lax.dot_general(grad[...], first[...], NT, preferred_element_type=F32).astype(BF16)
    second_out[...] = lax.dot_general(grad[...], second[...], NT, preferred_element_type=F32).astype(BF16)


def terms(grad, weight, info, at, after, later):
    rows, width = grad.shape
    block = min(width, 512)
    steps = width // block
    shape = jax.ShapeDtypeStruct((rows, width), BF16)
    out_spec = pl.BlockSpec((rows, block), lambda n, info: (0, n))
    return pl.pallas_call(
        terms_kernel,
        grid_spec=pltpu.PrefetchScalarGridSpec(
            num_scalar_prefetch=1,
            grid=(steps,),
            in_specs=[
                pl.BlockSpec((rows, width), lambda n, info: (0, 0)),
                pl.BlockSpec((block, width), lambda n, info: (info[at + 1] * steps + n, 0)),
                pl.BlockSpec((block, width), lambda n, info: (info[at] * steps + n, 0)),
                ANYWHERE,
                ANYWHERE,
            ],
            out_specs=[out_spec, out_spec],
        ),
        out_shape=[shape, shape],
        compiler_params=params(),
        cost_estimate=costs(4 * rows * width * width, 4 * width * width + 6 * rows * width),
        name="input_terms",
    )(info, grad, weight, weight, after, later)


def forward_kernel(finish, info, a, b, first, second, carry, before, after, out):
    total = carry[...] + jnp.dot(a[...], first[...], preferred_element_type=F32)
    total += jnp.dot(b[...], second[...], preferred_element_type=F32)
    if finish:
        total = jax.nn.gelu(total)
    out[...] = total.astype(out.dtype)


def forward_step(a, b, weight, info, at, carry, rows, h, finish, before, after):
    half, width = a.shape
    block = min(width, 512)
    piece = pl.BlockSpec((half, width), lambda n, info: (0, 0))
    out_rows, place = (rows, h) if finish else (half, 0)
    return pl.pallas_call(
        functools.partial(forward_kernel, finish),
        grid_spec=pltpu.PrefetchScalarGridSpec(
            num_scalar_prefetch=1,
            grid=(width // block,),
            in_specs=[
                piece,
                piece,
                pl.BlockSpec((width, block), lambda n, info: (info[at], n)),
                pl.BlockSpec((width, block), lambda n, info: (info[at + 1], n)),
                pl.BlockSpec((carry.shape[0], block), lambda n, info: (0, n)),
                ANYWHERE,
                ANYWHERE,
            ],
            out_specs=pl.BlockSpec((half, block), lambda n, info: (place, n)),
        ),
        out_shape=jax.ShapeDtypeStruct((out_rows, width), BF16 if finish else F32),
        input_output_aliases={6: 0} if finish and h else {},
        compiler_params=params(),
        cost_estimate=costs(4 * half * width * width, 4 * width * width + 8 * half * width),
        name="forward_step",
    )(info, a, b, weight, weight, carry, before, after)


def step_down(shard, stride):
    sections = lax.axis_size("section")
    return over("section", shard, [(s, s - stride) for s in range(stride, sections, 2 * stride)])


def local(
    sent_act,
    sent_grad,
    stash_in,
    stash_pre,
    layer_weight,
    layer_bias,
    seg_table,
    seg_index,
    seg_amp,
    field_angle,
    angle_weight,
    target,
    sched,
):
    section = lax.axis_index("section")
    sections = lax.axis_size("section")
    me = lax.axis_index("fsdp")
    count = lax.axis_size("fsdp")
    chips = count // CORES
    rows = sent_act.shape[1]
    halves = 2
    half = rows // halves
    weight = layer_weight[0]

    numbers = [section * seg_table.shape[0], section == 0, sched[0], section == sections - 1]
    for by in range(chips):
        base = lax.rem(me // CORES + by, chips) * CORES
        core = lax.rem(me, CORES)
        numbers += [base + core, base + 1 - core]
    info = jnp.stack([jnp.asarray(number, jnp.int32) for number in numbers])
    is_first = section == 0
    stashed_in = lax.dynamic_index_in_dim(stash_in[0], sched[0], 0, keepdims=False)
    stashed_full = lax.all_gather(stashed_in, "fsdp", axis=1, tiled=True)

    from_before = over("section", sent_act[0], [(s, s + 1) for s in range(sections - 1)])
    from_next = over("section", sent_grad[0], [(s, s - 1) for s in range(1, sections)])
    rounded = lookup_sum(seg_table, seg_index, seg_amp, field_angle, angle_weight, info)

    received = []
    for by in range(1, chips):
        at = BLOCKS + 2 * by
        if by == 1:
            pre_grad, *terms_out = first_terms(
                from_next, stash_pre, target, weight, info, at, rounded, from_before
            )
            to_other, kept = terms_out[:2], terms_out[2:]
        else:
            to_other, kept = [
                [term[:cuts(rows)[0]], term[cuts(rows)[0]:]]
                for term in terms(pre_grad, weight, info, at, info, info)
            ]
        received.append([
            to_chip((mine.astype(F32) + swap_cores(other).astype(F32)).astype(BF16), by)
            for mine, other in zip(kept, to_other)
        ])
    grad_bias = jnp.sum(pre_grad.astype(F32), axis=0)

    near = step_down(rounded, 1)
    near, received[0][0] = lax.optimization_barrier((near, received[0][0]))
    total = (rounded.astype(F32) + near.astype(F32)).astype(BF16)
    stride = 2
    while 2 * stride < sections:
        total = (total.astype(F32) + step_down(total, stride).astype(F32)).astype(BF16)
        stride *= 2
    leaving = [total[h * half:(h + 1) * half] for h in range(halves)]
    grad_w = lax.dot_general(
        stashed_full, pre_grad, (((0,), (0,)), ((), ())), preferred_element_type=F32
    ).astype(BF16)
    last = [step_down(leaving[0], stride)]
    leaving[1], grad_w = lax.optimization_barrier((leaving[1], grad_w))
    last.append(step_down(leaving[1], stride))
    last[0], received[0][1], grad_w = lax.optimization_barrier((last[0], received[0][1], grad_w))

    inputs, carries = [], []
    for h in range(halves):
        first_input = (leaving[h].astype(F32) + last[h].astype(F32)).astype(BF16)
        inputs.append(jnp.where(is_first, first_input, from_before[h * half:(h + 1) * half]))
        carry = forward_step(
            inputs[h], swap_cores(inputs[h]), weight, info, BLOCKS, layer_bias, rows, h, False, info, info
        )
        if h == 0:
            to_other, kept = terms(pre_grad, weight, info, BLOCKS, inputs[0], info)
            last[1], to_other, carry = lax.optimization_barrier((last[1], to_other, carry))
        carries.append(carry)
    beside = kept.astype(F32) + swap_cores(to_other).astype(F32)
    far = [sum(part[h].astype(F32) for part in received) for h in range(2)]
    grad_in = (beside + jnp.concatenate(far, axis=0)).astype(BF16)
    fwd_out = info
    for h, carry in enumerate(carries):
        for by in range(1, chips):
            arrived = to_chip(inputs[h], chips - by)
            if h:
                arrived, fwd_out, grad_in = lax.optimization_barrier((arrived, fwd_out, grad_in))
            carry = forward_step(
                arrived,
                swap_cores(arrived),
                weight,
                info,
                BLOCKS + 2 * by,
                carry,
                rows,
                h,
                by == chips - 1,
                fwd_out,
                info if h else carries[-1],
            )
        fwd_out = carry
    return (fwd_out[None], grad_in[None], grad_w[None], grad_bias[None])


def solution(mesh):
    return jax.shard_map(
        local,
        mesh=mesh,
        in_specs=(
            P("section", "groups", "fsdp"),
            P("section", "groups", "fsdp"),
            P("section", None, "groups", "fsdp"),
            P("section", None, "groups", "fsdp"),
            P("section", None, "fsdp"),
            P("section", "fsdp"),
            P("section", "fsdp"),
            P("groups", None),
            P("groups", None),
            P("groups", None),
            P(None, "fsdp"),
            P("groups", "fsdp"),
            P("section"),
        ),
        out_specs=(
            P("section", "groups", "fsdp"),
            P("section", "groups", "fsdp"),
            P("section", "groups", "fsdp"),
            P("section", ("groups", "fsdp")),
        ),
        check_vma=False,
    )
```

```python
import functools

import jax
import jax.numpy as jnp
from jax import lax
from jax.experimental import pallas as pl
from jax.experimental.pallas import tpu as pltpu
from jax.sharding import PartitionSpec as P

F32 = jnp.float32
BF16 = jnp.bfloat16
LANES = 128
GROUP = 8
CORES = 2
ROW, FIRST, SLOT, LAST, BLOCKS = range(5)


def over(axis, shard, pairs):
    return lax.ppermute(shard, axis, pairs)


def swap_cores(shard):
    count = lax.axis_size("fsdp")
    return over("fsdp", shard, [(i, i ^ 1) for i in range(count)])


def to_chip(shard, by):
    count = lax.axis_size("fsdp")
    return over("fsdp", shard, [(i, (i + CORES * by) % count) for i in range(count)])


def costs(flops, moved):
    return pl.CostEstimate(flops=flops, bytes_accessed=moved, transcendentals=0)


ANYWHERE = pl.BlockSpec(memory_space=pl.ANY)


def params():
    return pltpu.CompilerParams(vmem_limit_bytes=20 << 20)


def lookup_kernel(info, idx, amp, fa, aw, table, out, code, low_part, high, low, spread, split, edge):
    rows = table.shape[0]
    whole = rows // LANES * LANES
    rest = rows - whole
    high_count = spread.shape[1] // LANES
    groups, lanes = idx.shape
    per_sample = lanes // GROUP

    @pl.when(pl.program_id(0) == 0)
    def build():
        local_row = idx[...] - info[ROW]
        inside = (local_row >= 0) & (local_row < rows)
        sample = lax.broadcasted_iota(jnp.int32, idx.shape, 1) // per_sample
        code[...] = jnp.where(inside, (local_row // LANES) * GROUP + sample, -1)
        low_part[...] = local_row % LANES
        high[...] = amp[...].astype(BF16).astype(F32)
        low[...] = amp[...] - high[...]
        row_id = lax.broadcasted_iota(jnp.int32, (high_count * GROUP, lanes), 0)
        lane_id = lax.broadcasted_iota(jnp.int32, (LANES, lanes), 0)

        def one(group, unused):
            here = pl.ds(group, 1)
            matched = code[here, :] == row_id
            left_high = jnp.where(matched, high[here, :], 0.0).astype(BF16)
            left_low = jnp.where(matched, low[here, :], 0.0).astype(BF16)
            right = jnp.where(low_part[here, :] == lane_id, 1.0, 0.0).astype(BF16)
            left = jnp.concatenate([left_high, left_low], axis=0)
            summed = lax.dot_general(left, right, NT, preferred_element_type=F32)
            summed = summed[:high_count * GROUP] + summed[high_count * GROUP:]
            for k in range(high_count):
                spread[pl.ds(pl.multiple_of(group * GROUP, GROUP), GROUP), k * LANES:(k + 1) * LANES] = (
                    summed[k * GROUP:(k + 1) * GROUP, :]
                )
            return unused

        lax.fori_loop(0, groups, one, 0, unroll=8)
        split[...] = spread[...].astype(BF16)

    angular = fa[:, 0:1] * aw[0:1, :] + fa[:, 1:2] * aw[1:2, :]
    total = jnp.where(info[FIRST] == 1, angular, 0.0)
    if whole:
        total += jnp.dot(split[:, :whole], table[:whole, :], preferred_element_type=F32)
    if rest:
        edge[...] = jnp.zeros(edge.shape, BF16)
        edge[:rest, :] = table[whole:, :]
        total += jnp.dot(split[:, whole:], edge[...], preferred_element_type=F32)
    out[...] = total.astype(BF16)


def lookup_sum(table, seg_index, seg_amp, field_angle, angle_weight, info):
    rows, width = table.shape
    samples, active = seg_index.shape
    groups, lanes = samples // GROUP, GROUP * active
    columns = -(-rows // LANES) * LANES
    block = min(width, 256)
    small = pl.BlockSpec((groups, lanes), lambda n, info: (0, 0))
    return pl.pallas_call(
        lookup_kernel,
        grid_spec=pltpu.PrefetchScalarGridSpec(
            num_scalar_prefetch=1,
            grid=(width // block,),
            in_specs=[
                small,
                small,
                pl.BlockSpec((samples, 2), lambda n, info: (0, 0)),
                pl.BlockSpec((2, block), lambda n, info: (0, n)),
                pl.BlockSpec((rows, block), lambda n, info: (0, n)),
            ],
            out_specs=pl.BlockSpec((samples, block), lambda n, info: (0, n)),
            scratch_shapes=[
                pltpu.VMEM((groups, lanes), jnp.int32),
                pltpu.VMEM((groups, lanes), jnp.int32),
                pltpu.VMEM((groups, lanes), F32),
                pltpu.VMEM((groups, lanes), F32),
                pltpu.VMEM((samples, columns), F32),
                pltpu.VMEM((samples, columns), BF16),
                pltpu.VMEM((LANES, block), BF16),
            ],
        ),
        out_shape=jax.ShapeDtypeStruct((samples, width), BF16),
        compiler_params=params(),
        cost_estimate=costs(10 * samples * rows * width, 2 * rows * width),
        name="lookup_sum",
    )(info, seg_index.reshape(groups, lanes), seg_amp.reshape(groups, lanes), field_angle, angle_weight, table)


NT = (((1,), (1,)), ((), ()))


def cuts(rows):
    return [rows // 8 * 3, rows - rows // 8 * 3]


def first_terms_kernel(info, came, pre, target, first, second, after, later, grad, *outs):
    piece = 32

    @pl.when(pl.program_id(0) == 0)
    def differentiate():
        def one(k, unused):
            span = pl.ds(pl.multiple_of(k * piece, piece), piece)
            act, pullback = jax.vjp(jax.nn.gelu, pre[0, 0, span, :].astype(F32))
            slope = pullback(jnp.ones_like(act))[0]
            missed = act - target[span, :].astype(F32)
            cotangent = jnp.where(info[LAST] == 1, missed, came[span, :].astype(F32))
            grad[span, :] = (cotangent * slope).astype(BF16)
            return unused

        lax.fori_loop(0, grad.shape[0] // piece, one, 0)

    cut = outs[0].shape[0]
    for block, (upper, lower) in zip((first, second), (outs[:2], outs[2:])):
        term = lax.dot_general(grad[...], block[...], NT, preferred_element_type=F32).astype(BF16)
        upper[...] = term[:cut]
        lower[...] = term[cut:]


def first_terms(came, stash_pre, target, weight, info, at, after, later):
    rows, width = came.shape
    block = min(width, 256)
    steps = width // block
    pieces = cuts(rows) * 2
    shapes = [jax.ShapeDtypeStruct((piece, width), BF16) for piece in pieces]
    whole = pl.BlockSpec((rows, width), lambda n, info: (0, 0))
    out_specs = [pl.BlockSpec((piece, block), lambda n, info: (0, n)) for piece in pieces]
    return pl.pallas_call(
        first_terms_kernel,
        grid_spec=pltpu.PrefetchScalarGridSpec(
            num_scalar_prefetch=1,
            grid=(steps,),
            in_specs=[
                whole,
                pl.BlockSpec((1, 1, rows, width), lambda n, info: (0, info[SLOT], 0, 0)),
                whole,
                pl.BlockSpec((block, width), lambda n, info: (info[at + 1] * steps + n, 0)),
                pl.BlockSpec((block, width), lambda n, info: (info[at] * steps + n, 0)),
                ANYWHERE,
                ANYWHERE,
            ],
            out_specs=[whole] + out_specs,
        ),
        out_shape=[jax.ShapeDtypeStruct((rows, width), BF16)] + shapes,
        compiler_params=params(),
        cost_estimate=costs(4 * rows * width * width, 4 * width * width + 6 * rows * width),
        name="gradient_terms",
    )(info, came, stash_pre, target, weight, weight, after, later)


def terms_kernel(info, grad, first, second, after, later, first_out, second_out):
    first_out[...] = lax.dot_general(grad[...], first[...], NT, preferred_element_type=F32).astype(BF16)
    second_out[...] = lax.dot_general(grad[...], second[...], NT, preferred_element_type=F32).astype(BF16)


def terms(grad, weight, info, at, after, later):
    rows, width = grad.shape
    block = min(width, 512)
    steps = width // block
    shape = jax.ShapeDtypeStruct((rows, width), BF16)
    out_spec = pl.BlockSpec((rows, block), lambda n, info: (0, n))
    return pl.pallas_call(
        terms_kernel,
        grid_spec=pltpu.PrefetchScalarGridSpec(
            num_scalar_prefetch=1,
            grid=(steps,),
            in_specs=[
                pl.BlockSpec((rows, width), lambda n, info: (0, 0)),
                pl.BlockSpec((block, width), lambda n, info: (info[at + 1] * steps + n, 0)),
                pl.BlockSpec((block, width), lambda n, info: (info[at] * steps + n, 0)),
                ANYWHERE,
                ANYWHERE,
            ],
            out_specs=[out_spec, out_spec],
        ),
        out_shape=[shape, shape],
        compiler_params=params(),
        cost_estimate=costs(0, 0),
        name="input_terms",
    )(info, grad, weight, weight, after, later)


def forward_kernel(finish, info, a, b, first, second, carry, before, after, out):
    total = carry[...] + jnp.dot(a[...], first[...], preferred_element_type=F32)
    total += jnp.dot(b[...], second[...], preferred_element_type=F32)
    if finish:
        total = jax.nn.gelu(total)
    out[...] = total.astype(out.dtype)


def forward_step(a, b, weight, info, at, carry, rows, h, finish, before, after):
    half, width = a.shape
    block = min(width, 512)
    piece = pl.BlockSpec((half, width), lambda n, info: (0, 0))
    out_rows, place = (rows, h) if finish else (half, 0)
    return pl.pallas_call(
        functools.partial(forward_kernel, finish),
        grid_spec=pltpu.PrefetchScalarGridSpec(
            num_scalar_prefetch=1,
            grid=(width // block,),
            in_specs=[
                piece,
                piece,
                pl.BlockSpec((width, block), lambda n, info: (info[at], n)),
                pl.BlockSpec((width, block), lambda n, info: (info[at + 1], n)),
                pl.BlockSpec((carry.shape[0], block), lambda n, info: (0, n)),
                ANYWHERE,
                ANYWHERE,
            ],
            out_specs=pl.BlockSpec((half, block), lambda n, info: (place, n)),
        ),
        out_shape=jax.ShapeDtypeStruct((out_rows, width), BF16 if finish else F32),
        input_output_aliases={6: 0} if finish and h else {},
        compiler_params=params(),
        cost_estimate=costs(4 * half * width * width, 4 * width * width + 8 * half * width),
        name="forward_step",
    )(info, a, b, weight, weight, carry, before, after)


def step_down(shard, stride):
    sections = lax.axis_size("section")
    return over("section", shard, [(s, s - stride) for s in range(stride, sections, 2 * stride)])


def local(
    sent_act,
    sent_grad,
    stash_in,
    stash_pre,
    layer_weight,
    layer_bias,
    seg_table,
    seg_index,
    seg_amp,
    field_angle,
    angle_weight,
    target,
    sched,
):
    section = lax.axis_index("section")
    sections = lax.axis_size("section")
    me = lax.axis_index("fsdp")
    count = lax.axis_size("fsdp")
    chips = count // CORES
    rows = sent_act.shape[1]
    halves = 2
    half = rows // halves
    weight = layer_weight[0]

    numbers = [section * seg_table.shape[0], section == 0, sched[0], section == sections - 1]
    for by in range(chips):
        base = lax.rem(me // CORES + by, chips) * CORES
        core = lax.rem(me, CORES)
        numbers += [base + core, base + 1 - core]
    info = jnp.stack([jnp.asarray(number, jnp.int32) for number in numbers])
    is_first = section == 0
    stashed_in = lax.dynamic_index_in_dim(stash_in[0], sched[0], 0, keepdims=False)
    stashed_full = lax.all_gather(stashed_in, "fsdp", axis=1, tiled=True)

    from_before = over("section", sent_act[0], [(s, s + 1) for s in range(sections - 1)])
    from_next = over("section", sent_grad[0], [(s, s - 1) for s in range(1, sections)])
    rounded = lookup_sum(seg_table, seg_index, seg_amp, field_angle, angle_weight, info)

    received = []
    for by in range(1, chips):
        at = BLOCKS + 2 * by
        if by == 1:
            pre_grad, *terms_out = first_terms(
                from_next, stash_pre, target, weight, info, at, rounded, from_before
            )
            to_other, kept = terms_out[:2], terms_out[2:]
        else:
            to_other, kept = [
                [term[:cuts(rows)[0]], term[cuts(rows)[0]:]]
                for term in terms(pre_grad, weight, info, at, info, info)
            ]
        both = [
            (mine.astype(F32) + swap_cores(other).astype(F32)).astype(BF16)
            for mine, other in zip(kept, to_other)
        ]
        if by == 1:
            token = both[1]
        received.append([to_chip(piece, by) for piece in both])
    grad_bias = jnp.sum(pre_grad.astype(F32), axis=0)

    near = step_down(rounded, 1)
    near, token = lax.optimization_barrier((near, token))
    leaving = []
    for h in range(halves):
        span = slice(h * half, (h + 1) * half)
        leaving.append((rounded[span].astype(F32) + near[span].astype(F32)).astype(BF16))
    stride = 2
    while 2 * stride < sections:
        leaving = [(piece.astype(F32) + step_down(piece, stride).astype(F32)).astype(BF16) for piece in leaving]
        stride *= 2
    grad_w = lax.dot_general(
        stashed_full, pre_grad, (((0,), (0,)), ((), ())), preferred_element_type=F32
    ).astype(BF16)
    last = [step_down(leaving[0], stride)]
    leaving[1], grad_w = lax.optimization_barrier((leaving[1], grad_w))
    last.append(step_down(leaving[1], stride))
    last[0], received[0][1], grad_w, grad_bias = lax.optimization_barrier(
        (last[0], received[0][1], grad_w, grad_bias)
    )

    inputs, carries = [], []
    for h in range(halves):
        first_input = (leaving[h].astype(F32) + last[h].astype(F32)).astype(BF16)
        inputs.append(jnp.where(is_first, first_input, from_before[h * half:(h + 1) * half]))
        carry = forward_step(
            inputs[h], swap_cores(inputs[h]), weight, info, BLOCKS, layer_bias, rows, h, False, info, info
        )
        if h == 0:
            to_other, kept = terms(pre_grad, weight, info, BLOCKS, inputs[0], token)
            last[1], to_other, received[0][0] = lax.optimization_barrier((last[1], to_other, received[0][0]))
        carries.append(carry)
    beside = kept.astype(F32) + swap_cores(to_other).astype(F32)
    far = [sum(part[h].astype(F32) for part in received) for h in range(2)]
    grad_in = (beside + jnp.concatenate(far, axis=0)).astype(BF16)
    fwd_out = info
    for h, carry in enumerate(carries):
        for by in range(1, chips):
            arrived = to_chip(inputs[h], chips - by)
            if h:
                arrived, fwd_out, grad_in = lax.optimization_barrier((arrived, fwd_out, grad_in))
            carry = forward_step(
                arrived,
                swap_cores(arrived),
                weight,
                info,
                BLOCKS + 2 * by,
                carry,
                rows,
                h,
                by == chips - 1,
                fwd_out,
                info if h else carries[-1],
            )
        fwd_out = carry
    return (fwd_out[None], grad_in[None], grad_w[None], grad_bias[None])


def solution(mesh):
    return jax.shard_map(
        local,
        mesh=mesh,
        in_specs=(
            P("section", "groups", "fsdp"),
            P("section", "groups", "fsdp"),
            P("section", None, "groups", "fsdp"),
            P("section", None, "groups", "fsdp"),
            P("section", None, "fsdp"),
            P("section", "fsdp"),
            P("section", "fsdp"),
            P("groups", None),
            P("groups", None),
            P("groups", None),
            P(None, "fsdp"),
            P("groups", "fsdp"),
            P("section"),
        ),
        out_specs=(
            P("section", "groups", "fsdp"),
            P("section", "groups", "fsdp"),
            P("section", "groups", "fsdp"),
            P("section", ("groups", "fsdp")),
        ),
        check_vma=False,
    )
```

```python
import functools

import jax
import jax.numpy as jnp
from jax import lax
from jax.experimental import pallas as pl
from jax.experimental.pallas import tpu as pltpu
from jax.sharding import PartitionSpec as P

F32 = jnp.float32
BF16 = jnp.bfloat16
LANES = 128
GROUP = 8
CORES = 2
ROW, FIRST, SLOT, LAST, BLOCKS = range(5)


def over(axis, shard, pairs):
    return lax.ppermute(shard, axis, pairs)


def swap_cores(shard):
    count = lax.axis_size("fsdp")
    return over("fsdp", shard, [(i, i ^ 1) for i in range(count)])


def to_chip(shard, by):
    count = lax.axis_size("fsdp")
    return over("fsdp", shard, [(i, (i + CORES * by) % count) for i in range(count)])


def costs(flops, moved):
    return pl.CostEstimate(flops=flops, bytes_accessed=moved, transcendentals=0)


ANYWHERE = pl.BlockSpec(memory_space=pl.ANY)


def params():
    return pltpu.CompilerParams(vmem_limit_bytes=20 << 20)


def lookup_kernel(info, idx, amp, fa, aw, table, out, code, low_part, high, low, spread, split, edge):
    rows = table.shape[0]
    whole = rows // LANES * LANES
    rest = rows - whole
    high_count = spread.shape[1] // LANES
    groups, lanes = idx.shape
    per_sample = lanes // GROUP

    @pl.when(pl.program_id(0) == 0)
    def build():
        local_row = idx[...] - info[ROW]
        inside = (local_row >= 0) & (local_row < rows)
        sample = lax.broadcasted_iota(jnp.int32, idx.shape, 1) // per_sample
        code[...] = jnp.where(inside, (local_row // LANES) * GROUP + sample, -1)
        low_part[...] = local_row % LANES
        high[...] = amp[...].astype(BF16).astype(F32)
        low[...] = amp[...] - high[...]
        row_id = lax.broadcasted_iota(jnp.int32, (high_count * GROUP, lanes), 0)
        lane_id = lax.broadcasted_iota(jnp.int32, (LANES, lanes), 0)

        def one(group, unused):
            here = pl.ds(group, 1)
            matched = code[here, :] == row_id
            left_high = jnp.where(matched, high[here, :], 0.0).astype(BF16)
            left_low = jnp.where(matched, low[here, :], 0.0).astype(BF16)
            right = jnp.where(low_part[here, :] == lane_id, 1.0, 0.0).astype(BF16)
            left = jnp.concatenate([left_high, left_low], axis=0)
            summed = lax.dot_general(left, right, NT, preferred_element_type=F32)
            summed = summed[:high_count * GROUP] + summed[high_count * GROUP:]
            for k in range(high_count):
                spread[pl.ds(pl.multiple_of(group * GROUP, GROUP), GROUP), k * LANES:(k + 1) * LANES] = (
                    summed[k * GROUP:(k + 1) * GROUP, :]
                )
            return unused

        lax.fori_loop(0, groups, one, 0, unroll=8)
        split[...] = spread[...].astype(BF16)

    angular = fa[:, 0:1] * aw[0:1, :] + fa[:, 1:2] * aw[1:2, :]
    total = jnp.where(info[FIRST] == 1, angular, 0.0)
    if whole:
        total += jnp.dot(split[:, :whole], table[:whole, :], preferred_element_type=F32)
    if rest:
        edge[...] = jnp.zeros(edge.shape, BF16)
        edge[:rest, :] = table[whole:, :]
        total += jnp.dot(split[:, whole:], edge[...], preferred_element_type=F32)
    out[...] = total.astype(BF16)


def lookup_sum(table, seg_index, seg_amp, field_angle, angle_weight, info):
    rows, width = table.shape
    groups, lanes = seg_index.shape
    samples = field_angle.shape[0]
    columns = -(-rows // LANES) * LANES
    block = min(width, 256)
    small = pl.BlockSpec((groups, lanes), lambda n, info: (0, 0))
    return pl.pallas_call(
        lookup_kernel,
        grid_spec=pltpu.PrefetchScalarGridSpec(
            num_scalar_prefetch=1,
            grid=(width // block,),
            in_specs=[
                small,
                small,
                pl.BlockSpec((samples, 2), lambda n, info: (0, 0)),
                pl.BlockSpec((2, block), lambda n, info: (0, n)),
                pl.BlockSpec((rows, block), lambda n, info: (0, n)),
            ],
            out_specs=pl.BlockSpec((samples, block), lambda n, info: (0, n)),
            scratch_shapes=[
                pltpu.VMEM((groups, lanes), jnp.int32),
                pltpu.VMEM((groups, lanes), jnp.int32),
                pltpu.VMEM((groups, lanes), F32),
                pltpu.VMEM((groups, lanes), F32),
                pltpu.VMEM((samples, columns), F32),
                pltpu.VMEM((samples, columns), BF16),
                pltpu.VMEM((LANES, block), BF16),
            ],
        ),
        out_shape=jax.ShapeDtypeStruct((samples, width), BF16),
        compiler_params=params(),
        cost_estimate=costs(10 * samples * rows * width, 2 * rows * width),
        name="lookup_sum",
    )(info, seg_index, seg_amp, field_angle, angle_weight, table)


NT = (((1,), (1,)), ((), ()))


def cuts(rows):
    return [rows // 8 * 3, rows - rows // 8 * 3]


def slopes_kernel(info, pre, target, after, later, slope, closing):
    act, pullback = jax.vjp(jax.nn.gelu, pre[0, 0].astype(F32))
    slope[...] = pullback(jnp.ones_like(act))[0]
    closing[...] = ((act - target[...].astype(F32)) * slope[...]).astype(BF16)


def slopes(stash_pre, target, info, after, later):
    rows, width = target.shape
    block = min(rows, 64)
    span = pl.BlockSpec((block, width), lambda n, info: (n, 0))
    return pl.pallas_call(
        slopes_kernel,
        grid_spec=pltpu.PrefetchScalarGridSpec(
            num_scalar_prefetch=1,
            grid=(rows // block,),
            in_specs=[
                pl.BlockSpec((1, 1, block, width), lambda n, info: (0, info[SLOT], n, 0)),
                span,
                ANYWHERE,
                ANYWHERE,
            ],
            out_specs=[span, span],
        ),
        out_shape=[jax.ShapeDtypeStruct((rows, width), F32), jax.ShapeDtypeStruct((rows, width), BF16)],
        compiler_params=params(),
        cost_estimate=costs(0, 10 * rows * width),
        name="slopes",
    )(info, stash_pre, target, after, later)


def first_terms_kernel(info, came, slope, closing, first, second, after, grad, *outs):
    @pl.when(pl.program_id(0) == 0)
    def differentiate():
        grad[...] = jnp.where(info[LAST] == 1, closing[...], (came[...].astype(F32) * slope[...]).astype(BF16))

    cut = outs[0].shape[0]
    for block, (upper, lower) in zip((first, second), (outs[:2], outs[2:])):
        term = lax.dot_general(grad[...], block[...], NT, preferred_element_type=F32).astype(BF16)
        upper[...] = term[:cut]
        lower[...] = term[cut:]


def first_terms(came, slope, closing, weight, info, at, after):
    rows, width = came.shape
    block = min(width, 256)
    steps = width // block
    pieces = cuts(rows) * 2
    shapes = [jax.ShapeDtypeStruct((piece, width), BF16) for piece in pieces]
    whole = pl.BlockSpec((rows, width), lambda n, info: (0, 0))
    out_specs = [pl.BlockSpec((piece, block), lambda n, info: (0, n)) for piece in pieces]
    return pl.pallas_call(
        first_terms_kernel,
        grid_spec=pltpu.PrefetchScalarGridSpec(
            num_scalar_prefetch=1,
            grid=(steps,),
            in_specs=[
                whole,
                whole,
                whole,
                pl.BlockSpec((block, width), lambda n, info: (info[at + 1] * steps + n, 0)),
                pl.BlockSpec((block, width), lambda n, info: (info[at] * steps + n, 0)),
                ANYWHERE,
            ],
            out_specs=[whole] + out_specs,
        ),
        out_shape=[jax.ShapeDtypeStruct((rows, width), BF16)] + shapes,
        compiler_params=params(),
        cost_estimate=costs(4 * rows * width * width, 4 * width * width + 6 * rows * width),
        name="gradient_terms",
    )(info, came, slope, closing, weight, weight, after)


def terms_kernel(info, grad, first, second, after, later, first_out, second_out):
    first_out[...] = lax.dot_general(grad[...], first[...], NT, preferred_element_type=F32).astype(BF16)
    second_out[...] = lax.dot_general(grad[...], second[...], NT, preferred_element_type=F32).astype(BF16)


def terms(grad, weight, info, at, after, later):
    rows, width = grad.shape
    block = min(width, 512)
    steps = width // block
    shape = jax.ShapeDtypeStruct((rows, width), BF16)
    out_spec = pl.BlockSpec((rows, block), lambda n, info: (0, n))
    return pl.pallas_call(
        terms_kernel,
        grid_spec=pltpu.PrefetchScalarGridSpec(
            num_scalar_prefetch=1,
            grid=(steps,),
            in_specs=[
                pl.BlockSpec((rows, width), lambda n, info: (0, 0)),
                pl.BlockSpec((block, width), lambda n, info: (info[at + 1] * steps + n, 0)),
                pl.BlockSpec((block, width), lambda n, info: (info[at] * steps + n, 0)),
                ANYWHERE,
                ANYWHERE,
            ],
            out_specs=[out_spec, out_spec],
        ),
        out_shape=[shape, shape],
        compiler_params=params(),
        cost_estimate=costs(0, 0),
        name="input_terms",
    )(info, grad, weight, weight, after, later)


def forward_kernel(finish, info, a, b, first, second, carry, before, after, out):
    total = carry[...] + jnp.dot(a[...], first[...], preferred_element_type=F32)
    total += jnp.dot(b[...], second[...], preferred_element_type=F32)
    if finish:
        total = jax.nn.gelu(total)
    out[...] = total.astype(out.dtype)


def forward_step(a, b, weight, info, at, carry, rows, h, finish, before, after):
    half, width = a.shape
    block = min(width, 512)
    piece = pl.BlockSpec((half, width), lambda n, info: (0, 0))
    out_rows, place = (rows, h) if finish else (half, 0)
    return pl.pallas_call(
        functools.partial(forward_kernel, finish),
        grid_spec=pltpu.PrefetchScalarGridSpec(
            num_scalar_prefetch=1,
            grid=(width // block,),
            in_specs=[
                piece,
                piece,
                pl.BlockSpec((width, block), lambda n, info: (info[at], n)),
                pl.BlockSpec((width, block), lambda n, info: (info[at + 1], n)),
                pl.BlockSpec((carry.shape[0], block), lambda n, info: (0, n)),
                ANYWHERE,
                ANYWHERE,
            ],
            out_specs=pl.BlockSpec((half, block), lambda n, info: (place, n)),
        ),
        out_shape=jax.ShapeDtypeStruct((out_rows, width), BF16 if finish else F32),
        input_output_aliases={6: 0} if finish and h else {},
        compiler_params=params(),
        cost_estimate=costs(4 * half * width * width, 4 * width * width + 8 * half * width),
        name="forward_step",
    )(info, a, b, weight, weight, carry, before, after)


def step_down(shard, stride):
    sections = lax.axis_size("section")
    return over("section", shard, [(s, s - stride) for s in range(stride, sections, 2 * stride)])


def local(
    sent_act,
    sent_grad,
    stash_in,
    stash_pre,
    layer_weight,
    layer_bias,
    seg_table,
    seg_index,
    seg_amp,
    field_angle,
    angle_weight,
    target,
    sched,
):
    section = lax.axis_index("section")
    sections = lax.axis_size("section")
    me = lax.axis_index("fsdp")
    count = lax.axis_size("fsdp")
    chips = count // CORES
    rows = sent_act.shape[1]
    halves = 2
    half = rows // halves
    weight = layer_weight[0]

    numbers = [section * seg_table.shape[0], section == 0, sched[0], section == sections - 1]
    for by in range(chips):
        base = lax.rem(me // CORES + by, chips) * CORES
        core = lax.rem(me, CORES)
        numbers += [base + core, base + 1 - core]
    info = jnp.stack([jnp.asarray(number, jnp.int32) for number in numbers])
    is_first = section == 0
    stashed_in = lax.dynamic_index_in_dim(stash_in[0], sched[0], 0, keepdims=False)
    stashed_full = lax.all_gather(stashed_in, "fsdp", axis=1, tiled=True)
    from_before = over("section", sent_act[0], [(s, s + 1) for s in range(sections - 1)])
    from_next = over("section", sent_grad[0], [(s, s - 1) for s in range(1, sections)])
    samples, active = seg_index.shape
    by_group = (samples // GROUP, GROUP * active)
    rounded = lookup_sum(
        seg_table, seg_index.reshape(by_group), seg_amp.reshape(by_group), field_angle, angle_weight, info
    )

    received = []
    for by in range(1, chips):
        at = BLOCKS + 2 * by
        if by == 1:
            slope, closing = slopes(stash_pre, target, info, rounded, weight)
            pre_grad, *terms_out = first_terms(from_next, slope, closing, weight, info, at, from_before)
            to_other, kept = terms_out[:2], terms_out[2:]
        else:
            to_other, kept = [
                [term[:cuts(rows)[0]], term[cuts(rows)[0]:]]
                for term in terms(pre_grad, weight, info, at, info, info)
            ]
        both = [
            (mine.astype(F32) + swap_cores(other).astype(F32)).astype(BF16)
            for mine, other in zip(kept, to_other)
        ]
        if by == 1:
            token = both[1]
        received.append([to_chip(piece, by) for piece in both])
    grad_bias = jnp.sum(pre_grad.astype(F32), axis=0)

    to_other, kept = terms(pre_grad, weight, info, BLOCKS, token, info)
    near = step_down(rounded, 1)
    near, token, kept = lax.optimization_barrier((near, token, kept))
    beside = kept.astype(F32) + swap_cores(to_other).astype(F32)
    leaving = []
    for h in range(halves):
        span = slice(h * half, (h + 1) * half)
        leaving.append((rounded[span].astype(F32) + near[span].astype(F32)).astype(BF16))
    stride = 2
    while 2 * stride < sections:
        leaving = [(piece.astype(F32) + step_down(piece, stride).astype(F32)).astype(BF16) for piece in leaving]
        stride *= 2
    grad_w = lax.dot_general(
        stashed_full, pre_grad, (((0,), (0,)), ((), ())), preferred_element_type=F32
    ).astype(BF16)
    last = [step_down(leaving[0], stride)]
    leaving[1], grad_w = lax.optimization_barrier((leaving[1], grad_w))
    last.append(step_down(leaving[1], stride))
    last[0], received[0], grad_w, grad_bias = lax.optimization_barrier(
        (last[0], received[0], grad_w, grad_bias)
    )
    far = [sum(part[h].astype(F32) for part in received) for h in range(halves)]
    grad_in = (beside + jnp.concatenate(far, axis=0)).astype(BF16)

    inputs, carries = [], []
    for h in range(halves):
        first_input = (leaving[h].astype(F32) + last[h].astype(F32)).astype(BF16)
        inputs.append(jnp.where(is_first, first_input, from_before[h * half:(h + 1) * half]))
        mine = inputs[h]
        if h == 0:
            last[1], mine = lax.optimization_barrier((last[1], mine))
        carry = forward_step(
            mine, swap_cores(mine), weight, info, BLOCKS, layer_bias, rows, h, False, info, info
        )
        carries.append(carry)
    fwd_out = info
    for h in range(halves):
        carry = carries[h]
        for by in range(1, chips):
            arrived = to_chip(inputs[h], chips - by)
            if h == 0 and by == 1:
                arrived, carries[1] = lax.optimization_barrier((arrived, carries[1]))
            if h:
                arrived, fwd_out, grad_in = lax.optimization_barrier((arrived, fwd_out, grad_in))
            carry = forward_step(
                arrived,
                swap_cores(arrived),
                weight,
                info,
                BLOCKS + 2 * by,
                carry,
                rows,
                h,
                by == chips - 1,
                fwd_out,
                info,
            )
        fwd_out = carry
    return (fwd_out[None], grad_in[None], grad_w[None], grad_bias[None])


def solution(mesh):
    return jax.shard_map(
        local,
        mesh=mesh,
        in_specs=(
            P("section", "groups", "fsdp"),
            P("section", "groups", "fsdp"),
            P("section", None, "groups", "fsdp"),
            P("section", None, "groups", "fsdp"),
            P("section", None, "fsdp"),
            P("section", "fsdp"),
            P("section", "fsdp"),
            P("groups", None),
            P("groups", None),
            P("groups", None),
            P(None, "fsdp"),
            P("groups", "fsdp"),
            P("section"),
        ),
        out_specs=(
            P("section", "groups", "fsdp"),
            P("section", "groups", "fsdp"),
            P("section", "groups", "fsdp"),
            P("section", ("groups", "fsdp")),
        ),
        check_vma=False,
    )
```

```python
import functools

import jax
import jax.numpy as jnp
from jax import lax
from jax.experimental import pallas as pl
from jax.experimental.pallas import tpu as pltpu
from jax.sharding import PartitionSpec as P

F32 = jnp.float32
BF16 = jnp.bfloat16
LANES = 128
GROUP = 8
CORES = 2
ROW, FIRST, SLOT, LAST, BLOCKS = range(5)


def over(axis, shard, pairs):
    return lax.ppermute(shard, axis, pairs)


def swap_cores(shard):
    count = lax.axis_size("fsdp")
    return over("fsdp", shard, [(i, i ^ 1) for i in range(count)])


def to_chip(shard, by):
    count = lax.axis_size("fsdp")
    return over("fsdp", shard, [(i, (i + CORES * by) % count) for i in range(count)])


def costs(flops, moved):
    return pl.CostEstimate(flops=flops, bytes_accessed=moved, transcendentals=0)


ANYWHERE = pl.BlockSpec(memory_space=pl.ANY)


def params():
    return pltpu.CompilerParams(vmem_limit_bytes=20 << 20)


def lookup_kernel(info, idx, amp, fa, aw, table, out, code, low_part, high, low, spread, split, edge):
    rows = table.shape[0]
    whole = rows // LANES * LANES
    rest = rows - whole
    high_count = spread.shape[1] // LANES
    groups, lanes = idx.shape
    per_sample = lanes // GROUP

    @pl.when(pl.program_id(0) == 0)
    def build():
        local_row = idx[...] - info[ROW]
        inside = (local_row >= 0) & (local_row < rows)
        sample = lax.broadcasted_iota(jnp.int32, idx.shape, 1) // per_sample
        code[...] = jnp.where(inside, (local_row // LANES) * GROUP + sample, -1)
        low_part[...] = local_row % LANES
        high[...] = amp[...].astype(BF16).astype(F32)
        low[...] = amp[...] - high[...]
        row_id = lax.broadcasted_iota(jnp.int32, (high_count * GROUP, lanes), 0)
        lane_id = lax.broadcasted_iota(jnp.int32, (LANES, lanes), 0)

        def one(group, unused):
            here = pl.ds(group, 1)
            matched = code[here, :] == row_id
            left_high = jnp.where(matched, high[here, :], 0.0).astype(BF16)
            left_low = jnp.where(matched, low[here, :], 0.0).astype(BF16)
            right = jnp.where(low_part[here, :] == lane_id, 1.0, 0.0).astype(BF16)
            left = jnp.concatenate([left_high, left_low], axis=0)
            summed = lax.dot_general(left, right, NT, preferred_element_type=F32)
            summed = summed[:high_count * GROUP] + summed[high_count * GROUP:]
            for k in range(high_count):
                spread[pl.ds(pl.multiple_of(group * GROUP, GROUP), GROUP), k * LANES:(k + 1) * LANES] = (
                    summed[k * GROUP:(k + 1) * GROUP, :]
                )
            return unused

        lax.fori_loop(0, groups, one, 0, unroll=8)
        split[...] = spread[...].astype(BF16)

    angular = fa[:, 0:1] * aw[0:1, :] + fa[:, 1:2] * aw[1:2, :]
    total = jnp.where(info[FIRST] == 1, angular, 0.0)
    if whole:
        total += jnp.dot(split[:, :whole], table[:whole, :], preferred_element_type=F32)
    if rest:
        edge[...] = jnp.zeros(edge.shape, BF16)
        edge[:rest, :] = table[whole:, :]
        total += jnp.dot(split[:, whole:], edge[...], preferred_element_type=F32)
    out[...] = total.astype(BF16)


def lookup_sum(table, seg_index, seg_amp, field_angle, angle_weight, info):
    rows, width = table.shape
    samples, active = seg_index.shape
    groups, lanes = samples // GROUP, GROUP * active
    columns = -(-rows // LANES) * LANES
    block = min(width, 256)
    small = pl.BlockSpec((groups, lanes), lambda n, info: (0, 0))
    return pl.pallas_call(
        lookup_kernel,
        grid_spec=pltpu.PrefetchScalarGridSpec(
            num_scalar_prefetch=1,
            grid=(width // block,),
            in_specs=[
                small,
                small,
                pl.BlockSpec((samples, 2), lambda n, info: (0, 0)),
                pl.BlockSpec((2, block), lambda n, info: (0, n)),
                pl.BlockSpec((rows, block), lambda n, info: (0, n)),
            ],
            out_specs=pl.BlockSpec((samples, block), lambda n, info: (0, n)),
            scratch_shapes=[
                pltpu.VMEM((groups, lanes), jnp.int32),
                pltpu.VMEM((groups, lanes), jnp.int32),
                pltpu.VMEM((groups, lanes), F32),
                pltpu.VMEM((groups, lanes), F32),
                pltpu.VMEM((samples, columns), F32),
                pltpu.VMEM((samples, columns), BF16),
                pltpu.VMEM((LANES, block), BF16),
            ],
        ),
        out_shape=jax.ShapeDtypeStruct((samples, width), BF16),
        compiler_params=params(),
        cost_estimate=costs(10 * samples * rows * width, 2 * rows * width),
        name="lookup_sum",
    )(info, seg_index.reshape(groups, lanes), seg_amp.reshape(groups, lanes), field_angle, angle_weight, table)


NT = (((1,), (1,)), ((), ()))


def cuts(rows):
    return [rows // 8 * 3, rows - rows // 8 * 3]


def first_terms_kernel(info, came, pre, target, first, second, after, later, grad, *outs):
    piece = 32

    @pl.when(pl.program_id(0) == 0)
    def differentiate():
        def one(k, unused):
            span = pl.ds(pl.multiple_of(k * piece, piece), piece)
            act, pullback = jax.vjp(jax.nn.gelu, pre[0, 0, span, :].astype(F32))
            slope = pullback(jnp.ones_like(act))[0]
            missed = act - target[span, :].astype(F32)
            cotangent = jnp.where(info[LAST] == 1, missed, came[span, :].astype(F32))
            grad[span, :] = (cotangent * slope).astype(BF16)
            return unused

        lax.fori_loop(0, grad.shape[0] // piece, one, 0)

    cut = outs[0].shape[0]
    for block, (upper, lower) in zip((first, second), (outs[:2], outs[2:])):
        term = lax.dot_general(grad[...], block[...], NT, preferred_element_type=F32).astype(BF16)
        upper[...] = term[:cut]
        lower[...] = term[cut:]


def first_terms(came, stash_pre, target, weight, info, at, after, later):
    rows, width = came.shape
    block = min(width, 256)
    steps = width // block
    pieces = cuts(rows) * 2
    shapes = [jax.ShapeDtypeStruct((piece, width), BF16) for piece in pieces]
    whole = pl.BlockSpec((rows, width), lambda n, info: (0, 0))
    out_specs = [pl.BlockSpec((piece, block), lambda n, info: (0, n)) for piece in pieces]
    return pl.pallas_call(
        first_terms_kernel,
        grid_spec=pltpu.PrefetchScalarGridSpec(
            num_scalar_prefetch=1,
            grid=(steps,),
            in_specs=[
                whole,
                pl.BlockSpec((1, 1, rows, width), lambda n, info: (0, info[SLOT], 0, 0)),
                whole,
                pl.BlockSpec((block, width), lambda n, info: (info[at + 1] * steps + n, 0)),
                pl.BlockSpec((block, width), lambda n, info: (info[at] * steps + n, 0)),
                ANYWHERE,
                ANYWHERE,
            ],
            out_specs=[whole] + out_specs,
        ),
        out_shape=[jax.ShapeDtypeStruct((rows, width), BF16)] + shapes,
        compiler_params=params(),
        cost_estimate=costs(4 * rows * width * width, 4 * width * width + 6 * rows * width),
        name="gradient_terms",
    )(info, came, stash_pre, target, weight, weight, after, later)


def terms_kernel(info, grad, first, second, after, later, first_out, second_out):
    first_out[...] = lax.dot_general(grad[...], first[...], NT, preferred_element_type=F32).astype(BF16)
    second_out[...] = lax.dot_general(grad[...], second[...], NT, preferred_element_type=F32).astype(BF16)


def terms(grad, weight, info, at, after, later):
    rows, width = grad.shape
    block = min(width, 512)
    steps = width // block
    shape = jax.ShapeDtypeStruct((rows, width), BF16)
    out_spec = pl.BlockSpec((rows, block), lambda n, info: (0, n))
    return pl.pallas_call(
        terms_kernel,
        grid_spec=pltpu.PrefetchScalarGridSpec(
            num_scalar_prefetch=1,
            grid=(steps,),
            in_specs=[
                pl.BlockSpec((rows, width), lambda n, info: (0, 0)),
                pl.BlockSpec((block, width), lambda n, info: (info[at + 1] * steps + n, 0)),
                pl.BlockSpec((block, width), lambda n, info: (info[at] * steps + n, 0)),
                ANYWHERE,
                ANYWHERE,
            ],
            out_specs=[out_spec, out_spec],
        ),
        out_shape=[shape, shape],
        compiler_params=params(),
        cost_estimate=costs(0, 0),
        name="input_terms",
    )(info, grad, weight, weight, after, later)


def forward_kernel(finish, count, info, *refs):
    pieces, blocks, carry, out = refs[:count], refs[count:2 * count], refs[2 * count], refs[-1]
    total = carry[...]
    for piece, block in zip(pieces, blocks):
        total += jnp.dot(piece[...], block[...], preferred_element_type=F32)
    if finish:
        total = jax.nn.gelu(total)
    out[...] = total.astype(out.dtype)


def forward_step(pieces, ats, weight, info, carry, rows, h, finish, before):
    half, width = pieces[0].shape
    count = len(pieces)
    block = min(width, 512)
    piece = pl.BlockSpec((half, width), lambda n, info: (0, 0))
    out_rows, place = (rows, h) if finish else (half, 0)
    return pl.pallas_call(
        functools.partial(forward_kernel, finish, count),
        grid_spec=pltpu.PrefetchScalarGridSpec(
            num_scalar_prefetch=1,
            grid=(width // block,),
            in_specs=[piece] * count
            + [pl.BlockSpec((width, block), functools.partial(lambda at, n, info: (info[at], n), at)) for at in ats]
            + [pl.BlockSpec((carry.shape[0], block), lambda n, info: (0, n)), ANYWHERE],
            out_specs=pl.BlockSpec((half, block), lambda n, info: (place, n)),
        ),
        out_shape=jax.ShapeDtypeStruct((out_rows, width), BF16 if finish else F32),
        input_output_aliases={2 * count + 2: 0} if finish and h else {},
        compiler_params=params(),
        cost_estimate=costs(2 * count * half * width * width, 2 * count * width * width + 8 * half * width),
        name="forward_step",
    )(info, *pieces, *[weight] * count, carry, before)


def step_down(shard, stride):
    sections = lax.axis_size("section")
    return over("section", shard, [(s, s - stride) for s in range(stride, sections, 2 * stride)])


def local(
    sent_act,
    sent_grad,
    stash_in,
    stash_pre,
    layer_weight,
    layer_bias,
    seg_table,
    seg_index,
    seg_amp,
    field_angle,
    angle_weight,
    target,
    sched,
):
    section = lax.axis_index("section")
    sections = lax.axis_size("section")
    me = lax.axis_index("fsdp")
    count = lax.axis_size("fsdp")
    chips = count // CORES
    rows = sent_act.shape[1]
    halves = 2
    half = rows // halves
    weight = layer_weight[0]

    numbers = [section * seg_table.shape[0], section == 0, sched[0], section == sections - 1]
    for by in range(chips):
        base = lax.rem(me // CORES + by, chips) * CORES
        core = lax.rem(me, CORES)
        numbers += [base + core, base + 1 - core]
    info = jnp.stack([jnp.asarray(number, jnp.int32) for number in numbers])
    is_first = section == 0
    stashed_in = lax.dynamic_index_in_dim(stash_in[0], sched[0], 0, keepdims=False)
    stashed_full = lax.all_gather(stashed_in, "fsdp", axis=1, tiled=True)

    from_before = over("section", sent_act[0], [(s, s + 1) for s in range(sections - 1)])
    from_next = over("section", sent_grad[0], [(s, s - 1) for s in range(1, sections)])
    rounded = lookup_sum(seg_table, seg_index, seg_amp, field_angle, angle_weight, info)

    received = []
    for by in range(1, chips):
        at = BLOCKS + 2 * by
        if by == 1:
            pre_grad, *terms_out = first_terms(
                from_next, stash_pre, target, weight, info, at, rounded, from_before
            )
            to_other, kept = terms_out[:2], terms_out[2:]
        else:
            to_other, kept = [
                [term[:cuts(rows)[0]], term[cuts(rows)[0]:]]
                for term in terms(pre_grad, weight, info, at, info, info)
            ]
        both = [
            (mine.astype(F32) + swap_cores(other).astype(F32)).astype(BF16)
            for mine, other in zip(kept, to_other)
        ]
        if by == 1:
            token = both[0]
        received.append([to_chip(piece, by) for piece in both])
    grad_bias = jnp.sum(pre_grad.astype(F32), axis=0)

    early = rows // 4 * 3
    near = step_down(rounded[:early], 1)
    near, token = lax.optimization_barrier((near, token))
    late = step_down(rounded[early:], 1)
    leaving = [(rounded[:half].astype(F32) + near[:half].astype(F32)).astype(BF16)]
    grad_w = lax.dot_general(
        stashed_full, pre_grad, (((0,), (0,)), ((), ())), preferred_element_type=F32
    ).astype(BF16)
    late, grad_w, kept_back = lax.optimization_barrier((late, grad_w, leaving[0]))
    late = jnp.concatenate([near[half:], late], axis=0)
    leaving.append((rounded[half:].astype(F32) + late.astype(F32)).astype(BF16))
    stride = 2
    while 2 * stride < sections:
        kept_back = None
        leaving = [(piece.astype(F32) + step_down(piece, stride).astype(F32)).astype(BF16) for piece in leaving]
        stride *= 2
    last = [step_down(leaving[0], stride)]
    last.append(step_down(leaving[1], stride))
    last[0], received[0], grad_w, grad_bias = lax.optimization_barrier(
        (last[0], received[0], grad_w, grad_bias)
    )

    if kept_back is not None:
        leaving[0] = kept_back
    inputs, carries = [], []
    for h in range(halves):
        first_input = (leaving[h].astype(F32) + last[h].astype(F32)).astype(BF16)
        inputs.append(jnp.where(is_first, first_input, from_before[h * half:(h + 1) * half]))
        carry = forward_step(
            [inputs[h], swap_cores(inputs[h])], [BLOCKS, BLOCKS + 1], weight, info, layer_bias, rows, h, False, info
        )
        if h == 0:
            to_other, kept = terms(pre_grad, weight, info, BLOCKS, inputs[0], token)
            last[1], to_other = lax.optimization_barrier((last[1], to_other))
        carries.append(carry)
    beside = kept.astype(F32) + swap_cores(to_other).astype(F32)
    far = [sum(part[h].astype(F32) for part in received) for h in range(2)]
    grad_in = (beside + jnp.concatenate(far, axis=0)).astype(BF16)
    fwd_out = info
    for h, carry in enumerate(carries):
        for by in range(1, chips):
            at = BLOCKS + 2 * by
            finish = by == chips - 1
            arrived = to_chip(inputs[h], chips - by)
            if h:
                arrived, fwd_out, grad_in = lax.optimization_barrier((arrived, fwd_out, grad_in))
                carry = forward_step([arrived], [at], weight, info, carry, rows, h, False, info)
                carry = forward_step(
                    [swap_cores(arrived)], [at + 1], weight, info, carry, rows, h, finish, fwd_out
                )
            else:
                before = carries[-1] if by == 1 else info
                carry = forward_step(
                    [arrived, swap_cores(arrived)], [at, at + 1], weight, info, carry, rows, h, finish, before
                )
        fwd_out = carry
    return (fwd_out[None], grad_in[None], grad_w[None], grad_bias[None])


def solution(mesh):
    return jax.shard_map(
        local,
        mesh=mesh,
        in_specs=(
            P("section", "groups", "fsdp"),
            P("section", "groups", "fsdp"),
            P("section", None, "groups", "fsdp"),
            P("section", None, "groups", "fsdp"),
            P("section", None, "fsdp"),
            P("section", "fsdp"),
            P("section", "fsdp"),
            P("groups", None),
            P("groups", None),
            P("groups", None),
            P(None, "fsdp"),
            P("groups", "fsdp"),
            P("section"),
        ),
        out_specs=(
            P("section", "groups", "fsdp"),
            P("section", "groups", "fsdp"),
            P("section", "groups", "fsdp"),
            P("section", ("groups", "fsdp")),
        ),
        check_vma=False,
    )
```

```python
import functools

import jax
import jax.numpy as jnp
from jax import lax
from jax.experimental import pallas as pl
from jax.experimental.pallas import tpu as pltpu
from jax.sharding import PartitionSpec as P

F32 = jnp.float32
BF16 = jnp.bfloat16
LANES = 128
GROUP = 8
CORES = 2
ROW, FIRST, SLOT, LAST, BLOCKS = range(5)


def over(axis, shard, pairs):
    return lax.ppermute(shard, axis, pairs)


def swap_cores(shard):
    count = lax.axis_size("fsdp")
    return over("fsdp", shard, [(i, i ^ 1) for i in range(count)])


def to_chip(shard, by):
    count = lax.axis_size("fsdp")
    return over("fsdp", shard, [(i, (i + CORES * by) % count) for i in range(count)])


def costs(flops, moved):
    return pl.CostEstimate(flops=flops, bytes_accessed=moved, transcendentals=0)


ANYWHERE = pl.BlockSpec(memory_space=pl.ANY)


def params():
    return pltpu.CompilerParams(vmem_limit_bytes=16 << 20)


def lookup_kernel(info, idx, amp, fa, aw, table, out, code, low_part, high, low, spread, split, edge):
    rows = table.shape[0]
    whole = rows // LANES * LANES
    rest = rows - whole
    high_count = spread.shape[1] // LANES
    groups, lanes = idx.shape
    per_sample = lanes // GROUP

    @pl.when(pl.program_id(0) == 0)
    def build():
        local_row = idx[...] - info[ROW]
        inside = (local_row >= 0) & (local_row < rows)
        sample = lax.broadcasted_iota(jnp.int32, idx.shape, 1) // per_sample
        code[...] = jnp.where(inside, (local_row // LANES) * GROUP + sample, -1)
        low_part[...] = local_row % LANES
        high[...] = amp[...].astype(BF16).astype(F32)
        low[...] = amp[...] - high[...]
        row_id = lax.broadcasted_iota(jnp.int32, (high_count * GROUP, lanes), 0)
        lane_id = lax.broadcasted_iota(jnp.int32, (LANES, lanes), 0)

        def one(group, unused):
            here = pl.ds(group, 1)
            matched = code[here, :] == row_id
            left_high = jnp.where(matched, high[here, :], 0.0).astype(BF16)
            left_low = jnp.where(matched, low[here, :], 0.0).astype(BF16)
            right = jnp.where(low_part[here, :] == lane_id, 1.0, 0.0).astype(BF16)
            left = jnp.concatenate([left_high, left_low], axis=0)
            summed = lax.dot_general(left, right, NT, preferred_element_type=F32)
            summed = summed[:high_count * GROUP] + summed[high_count * GROUP:]
            for k in range(high_count):
                spread[pl.ds(pl.multiple_of(group * GROUP, GROUP), GROUP), k * LANES:(k + 1) * LANES] = (
                    summed[k * GROUP:(k + 1) * GROUP, :]
                )
            return unused

        lax.fori_loop(0, groups, one, 0, unroll=8)
        split[...] = spread[...].astype(BF16)

    angular = fa[:, 0:1] * aw[0:1, :] + fa[:, 1:2] * aw[1:2, :]
    total = jnp.where(info[FIRST] == 1, angular, 0.0)
    if whole:
        total += jnp.dot(split[:, :whole], table[:whole, :], preferred_element_type=F32)
    if rest:
        edge[...] = jnp.zeros(edge.shape, BF16)
        edge[:rest, :] = table[whole:, :]
        total += jnp.dot(split[:, whole:], edge[...], preferred_element_type=F32)
    out[...] = total.astype(BF16)


def lookup_sum(table, seg_index, seg_amp, field_angle, angle_weight, info):
    rows, width = table.shape
    samples, active = seg_index.shape
    groups, lanes = samples // GROUP, GROUP * active
    columns = -(-rows // LANES) * LANES
    block = min(width, 256)
    small = pl.BlockSpec((groups, lanes), lambda n, info: (0, 0))
    return pl.pallas_call(
        lookup_kernel,
        grid_spec=pltpu.PrefetchScalarGridSpec(
            num_scalar_prefetch=1,
            grid=(width // block,),
            in_specs=[
                small,
                small,
                pl.BlockSpec((samples, 2), lambda n, info: (0, 0)),
                pl.BlockSpec((2, block), lambda n, info: (0, n)),
                pl.BlockSpec((rows, block), lambda n, info: (0, n)),
            ],
            out_specs=pl.BlockSpec((samples, block), lambda n, info: (0, n)),
            scratch_shapes=[
                pltpu.VMEM((groups, lanes), jnp.int32),
                pltpu.VMEM((groups, lanes), jnp.int32),
                pltpu.VMEM((groups, lanes), F32),
                pltpu.VMEM((groups, lanes), F32),
                pltpu.VMEM((samples, columns), F32),
                pltpu.VMEM((samples, columns), BF16),
                pltpu.VMEM((LANES, block), BF16),
            ],
        ),
        out_shape=jax.ShapeDtypeStruct((samples, width), BF16),
        compiler_params=params(),
        cost_estimate=costs(10 * samples * rows * width, 2 * rows * width),
        name="lookup_sum",
    )(info, seg_index.reshape(groups, lanes), seg_amp.reshape(groups, lanes), field_angle, angle_weight, table)


NT = (((1,), (1,)), ((), ()))


def cuts(rows):
    return [rows // 8 * 3, rows - rows // 8 * 3]


def slopes_kernel(info, pre, target, after, slope, closing):
    act, pullback = jax.vjp(jax.nn.gelu, pre[0, 0].astype(F32))
    slope[...] = pullback(jnp.ones_like(act))[0]
    closing[...] = ((act - target[...].astype(F32)) * slope[...]).astype(BF16)


def slopes(stash_pre, target, info, after):
    rows, width = target.shape
    block = min(rows, 64)
    span = pl.BlockSpec((block, width), lambda n, info: (n, 0))
    return pl.pallas_call(
        slopes_kernel,
        grid_spec=pltpu.PrefetchScalarGridSpec(
            num_scalar_prefetch=1,
            grid=(rows // block,),
            in_specs=[
                pl.BlockSpec((1, 1, block, width), lambda n, info: (0, info[SLOT], n, 0)),
                span,
                ANYWHERE,
            ],
            out_specs=[span, span],
        ),
        out_shape=[jax.ShapeDtypeStruct((rows, width), F32), jax.ShapeDtypeStruct((rows, width), BF16)],
        compiler_params=params(),
        cost_estimate=costs(0, 10 * rows * width),
        name="slopes",
    )(info, stash_pre, target, after)


def first_terms_kernel(info, came, slope, closing, first, second, grad, *outs):
    @pl.when(pl.program_id(0) == 0)
    def differentiate():
        grad[...] = jnp.where(info[LAST] == 1, closing[...], (came[...].astype(F32) * slope[...]).astype(BF16))

    cut = outs[0].shape[0]
    for block, (upper, lower) in zip((first, second), (outs[:2], outs[2:])):
        term = lax.dot_general(grad[...], block[...], NT, preferred_element_type=F32).astype(BF16)
        upper[...] = term[:cut]
        lower[...] = term[cut:]


def first_terms(came, slope, closing, weight, info, at):
    rows, width = came.shape
    block = min(width, 256)
    steps = width // block
    pieces = cuts(rows) * 2
    shapes = [jax.ShapeDtypeStruct((piece, width), BF16) for piece in pieces]
    whole = pl.BlockSpec((rows, width), lambda n, info: (0, 0))
    out_specs = [pl.BlockSpec((piece, block), lambda n, info: (0, n)) for piece in pieces]
    return pl.pallas_call(
        first_terms_kernel,
        grid_spec=pltpu.PrefetchScalarGridSpec(
            num_scalar_prefetch=1,
            grid=(steps,),
            in_specs=[
                whole,
                whole,
                whole,
                pl.BlockSpec((block, width), lambda n, info: (info[at + 1] * steps + n, 0)),
                pl.BlockSpec((block, width), lambda n, info: (info[at] * steps + n, 0)),
            ],
            out_specs=[whole] + out_specs,
        ),
        out_shape=[jax.ShapeDtypeStruct((rows, width), BF16)] + shapes,
        compiler_params=params(),
        cost_estimate=costs(4 * rows * width * width, 4 * width * width + 6 * rows * width),
        name="gradient_terms",
    )(info, came, slope, closing, weight, weight)


def terms_kernel(info, grad, first, second, after, later, first_out, second_out):
    first_out[...] = lax.dot_general(grad[...], first[...], NT, preferred_element_type=F32).astype(BF16)
    second_out[...] = lax.dot_general(grad[...], second[...], NT, preferred_element_type=F32).astype(BF16)


def terms(grad, weight, info, at, after, later):
    rows, width = grad.shape
    block = min(width, 512)
    steps = width // block
    shape = jax.ShapeDtypeStruct((rows, width), BF16)
    out_spec = pl.BlockSpec((rows, block), lambda n, info: (0, n))
    return pl.pallas_call(
        terms_kernel,
        grid_spec=pltpu.PrefetchScalarGridSpec(
            num_scalar_prefetch=1,
            grid=(steps,),
            in_specs=[
                pl.BlockSpec((rows, width), lambda n, info: (0, 0)),
                pl.BlockSpec((block, width), lambda n, info: (info[at + 1] * steps + n, 0)),
                pl.BlockSpec((block, width), lambda n, info: (info[at] * steps + n, 0)),
                ANYWHERE,
                ANYWHERE,
            ],
            out_specs=[out_spec, out_spec],
        ),
        out_shape=[shape, shape],
        compiler_params=params(),
        cost_estimate=costs(0, 0),
        name="input_terms",
    )(info, grad, weight, weight, after, later)


def forward_kernel(finish, count, info, *refs):
    pieces, blocks, carry, out = refs[:count], refs[count:2 * count], refs[2 * count], refs[-1]
    total = carry[...]
    for piece, block in zip(pieces, blocks):
        total += jnp.dot(piece[...], block[...], preferred_element_type=F32)
    if finish:
        total = jax.nn.gelu(total)
    out[...] = total.astype(out.dtype)


def forward_step(pieces, ats, weight, info, carry, rows, h, finish, before):
    half, width = pieces[0].shape
    count = len(pieces)
    block = min(width, 512)
    piece = pl.BlockSpec((half, width), lambda n, info: (0, 0))
    out_rows, place = (rows, h) if finish else (half, 0)
    return pl.pallas_call(
        functools.partial(forward_kernel, finish, count),
        grid_spec=pltpu.PrefetchScalarGridSpec(
            num_scalar_prefetch=1,
            grid=(width // block,),
            in_specs=[piece] * count
            + [pl.BlockSpec((width, block), functools.partial(lambda at, n, info: (info[at], n), at)) for at in ats]
            + [pl.BlockSpec((carry.shape[0], block), lambda n, info: (0, n)), ANYWHERE],
            out_specs=pl.BlockSpec((half, block), lambda n, info: (place, n)),
        ),
        out_shape=jax.ShapeDtypeStruct((out_rows, width), BF16 if finish else F32),
        input_output_aliases={2 * count + 2: 0} if finish and h else {},
        compiler_params=params(),
        cost_estimate=costs(2 * count * half * width * width, 2 * count * width * width + 8 * half * width),
        name="forward_step",
    )(info, *pieces, *[weight] * count, carry, before)


def step_down(shard, stride):
    sections = lax.axis_size("section")
    return over("section", shard, [(s, s - stride) for s in range(stride, sections, 2 * stride)])


def local(
    sent_act,
    sent_grad,
    stash_in,
    stash_pre,
    layer_weight,
    layer_bias,
    seg_table,
    seg_index,
    seg_amp,
    field_angle,
    angle_weight,
    target,
    sched,
):
    section = lax.axis_index("section")
    sections = lax.axis_size("section")
    me = lax.axis_index("fsdp")
    count = lax.axis_size("fsdp")
    chips = count // CORES
    rows = sent_act.shape[1]
    halves = 2
    half = rows // halves
    weight = layer_weight[0]

    numbers = [section * seg_table.shape[0], section == 0, sched[0], section == sections - 1]
    for by in range(chips):
        base = lax.rem(me // CORES + by, chips) * CORES
        core = lax.rem(me, CORES)
        numbers += [base + core, base + 1 - core]
    info = jnp.stack([jnp.asarray(number, jnp.int32) for number in numbers])
    is_first = section == 0
    stashed_in = lax.dynamic_index_in_dim(stash_in[0], sched[0], 0, keepdims=False)
    stashed_full = lax.all_gather(stashed_in, "fsdp", axis=1, tiled=True)

    from_before = over("section", sent_act[0], [(s, s + 1) for s in range(sections - 1)])
    from_next = over("section", sent_grad[0], [(s, s - 1) for s in range(1, sections)])
    rounded = lookup_sum(seg_table, seg_index, seg_amp, field_angle, angle_weight, info)

    received = []
    for by in range(1, chips):
        at = BLOCKS + 2 * by
        if by == 1:
            slope, closing = slopes(stash_pre, target, info, rounded)
            pre_grad, *terms_out = first_terms(from_next, slope, closing, weight, info, at)
            to_other, kept = terms_out[:2], terms_out[2:]
        else:
            to_other, kept = [
                [term[:cuts(rows)[0]], term[cuts(rows)[0]:]]
                for term in terms(pre_grad, weight, info, at, info, info)
            ]
        both = [
            (mine.astype(F32) + swap_cores(other).astype(F32)).astype(BF16)
            for mine, other in zip(kept, to_other)
        ]
        if by == 1:
            token = both[0]
        received.append([to_chip(piece, by) for piece in both])
    grad_bias = jnp.sum(pre_grad.astype(F32), axis=0)

    early = rows // 4 * 3
    near = step_down(rounded[:early], 1)
    near, token, from_before = lax.optimization_barrier((near, token, from_before))
    late = step_down(rounded[early:], 1)
    leaving = [(rounded[:half].astype(F32) + near[:half].astype(F32)).astype(BF16)]
    grad_w = lax.dot_general(
        stashed_full, pre_grad, (((0,), (0,)), ((), ())), preferred_element_type=F32
    ).astype(BF16)
    late, grad_w, kept_back = lax.optimization_barrier((late, grad_w, leaving[0]))
    late = jnp.concatenate([near[half:], late], axis=0)
    leaving.append((rounded[half:].astype(F32) + late.astype(F32)).astype(BF16))
    stride = 2
    while 2 * stride < sections:
        kept_back = None
        leaving = [(piece.astype(F32) + step_down(piece, stride).astype(F32)).astype(BF16) for piece in leaving]
        stride *= 2
    last = [step_down(leaving[0], stride)]
    last.append(step_down(leaving[1], stride))
    last[0], received[0], grad_w, grad_bias = lax.optimization_barrier(
        (last[0], received[0], grad_w, grad_bias)
    )

    if kept_back is not None:
        leaving[0] = kept_back
    inputs, carries = [], []
    for h in range(halves):
        first_input = (leaving[h].astype(F32) + last[h].astype(F32)).astype(BF16)
        inputs.append(jnp.where(is_first, first_input, from_before[h * half:(h + 1) * half]))
        carry = forward_step(
            [inputs[h], swap_cores(inputs[h])], [BLOCKS, BLOCKS + 1], weight, info, layer_bias, rows, h, False, info
        )
        if h == 0:
            to_other, kept = terms(pre_grad, weight, info, BLOCKS, inputs[0], token)
            last[1], to_other = lax.optimization_barrier((last[1], to_other))
        carries.append(carry)
    beside = kept.astype(F32) + swap_cores(to_other).astype(F32)
    far = [sum(part[h].astype(F32) for part in received) for h in range(2)]
    grad_in = (beside + jnp.concatenate(far, axis=0)).astype(BF16)
    fwd_out = info
    for h, carry in enumerate(carries):
        for by in range(1, chips):
            at = BLOCKS + 2 * by
            finish = by == chips - 1
            arrived = to_chip(inputs[h], chips - by)
            if h:
                arrived, fwd_out, grad_in = lax.optimization_barrier((arrived, fwd_out, grad_in))
                carry = forward_step([arrived], [at], weight, info, carry, rows, h, False, info)
                carry = forward_step(
                    [swap_cores(arrived)], [at + 1], weight, info, carry, rows, h, finish, fwd_out
                )
            else:
                before = carries[-1] if by == 1 else info
                carry = forward_step(
                    [arrived, swap_cores(arrived)], [at, at + 1], weight, info, carry, rows, h, finish, before
                )
        fwd_out = carry
    return (fwd_out[None], grad_in[None], grad_w[None], grad_bias[None])


def solution(mesh):
    return jax.shard_map(
        local,
        mesh=mesh,
        in_specs=(
            P("section", "groups", "fsdp"),
            P("section", "groups", "fsdp"),
            P("section", None, "groups", "fsdp"),
            P("section", None, "groups", "fsdp"),
            P("section", None, "fsdp"),
            P("section", "fsdp"),
            P("section", "fsdp"),
            P("groups", None),
            P("groups", None),
            P("groups", None),
            P(None, "fsdp"),
            P("groups", "fsdp"),
            P("section"),
        ),
        out_specs=(
            P("section", "groups", "fsdp"),
            P("section", "groups", "fsdp"),
            P("section", "groups", "fsdp"),
            P("section", ("groups", "fsdp")),
        ),
        check_vma=False,
    )
```

```python
import functools

import jax
import jax.numpy as jnp
from jax import lax
from jax.experimental import pallas as pl
from jax.experimental.pallas import tpu as pltpu
from jax.sharding import PartitionSpec as P

F32 = jnp.float32
BF16 = jnp.bfloat16
LANES = 128
GROUP = 8
CORES = 2
ROW, FIRST, SLOT, LAST, BLOCKS = range(5)


def over(axis, shard, pairs):
    return lax.ppermute(shard, axis, pairs)


def swap_cores(shard):
    count = lax.axis_size("fsdp")
    return over("fsdp", shard, [(i, i ^ 1) for i in range(count)])


def to_chip(shard, by):
    count = lax.axis_size("fsdp")
    return over("fsdp", shard, [(i, (i + CORES * by) % count) for i in range(count)])


def costs(flops, moved):
    return pl.CostEstimate(flops=flops, bytes_accessed=moved, transcendentals=0)


ANYWHERE = pl.BlockSpec(memory_space=pl.ANY)


def params():
    return pltpu.CompilerParams(vmem_limit_bytes=16 << 20)


def lookup_kernel(info, idx, amp, fa, aw, table, out, code, low_part, high, low, spread, split, edge):
    rows = table.shape[0]
    whole = rows // LANES * LANES
    rest = rows - whole
    high_count = spread.shape[1] // LANES
    groups, lanes = idx.shape
    per_sample = lanes // GROUP

    @pl.when(pl.program_id(0) == 0)
    def build():
        local_row = idx[...] - info[ROW]
        inside = (local_row >= 0) & (local_row < rows)
        sample = lax.broadcasted_iota(jnp.int32, idx.shape, 1) // per_sample
        code[...] = jnp.where(inside, (local_row // LANES) * GROUP + sample, -1)
        low_part[...] = local_row % LANES
        high[...] = amp[...].astype(BF16).astype(F32)
        low[...] = amp[...] - high[...]
        row_id = lax.broadcasted_iota(jnp.int32, (high_count * GROUP, lanes), 0)
        lane_id = lax.broadcasted_iota(jnp.int32, (LANES, lanes), 0)

        def one(group, unused):
            here = pl.ds(group, 1)
            matched = code[here, :] == row_id
            left_high = jnp.where(matched, high[here, :], 0.0).astype(BF16)
            left_low = jnp.where(matched, low[here, :], 0.0).astype(BF16)
            right = jnp.where(low_part[here, :] == lane_id, 1.0, 0.0).astype(BF16)
            left = jnp.concatenate([left_high, left_low], axis=0)
            summed = lax.dot_general(left, right, NT, preferred_element_type=F32)
            summed = summed[:high_count * GROUP] + summed[high_count * GROUP:]
            for k in range(high_count):
                spread[pl.ds(pl.multiple_of(group * GROUP, GROUP), GROUP), k * LANES:(k + 1) * LANES] = (
                    summed[k * GROUP:(k + 1) * GROUP, :]
                )
            return unused

        lax.fori_loop(0, groups, one, 0, unroll=8)
        split[...] = spread[...].astype(BF16)

    angular = fa[:, 0:1] * aw[0:1, :] + fa[:, 1:2] * aw[1:2, :]
    total = jnp.where(info[FIRST] == 1, angular, 0.0)
    if whole:
        total += jnp.dot(split[:, :whole], table[:whole, :], preferred_element_type=F32)
    if rest:
        edge[...] = jnp.zeros(edge.shape, BF16)
        edge[:rest, :] = table[whole:, :]
        total += jnp.dot(split[:, whole:], edge[...], preferred_element_type=F32)
    out[...] = total.astype(BF16)


def lookup_sum(table, seg_index, seg_amp, field_angle, angle_weight, info):
    rows, width = table.shape
    samples, active = seg_index.shape
    groups, lanes = samples // GROUP, GROUP * active
    columns = -(-rows // LANES) * LANES
    block = min(width, 256)
    small = pl.BlockSpec((groups, lanes), lambda n, info: (0, 0))
    return pl.pallas_call(
        lookup_kernel,
        grid_spec=pltpu.PrefetchScalarGridSpec(
            num_scalar_prefetch=1,
            grid=(width // block,),
            in_specs=[
                small,
                small,
                pl.BlockSpec((samples, 2), lambda n, info: (0, 0)),
                pl.BlockSpec((2, block), lambda n, info: (0, n)),
                pl.BlockSpec((rows, block), lambda n, info: (0, n)),
            ],
            out_specs=pl.BlockSpec((samples, block), lambda n, info: (0, n)),
            scratch_shapes=[
                pltpu.VMEM((groups, lanes), jnp.int32),
                pltpu.VMEM((groups, lanes), jnp.int32),
                pltpu.VMEM((groups, lanes), F32),
                pltpu.VMEM((groups, lanes), F32),
                pltpu.VMEM((samples, columns), F32),
                pltpu.VMEM((samples, columns), BF16),
                pltpu.VMEM((LANES, block), BF16),
            ],
        ),
        out_shape=jax.ShapeDtypeStruct((samples, width), BF16),
        compiler_params=params(),
        cost_estimate=costs(10 * samples * rows * width, 2 * rows * width),
        name="lookup_sum",
    )(info, seg_index.reshape(groups, lanes), seg_amp.reshape(groups, lanes), field_angle, angle_weight, table)


NT = (((1,), (1,)), ((), ()))


def cuts(rows):
    return [rows // 8 * 3, rows - rows // 8 * 3]


def slopes_kernel(info, pre, target, after, slope, closing):
    act, pullback = jax.vjp(jax.nn.gelu, pre[0, 0].astype(F32))
    slope[...] = pullback(jnp.ones_like(act))[0]
    closing[...] = ((act - target[...].astype(F32)) * slope[...]).astype(BF16)


def slopes(stash_pre, target, info, after):
    rows, width = target.shape
    block = min(rows, 64)
    span = pl.BlockSpec((block, width), lambda n, info: (n, 0))
    return pl.pallas_call(
        slopes_kernel,
        grid_spec=pltpu.PrefetchScalarGridSpec(
            num_scalar_prefetch=1,
            grid=(rows // block,),
            in_specs=[
                pl.BlockSpec((1, 1, block, width), lambda n, info: (0, info[SLOT], n, 0)),
                span,
                ANYWHERE,
            ],
            out_specs=[span, span],
        ),
        out_shape=[jax.ShapeDtypeStruct((rows, width), F32), jax.ShapeDtypeStruct((rows, width), BF16)],
        compiler_params=params(),
        cost_estimate=costs(8000 * rows * width, 10 * rows * width),
        name="slopes",
    )(info, stash_pre, target, after)


def first_terms_kernel(info, came, slope, closing, first, second, grad, *outs):
    @pl.when(pl.program_id(0) == 0)
    def differentiate():
        grad[...] = jnp.where(info[LAST] == 1, closing[...], (came[...].astype(F32) * slope[...]).astype(BF16))

    cut = outs[0].shape[0]
    for block, (upper, lower) in zip((first, second), (outs[:2], outs[2:])):
        term = lax.dot_general(grad[...], block[...], NT, preferred_element_type=F32).astype(BF16)
        upper[...] = term[:cut]
        lower[...] = term[cut:]


def first_terms(came, slope, closing, weight, info, at):
    rows, width = came.shape
    block = min(width, 256)
    steps = width // block
    pieces = cuts(rows) * 2
    shapes = [jax.ShapeDtypeStruct((piece, width), BF16) for piece in pieces]
    whole = pl.BlockSpec((rows, width), lambda n, info: (0, 0))
    out_specs = [pl.BlockSpec((piece, block), lambda n, info: (0, n)) for piece in pieces]
    return pl.pallas_call(
        first_terms_kernel,
        grid_spec=pltpu.PrefetchScalarGridSpec(
            num_scalar_prefetch=1,
            grid=(steps,),
            in_specs=[
                whole,
                whole,
                whole,
                pl.BlockSpec((block, width), lambda n, info: (info[at + 1] * steps + n, 0)),
                pl.BlockSpec((block, width), lambda n, info: (info[at] * steps + n, 0)),
            ],
            out_specs=[whole] + out_specs,
        ),
        out_shape=[jax.ShapeDtypeStruct((rows, width), BF16)] + shapes,
        compiler_params=params(),
        cost_estimate=costs(4 * rows * width * width, 4 * width * width + 6 * rows * width),
        name="gradient_terms",
    )(info, came, slope, closing, weight, weight)


def terms_kernel(info, grad, first, second, after, later, first_out, second_out):
    first_out[...] = lax.dot_general(grad[...], first[...], NT, preferred_element_type=F32).astype(BF16)
    second_out[...] = lax.dot_general(grad[...], second[...], NT, preferred_element_type=F32).astype(BF16)


def terms(grad, weight, info, at, after, later):
    rows, width = grad.shape
    block = min(width, 512)
    steps = width // block
    shape = jax.ShapeDtypeStruct((rows, width), BF16)
    out_spec = pl.BlockSpec((rows, block), lambda n, info: (0, n))
    return pl.pallas_call(
        terms_kernel,
        grid_spec=pltpu.PrefetchScalarGridSpec(
            num_scalar_prefetch=1,
            grid=(steps,),
            in_specs=[
                pl.BlockSpec((rows, width), lambda n, info: (0, 0)),
                pl.BlockSpec((block, width), lambda n, info: (info[at + 1] * steps + n, 0)),
                pl.BlockSpec((block, width), lambda n, info: (info[at] * steps + n, 0)),
                ANYWHERE,
                ANYWHERE,
            ],
            out_specs=[out_spec, out_spec],
        ),
        out_shape=[shape, shape],
        compiler_params=params(),
        cost_estimate=costs(0, 0),
        name="input_terms",
    )(info, grad, weight, weight, after, later)


def forward_kernel(finish, count, info, *refs):
    pieces, blocks, carry, out = refs[:count], refs[count:2 * count], refs[2 * count], refs[-1]
    total = carry[...]
    for piece, block in zip(pieces, blocks):
        total += jnp.dot(piece[...], block[...], preferred_element_type=F32)
    if finish:
        total = jax.nn.gelu(total)
    out[...] = total.astype(out.dtype)


def forward_step(pieces, ats, weight, info, carry, rows, h, finish, before):
    half, width = pieces[0].shape
    count = len(pieces)
    block = min(width, 512)
    piece = pl.BlockSpec((half, width), lambda n, info: (0, 0))
    out_rows, place = (rows, h) if finish else (half, 0)
    return pl.pallas_call(
        functools.partial(forward_kernel, finish, count),
        grid_spec=pltpu.PrefetchScalarGridSpec(
            num_scalar_prefetch=1,
            grid=(width // block,),
            in_specs=[piece] * count
            + [pl.BlockSpec((width, block), functools.partial(lambda at, n, info: (info[at], n), at)) for at in ats]
            + [pl.BlockSpec((carry.shape[0], block), lambda n, info: (0, n)), ANYWHERE],
            out_specs=pl.BlockSpec((half, block), lambda n, info: (place, n)),
        ),
        out_shape=jax.ShapeDtypeStruct((out_rows, width), BF16 if finish else F32),
        input_output_aliases={2 * count + 2: 0} if finish and h else {},
        compiler_params=params(),
        cost_estimate=costs(2 * count * half * width * width, 2 * count * width * width + 8 * half * width),
        name="forward_step",
    )(info, *pieces, *[weight] * count, carry, before)


def step_down(shard, stride):
    sections = lax.axis_size("section")
    return over("section", shard, [(s, s - stride) for s in range(stride, sections, 2 * stride)])


def local(
    sent_act,
    sent_grad,
    stash_in,
    stash_pre,
    layer_weight,
    layer_bias,
    seg_table,
    seg_index,
    seg_amp,
    field_angle,
    angle_weight,
    target,
    sched,
):
    section = lax.axis_index("section")
    sections = lax.axis_size("section")
    me = lax.axis_index("fsdp")
    count = lax.axis_size("fsdp")
    chips = count // CORES
    rows = sent_act.shape[1]
    halves = 2
    half = rows // halves
    weight = layer_weight[0]

    numbers = [section * seg_table.shape[0], section == 0, sched[0], section == sections - 1]
    for by in range(chips):
        base = lax.rem(me // CORES + by, chips) * CORES
        core = lax.rem(me, CORES)
        numbers += [base + core, base + 1 - core]
    info = jnp.stack([jnp.asarray(number, jnp.int32) for number in numbers])
    is_first = section == 0
    stashed_in = lax.dynamic_index_in_dim(stash_in[0], sched[0], 0, keepdims=False)
    stashed_full = lax.all_gather(stashed_in, "fsdp", axis=1, tiled=True)

    from_before = over("section", sent_act[0], [(s, s + 1) for s in range(sections - 1)])
    from_next = over("section", sent_grad[0], [(s, s - 1) for s in range(1, sections)])
    rounded = lookup_sum(seg_table, seg_index, seg_amp, field_angle, angle_weight, info)

    received = []
    for by in range(1, chips):
        at = BLOCKS + 2 * by
        if by == 1:
            slope, closing = slopes(stash_pre, target, info, rounded)
            pre_grad, *terms_out = first_terms(from_next, slope, closing, weight, info, at)
            to_other, kept = terms_out[:2], terms_out[2:]
        else:
            to_other, kept = [
                [term[:cuts(rows)[0]], term[cuts(rows)[0]:]]
                for term in terms(pre_grad, weight, info, at, info, info)
            ]
        both = [
            (mine.astype(F32) + swap_cores(other).astype(F32)).astype(BF16)
            for mine, other in zip(kept, to_other)
        ]
        if by == 1:
            token = both[0]
        received.append([to_chip(piece, by) for piece in both])
    grad_bias = jnp.sum(pre_grad.astype(F32), axis=0)

    early = rows // 4 * 3
    near = step_down(rounded[:early], 1)
    near, token, from_before = lax.optimization_barrier((near, token, from_before))
    late = step_down(rounded[early:], 1)
    leaving = [(rounded[:half].astype(F32) + near[:half].astype(F32)).astype(BF16)]
    grad_w = lax.dot_general(
        stashed_full, pre_grad, (((0,), (0,)), ((), ())), preferred_element_type=F32
    ).astype(BF16)
    late, grad_w, kept_back = lax.optimization_barrier((late, grad_w, leaving[0]))
    late = jnp.concatenate([near[half:], late], axis=0)
    leaving.append((rounded[half:].astype(F32) + late.astype(F32)).astype(BF16))
    stride = 2
    while 2 * stride < sections:
        kept_back = None
        leaving = [(piece.astype(F32) + step_down(piece, stride).astype(F32)).astype(BF16) for piece in leaving]
        stride *= 2
    last = [step_down(leaving[0], stride)]
    last.append(step_down(leaving[1], stride))
    last[0], received[0], grad_w = lax.optimization_barrier((last[0], received[0], grad_w))

    if kept_back is not None:
        leaving[0] = kept_back
    inputs, carries = [], []
    for h in range(halves):
        first_input = (leaving[h].astype(F32) + last[h].astype(F32)).astype(BF16)
        inputs.append(jnp.where(is_first, first_input, from_before[h * half:(h + 1) * half]))
        carry = forward_step(
            [inputs[h], swap_cores(inputs[h])], [BLOCKS, BLOCKS + 1], weight, info, layer_bias, rows, h, False, info
        )
        if h == 0:
            to_other, kept = terms(pre_grad, weight, info, BLOCKS, inputs[0], token)
            last[1], to_other, grad_bias = lax.optimization_barrier((last[1], to_other, grad_bias))
        carries.append(carry)
    beside = kept.astype(F32) + swap_cores(to_other).astype(F32)
    far = [sum(part[h].astype(F32) for part in received) for h in range(2)]
    grad_in = (beside + jnp.concatenate(far, axis=0)).astype(BF16)
    fwd_out = info
    for h, carry in enumerate(carries):
        for by in range(1, chips):
            at = BLOCKS + 2 * by
            finish = by == chips - 1
            arrived = to_chip(inputs[h], chips - by)
            if h:
                arrived, fwd_out, grad_in = lax.optimization_barrier((arrived, fwd_out, grad_in))
                carry = forward_step([arrived], [at], weight, info, carry, rows, h, False, info)
                carry = forward_step(
                    [swap_cores(arrived)], [at + 1], weight, info, carry, rows, h, finish, fwd_out
                )
            else:
                before = carries[-1] if by == 1 else info
                carry = forward_step(
                    [arrived, swap_cores(arrived)], [at, at + 1], weight, info, carry, rows, h, finish, before
                )
        fwd_out = carry
    return (fwd_out[None], grad_in[None], grad_w[None], grad_bias[None])


def solution(mesh):
    return jax.shard_map(
        local,
        mesh=mesh,
        in_specs=(
            P("section", "groups", "fsdp"),
            P("section", "groups", "fsdp"),
            P("section", None, "groups", "fsdp"),
            P("section", None, "groups", "fsdp"),
            P("section", None, "fsdp"),
            P("section", "fsdp"),
            P("section", "fsdp"),
            P("groups", None),
            P("groups", None),
            P("groups", None),
            P(None, "fsdp"),
            P("groups", "fsdp"),
            P("section"),
        ),
        out_specs=(
            P("section", "groups", "fsdp"),
            P("section", "groups", "fsdp"),
            P("section", "groups", "fsdp"),
            P("section", ("groups", "fsdp")),
        ),
        check_vma=False,
    )
```

```python
import functools

import jax
import jax.numpy as jnp
from jax import lax
from jax.experimental import pallas as pl
from jax.experimental.pallas import tpu as pltpu
from jax.sharding import PartitionSpec as P

F32 = jnp.float32
BF16 = jnp.bfloat16
LANES = 128
GROUP = 8
CORES = 2
ROW, FIRST, SLOT, LAST, BLOCKS = range(5)


def over(axis, shard, pairs):
    return lax.ppermute(shard, axis, pairs)


def swap_cores(shard):
    count = lax.axis_size("fsdp")
    return over("fsdp", shard, [(i, i ^ 1) for i in range(count)])


def to_chip(shard, by):
    count = lax.axis_size("fsdp")
    return over("fsdp", shard, [(i, (i + CORES * by) % count) for i in range(count)])


def costs(flops, moved):
    return pl.CostEstimate(flops=flops, bytes_accessed=moved, transcendentals=0)


ANYWHERE = pl.BlockSpec(memory_space=pl.ANY)


def params():
    return pltpu.CompilerParams(vmem_limit_bytes=16 << 20)


def lookup_kernel(info, idx, amp, fa, aw, table, out, code, low_part, high, low, spread, split, edge):
    rows = table.shape[0]
    whole = rows // LANES * LANES
    rest = rows - whole
    high_count = spread.shape[1] // LANES
    groups, lanes = idx.shape
    per_sample = lanes // GROUP

    @pl.when(pl.program_id(0) == 0)
    def build():
        local_row = idx[...] - info[ROW]
        inside = (local_row >= 0) & (local_row < rows)
        sample = lax.broadcasted_iota(jnp.int32, idx.shape, 1) // per_sample
        code[...] = jnp.where(inside, (local_row // LANES) * GROUP + sample, -1)
        low_part[...] = local_row % LANES
        high[...] = amp[...].astype(BF16).astype(F32)
        low[...] = amp[...] - high[...]
        row_id = lax.broadcasted_iota(jnp.int32, (high_count * GROUP, lanes), 0)
        lane_id = lax.broadcasted_iota(jnp.int32, (LANES, lanes), 0)

        def one(group, unused):
            here = pl.ds(group, 1)
            matched = code[here, :] == row_id
            left_high = jnp.where(matched, high[here, :], 0.0).astype(BF16)
            left_low = jnp.where(matched, low[here, :], 0.0).astype(BF16)
            right = jnp.where(low_part[here, :] == lane_id, 1.0, 0.0).astype(BF16)
            left = jnp.concatenate([left_high, left_low], axis=0)
            summed = lax.dot_general(left, right, NT, preferred_element_type=F32)
            summed = summed[:high_count * GROUP] + summed[high_count * GROUP:]
            for k in range(high_count):
                spread[pl.ds(pl.multiple_of(group * GROUP, GROUP), GROUP), k * LANES:(k + 1) * LANES] = (
                    summed[k * GROUP:(k + 1) * GROUP, :]
                )
            return unused

        lax.fori_loop(0, groups, one, 0, unroll=8)
        split[...] = spread[...].astype(BF16)

    angular = fa[:, 0:1] * aw[0:1, :] + fa[:, 1:2] * aw[1:2, :]
    total = jnp.where(info[FIRST] == 1, angular, 0.0)
    if whole:
        total += jnp.dot(split[:, :whole], table[:whole, :], preferred_element_type=F32)
    if rest:
        edge[...] = jnp.zeros(edge.shape, BF16)
        edge[:rest, :] = table[whole:, :]
        total += jnp.dot(split[:, whole:], edge[...], preferred_element_type=F32)
    out[...] = total.astype(BF16)


def lookup_sum(table, seg_index, seg_amp, field_angle, angle_weight, info):
    rows, width = table.shape
    samples, active = seg_index.shape
    groups, lanes = samples // GROUP, GROUP * active
    columns = -(-rows // LANES) * LANES
    block = min(width, 256)
    small = pl.BlockSpec((groups, lanes), lambda n, info: (0, 0))
    return pl.pallas_call(
        lookup_kernel,
        grid_spec=pltpu.PrefetchScalarGridSpec(
            num_scalar_prefetch=1,
            grid=(width // block,),
            in_specs=[
                small,
                small,
                pl.BlockSpec((samples, 2), lambda n, info: (0, 0)),
                pl.BlockSpec((2, block), lambda n, info: (0, n)),
                pl.BlockSpec((rows, block), lambda n, info: (0, n)),
            ],
            out_specs=pl.BlockSpec((samples, block), lambda n, info: (0, n)),
            scratch_shapes=[
                pltpu.VMEM((groups, lanes), jnp.int32),
                pltpu.VMEM((groups, lanes), jnp.int32),
                pltpu.VMEM((groups, lanes), F32),
                pltpu.VMEM((groups, lanes), F32),
                pltpu.VMEM((samples, columns), F32),
                pltpu.VMEM((samples, columns), BF16),
                pltpu.VMEM((LANES, block), BF16),
            ],
        ),
        out_shape=jax.ShapeDtypeStruct((samples, width), BF16),
        compiler_params=params(),
        cost_estimate=costs(10 * samples * rows * width, 2 * rows * width),
        name="lookup_sum",
    )(info, seg_index.reshape(groups, lanes), seg_amp.reshape(groups, lanes), field_angle, angle_weight, table)


NT = (((1,), (1,)), ((), ()))


def cuts(rows):
    return [rows // 8 * 3, rows - rows // 8 * 3]


def slopes_kernel(info, pre, target, after, slope, closing):
    act, pullback = jax.vjp(jax.nn.gelu, pre[0, 0].astype(F32))
    slope[...] = pullback(jnp.ones_like(act))[0]
    closing[...] = ((act - target[...].astype(F32)) * slope[...]).astype(BF16)


def slopes(stash_pre, target, info, after):
    rows, width = target.shape
    block = min(rows, 64)
    span = pl.BlockSpec((block, width), lambda n, info: (n, 0))
    return pl.pallas_call(
        slopes_kernel,
        grid_spec=pltpu.PrefetchScalarGridSpec(
            num_scalar_prefetch=1,
            grid=(rows // block,),
            in_specs=[
                pl.BlockSpec((1, 1, block, width), lambda n, info: (0, info[SLOT], n, 0)),
                span,
                ANYWHERE,
            ],
            out_specs=[span, span],
        ),
        out_shape=[jax.ShapeDtypeStruct((rows, width), F32), jax.ShapeDtypeStruct((rows, width), BF16)],
        compiler_params=params(),
        cost_estimate=costs(8000 * rows * width, 10 * rows * width),
        name="slopes",
    )(info, stash_pre, target, after)


def first_terms_kernel(info, came, slope, closing, first, second, grad, *outs):
    @pl.when(pl.program_id(0) == 0)
    def differentiate():
        grad[...] = jnp.where(info[LAST] == 1, closing[...], (came[...].astype(F32) * slope[...]).astype(BF16))

    cut = outs[0].shape[0]
    for block, (upper, lower) in zip((first, second), (outs[:2], outs[2:])):
        term = lax.dot_general(grad[...], block[...], NT, preferred_element_type=F32).astype(BF16)
        upper[...] = term[:cut]
        lower[...] = term[cut:]


def first_terms(came, slope, closing, weight, info, at):
    rows, width = came.shape
    block = min(width, 256)
    steps = width // block
    pieces = cuts(rows) * 2
    shapes = [jax.ShapeDtypeStruct((piece, width), BF16) for piece in pieces]
    whole = pl.BlockSpec((rows, width), lambda n, info: (0, 0))
    out_specs = [pl.BlockSpec((piece, block), lambda n, info: (0, n)) for piece in pieces]
    return pl.pallas_call(
        first_terms_kernel,
        grid_spec=pltpu.PrefetchScalarGridSpec(
            num_scalar_prefetch=1,
            grid=(steps,),
            in_specs=[
                whole,
                whole,
                whole,
                pl.BlockSpec((block, width), lambda n, info: (info[at + 1] * steps + n, 0)),
                pl.BlockSpec((block, width), lambda n, info: (info[at] * steps + n, 0)),
            ],
            out_specs=[whole] + out_specs,
        ),
        out_shape=[jax.ShapeDtypeStruct((rows, width), BF16)] + shapes,
        compiler_params=params(),
        cost_estimate=costs(4 * rows * width * width, 4 * width * width + 6 * rows * width),
        name="gradient_terms",
    )(info, came, slope, closing, weight, weight)


def terms_kernel(info, grad, first, second, after, later, first_out, second_out):
    first_out[...] = lax.dot_general(grad[...], first[...], NT, preferred_element_type=F32).astype(BF16)
    second_out[...] = lax.dot_general(grad[...], second[...], NT, preferred_element_type=F32).astype(BF16)


def terms(grad, weight, info, at, after, later):
    rows, width = grad.shape
    block = min(width, 512)
    steps = width // block
    shape = jax.ShapeDtypeStruct((rows, width), BF16)
    out_spec = pl.BlockSpec((rows, block), lambda n, info: (0, n))
    return pl.pallas_call(
        terms_kernel,
        grid_spec=pltpu.PrefetchScalarGridSpec(
            num_scalar_prefetch=1,
            grid=(steps,),
            in_specs=[
                pl.BlockSpec((rows, width), lambda n, info: (0, 0)),
                pl.BlockSpec((block, width), lambda n, info: (info[at + 1] * steps + n, 0)),
                pl.BlockSpec((block, width), lambda n, info: (info[at] * steps + n, 0)),
                ANYWHERE,
                ANYWHERE,
            ],
            out_specs=[out_spec, out_spec],
        ),
        out_shape=[shape, shape],
        compiler_params=params(),
        cost_estimate=costs(0, 0),
        name="input_terms",
    )(info, grad, weight, weight, after, later)


def forward_kernel(finish, count, info, *refs):
    pieces, blocks, carry, out = refs[:count], refs[count:2 * count], refs[2 * count], refs[-1]
    total = carry[...]
    for piece, block in zip(pieces, blocks):
        total += jnp.dot(piece[...], block[...], preferred_element_type=F32)
    if finish:
        total = jax.nn.gelu(total)
    out[...] = total.astype(out.dtype)


def forward_step(pieces, ats, weight, info, carry, rows, h, finish, before):
    half, width = pieces[0].shape
    count = len(pieces)
    block = min(width, 512)
    piece = pl.BlockSpec((half, width), lambda n, info: (0, 0))
    out_rows, place = (rows, h * (rows - half)) if finish else (half, 0)
    return pl.pallas_call(
        functools.partial(forward_kernel, finish, count),
        grid_spec=pltpu.PrefetchScalarGridSpec(
            num_scalar_prefetch=1,
            grid=(width // block,),
            in_specs=[piece] * count
            + [pl.BlockSpec((width, block), functools.partial(lambda at, n, info: (info[at], n), at)) for at in ats]
            + [pl.BlockSpec((carry.shape[0], block), lambda n, info: (0, n)), ANYWHERE],
            out_specs=pl.BlockSpec(
                (pl.Element(half), pl.Element(block)), lambda n, info: (place, pl.multiple_of(n * block, block))
            ),
        ),
        out_shape=jax.ShapeDtypeStruct((out_rows, width), BF16 if finish else F32),
        input_output_aliases={2 * count + 2: 0} if finish and h else {},
        compiler_params=params(),
        cost_estimate=costs(2 * count * half * width * width, 2 * count * width * width + 8 * half * width),
        name="forward_step",
    )(info, *pieces, *[weight] * count, carry, before)


def step_down(shard, stride):
    sections = lax.axis_size("section")
    return over("section", shard, [(s, s - stride) for s in range(stride, sections, 2 * stride)])


def local(
    sent_act,
    sent_grad,
    stash_in,
    stash_pre,
    layer_weight,
    layer_bias,
    seg_table,
    seg_index,
    seg_amp,
    field_angle,
    angle_weight,
    target,
    sched,
):
    section = lax.axis_index("section")
    sections = lax.axis_size("section")
    me = lax.axis_index("fsdp")
    count = lax.axis_size("fsdp")
    chips = count // CORES
    rows = sent_act.shape[1]
    halves = 2
    cut = rows // 8 * 5
    weight = layer_weight[0]

    numbers = [section * seg_table.shape[0], section == 0, sched[0], section == sections - 1]
    for by in range(chips):
        base = lax.rem(me // CORES + by, chips) * CORES
        core = lax.rem(me, CORES)
        numbers += [base + core, base + 1 - core]
    info = jnp.stack([jnp.asarray(number, jnp.int32) for number in numbers])
    is_first = section == 0
    stashed_in = lax.dynamic_index_in_dim(stash_in[0], sched[0], 0, keepdims=False)
    stashed_full = lax.all_gather(stashed_in, "fsdp", axis=1, tiled=True)

    from_before = over("section", sent_act[0], [(s, s + 1) for s in range(sections - 1)])
    from_next = over("section", sent_grad[0], [(s, s - 1) for s in range(1, sections)])
    rounded = lookup_sum(seg_table, seg_index, seg_amp, field_angle, angle_weight, info)

    received = []
    for by in range(1, chips):
        at = BLOCKS + 2 * by
        if by == 1:
            slope, closing = slopes(stash_pre, target, info, rounded)
            pre_grad, *terms_out = first_terms(from_next, slope, closing, weight, info, at)
            to_other, kept = terms_out[:2], terms_out[2:]
        else:
            to_other, kept = [
                [term[:cuts(rows)[0]], term[cuts(rows)[0]:]]
                for term in terms(pre_grad, weight, info, at, info, info)
            ]
        both = [
            (mine.astype(F32) + swap_cores(other).astype(F32)).astype(BF16)
            for mine, other in zip(kept, to_other)
        ]
        if by == 1:
            token = both[0]
        received.append([to_chip(piece, by) for piece in both])
    grad_bias = jnp.sum(pre_grad.astype(F32), axis=0)

    early = rows // 4 * 3
    near = step_down(rounded[:early], 1)
    near, token, from_before = lax.optimization_barrier((near, token, from_before))
    late = step_down(rounded[early:], 1)
    leaving = [(rounded[:cut].astype(F32) + near[:cut].astype(F32)).astype(BF16)]
    grad_w = lax.dot_general(
        stashed_full, pre_grad, (((0,), (0,)), ((), ())), preferred_element_type=F32
    ).astype(BF16)
    late, grad_w, kept_back = lax.optimization_barrier((late, grad_w, leaving[0]))
    late = jnp.concatenate([near[cut:], late], axis=0)
    leaving.append((rounded[cut:].astype(F32) + late.astype(F32)).astype(BF16))
    stride = 2
    while 2 * stride < sections:
        kept_back = None
        leaving = [(piece.astype(F32) + step_down(piece, stride).astype(F32)).astype(BF16) for piece in leaving]
        stride *= 2
    last = [step_down(leaving[0], stride)]
    last.append(step_down(leaving[1], stride))
    last[0], received[0], grad_w = lax.optimization_barrier((last[0], received[0], grad_w))

    if kept_back is not None:
        leaving[0] = kept_back
    inputs, carries = [], []
    for h in range(halves):
        first_input = (leaving[h].astype(F32) + last[h].astype(F32)).astype(BF16)
        span = slice(cut, rows) if h else slice(0, cut)
        inputs.append(jnp.where(is_first, first_input, from_before[span]))
        carry = forward_step(
            [inputs[h], swap_cores(inputs[h])], [BLOCKS, BLOCKS + 1], weight, info, layer_bias, rows, h, False, info
        )
        if h == 0:
            to_other, kept = terms(pre_grad, weight, info, BLOCKS, inputs[0], token)
            last[1], to_other, grad_bias, carry = lax.optimization_barrier((last[1], to_other, grad_bias, carry))
        carries.append(carry)
    beside = kept.astype(F32) + swap_cores(to_other).astype(F32)
    far = [sum(part[h].astype(F32) for part in received) for h in range(2)]
    grad_in = (beside + jnp.concatenate(far, axis=0)).astype(BF16)
    fwd_out = info
    for h, carry in enumerate(carries):
        for by in range(1, chips):
            at = BLOCKS + 2 * by
            finish = by == chips - 1
            arrived = to_chip(inputs[h], chips - by)
            if h:
                arrived, fwd_out, grad_in = lax.optimization_barrier((arrived, fwd_out, grad_in))
                carry = forward_step([arrived], [at], weight, info, carry, rows, h, False, info)
                carry = forward_step(
                    [swap_cores(arrived)], [at + 1], weight, info, carry, rows, h, finish, fwd_out
                )
            else:
                before = carries[-1] if by == 1 else info
                carry = forward_step(
                    [arrived, swap_cores(arrived)], [at, at + 1], weight, info, carry, rows, h, finish, before
                )
        fwd_out = carry
    return (fwd_out[None], grad_in[None], grad_w[None], grad_bias[None])


def solution(mesh):
    return jax.shard_map(
        local,
        mesh=mesh,
        in_specs=(
            P("section", "groups", "fsdp"),
            P("section", "groups", "fsdp"),
            P("section", None, "groups", "fsdp"),
            P("section", None, "groups", "fsdp"),
            P("section", None, "fsdp"),
            P("section", "fsdp"),
            P("section", "fsdp"),
            P("groups", None),
            P("groups", None),
            P("groups", None),
            P(None, "fsdp"),
            P("groups", "fsdp"),
            P("section"),
        ),
        out_specs=(
            P("section", "groups", "fsdp"),
            P("section", "groups", "fsdp"),
            P("section", "groups", "fsdp"),
            P("section", ("groups", "fsdp")),
        ),
        check_vma=False,
    )
```

```python
import functools

import jax
import jax.numpy as jnp
from jax import lax
from jax.experimental import pallas as pl
from jax.experimental.pallas import tpu as pltpu
from jax.sharding import PartitionSpec as P

F32 = jnp.float32
BF16 = jnp.bfloat16
LANES = 128
GROUP = 8
CORES = 2
ROW, FIRST, SLOT, LAST, BLOCKS = range(5)


def over(axis, shard, pairs):
    return lax.ppermute(shard, axis, pairs)


def swap_cores(shard):
    count = lax.axis_size("fsdp")
    return over("fsdp", shard, [(i, i ^ 1) for i in range(count)])


def to_chip(shard, by):
    count = lax.axis_size("fsdp")
    return over("fsdp", shard, [(i, (i + CORES * by) % count) for i in range(count)])


def costs(flops, moved):
    return pl.CostEstimate(flops=flops, bytes_accessed=moved, transcendentals=0)


ANYWHERE = pl.BlockSpec(memory_space=pl.ANY)


def params():
    return pltpu.CompilerParams(vmem_limit_bytes=16 << 20)


def lookup_kernel(info, idx, amp, fa, aw, table, out, code, low_part, high, low, spread, split, edge):
    rows = table.shape[0]
    whole = rows // LANES * LANES
    rest = rows - whole
    high_count = spread.shape[1] // LANES
    groups, lanes = idx.shape
    per_sample = lanes // GROUP

    @pl.when(pl.program_id(0) == 0)
    def build():
        local_row = idx[...] - info[ROW]
        inside = (local_row >= 0) & (local_row < rows)
        sample = lax.broadcasted_iota(jnp.int32, idx.shape, 1) // per_sample
        code[...] = jnp.where(inside, (local_row // LANES) * GROUP + sample, -1)
        low_part[...] = local_row % LANES
        high[...] = amp[...].astype(BF16).astype(F32)
        low[...] = amp[...] - high[...]
        row_id = lax.broadcasted_iota(jnp.int32, (high_count * GROUP, lanes), 0)
        lane_id = lax.broadcasted_iota(jnp.int32, (LANES, lanes), 0)

        def one(group, unused):
            here = pl.ds(group, 1)
            matched = code[here, :] == row_id
            left_high = jnp.where(matched, high[here, :], 0.0).astype(BF16)
            left_low = jnp.where(matched, low[here, :], 0.0).astype(BF16)
            right = jnp.where(low_part[here, :] == lane_id, 1.0, 0.0).astype(BF16)
            left = jnp.concatenate([left_high, left_low], axis=0)
            summed = lax.dot_general(left, right, NT, preferred_element_type=F32)
            summed = summed[:high_count * GROUP] + summed[high_count * GROUP:]
            for k in range(high_count):
                spread[pl.ds(pl.multiple_of(group * GROUP, GROUP), GROUP), k * LANES:(k + 1) * LANES] = (
                    summed[k * GROUP:(k + 1) * GROUP, :]
                )
            return unused

        lax.fori_loop(0, groups, one, 0, unroll=8)
        split[...] = spread[...].astype(BF16)

    angular = fa[:, 0:1] * aw[0:1, :] + fa[:, 1:2] * aw[1:2, :]
    total = jnp.where(info[FIRST] == 1, angular, 0.0)
    if whole:
        total += jnp.dot(split[:, :whole], table[:whole, :], preferred_element_type=F32)
    if rest:
        edge[...] = jnp.zeros(edge.shape, BF16)
        edge[:rest, :] = table[whole:, :]
        total += jnp.dot(split[:, whole:], edge[...], preferred_element_type=F32)
    out[...] = total.astype(BF16)


def lookup_sum(table, seg_index, seg_amp, field_angle, angle_weight, info):
    rows, width = table.shape
    samples, active = seg_index.shape
    groups, lanes = samples // GROUP, GROUP * active
    columns = -(-rows // LANES) * LANES
    block = min(width, 256)
    small = pl.BlockSpec((groups, lanes), lambda n, info: (0, 0))
    return pl.pallas_call(
        lookup_kernel,
        grid_spec=pltpu.PrefetchScalarGridSpec(
            num_scalar_prefetch=1,
            grid=(width // block,),
            in_specs=[
                small,
                small,
                pl.BlockSpec((samples, 2), lambda n, info: (0, 0)),
                pl.BlockSpec((2, block), lambda n, info: (0, n)),
                pl.BlockSpec((rows, block), lambda n, info: (0, n)),
            ],
            out_specs=pl.BlockSpec((samples, block), lambda n, info: (0, n)),
            scratch_shapes=[
                pltpu.VMEM((groups, lanes), jnp.int32),
                pltpu.VMEM((groups, lanes), jnp.int32),
                pltpu.VMEM((groups, lanes), F32),
                pltpu.VMEM((groups, lanes), F32),
                pltpu.VMEM((samples, columns), F32),
                pltpu.VMEM((samples, columns), BF16),
                pltpu.VMEM((LANES, block), BF16),
            ],
        ),
        out_shape=jax.ShapeDtypeStruct((samples, width), BF16),
        compiler_params=params(),
        cost_estimate=costs(10 * samples * rows * width, 2 * rows * width),
        name="lookup_sum",
    )(info, seg_index.reshape(groups, lanes), seg_amp.reshape(groups, lanes), field_angle, angle_weight, table)


NT = (((1,), (1,)), ((), ()))


def cuts(rows):
    return [rows // 8 * 3, rows - rows // 8 * 3]


def slopes_kernel(info, pre, target, after, slope, closing):
    act, pullback = jax.vjp(jax.nn.gelu, pre[0, 0].astype(F32))
    slope[...] = pullback(jnp.ones_like(act))[0]
    closing[...] = ((act - target[...].astype(F32)) * slope[...]).astype(BF16)


def slopes(stash_pre, target, info, after):
    rows, width = target.shape
    block = min(rows, 64)
    span = pl.BlockSpec((block, width), lambda n, info: (n, 0))
    return pl.pallas_call(
        slopes_kernel,
        grid_spec=pltpu.PrefetchScalarGridSpec(
            num_scalar_prefetch=1,
            grid=(rows // block,),
            in_specs=[
                pl.BlockSpec((1, 1, block, width), lambda n, info: (0, info[SLOT], n, 0)),
                span,
                ANYWHERE,
            ],
            out_specs=[span, span],
        ),
        out_shape=[jax.ShapeDtypeStruct((rows, width), F32), jax.ShapeDtypeStruct((rows, width), BF16)],
        compiler_params=params(),
        cost_estimate=costs(8000 * rows * width, 10 * rows * width),
        name="slopes",
    )(info, stash_pre, target, after)


def first_terms_kernel(info, came, slope, closing, first, second, grad, *outs):
    @pl.when(pl.program_id(0) == 0)
    def differentiate():
        grad[...] = jnp.where(info[LAST] == 1, closing[...], (came[...].astype(F32) * slope[...]).astype(BF16))

    cut = outs[0].shape[0]
    for block, (upper, lower) in zip((first, second), (outs[:2], outs[2:])):
        term = lax.dot_general(grad[...], block[...], NT, preferred_element_type=F32).astype(BF16)
        upper[...] = term[:cut]
        lower[...] = term[cut:]


def first_terms(came, slope, closing, weight, info, at):
    rows, width = came.shape
    block = min(width, 256)
    steps = width // block
    pieces = cuts(rows) * 2
    shapes = [jax.ShapeDtypeStruct((piece, width), BF16) for piece in pieces]
    whole = pl.BlockSpec((rows, width), lambda n, info: (0, 0))
    out_specs = [pl.BlockSpec((piece, block), lambda n, info: (0, n)) for piece in pieces]
    return pl.pallas_call(
        first_terms_kernel,
        grid_spec=pltpu.PrefetchScalarGridSpec(
            num_scalar_prefetch=1,
            grid=(steps,),
            in_specs=[
                whole,
                whole,
                whole,
                pl.BlockSpec((block, width), lambda n, info: (info[at + 1] * steps + n, 0)),
                pl.BlockSpec((block, width), lambda n, info: (info[at] * steps + n, 0)),
            ],
            out_specs=[whole] + out_specs,
        ),
        out_shape=[jax.ShapeDtypeStruct((rows, width), BF16)] + shapes,
        compiler_params=params(),
        cost_estimate=costs(4 * rows * width * width, 4 * width * width + 6 * rows * width),
        name="gradient_terms",
    )(info, came, slope, closing, weight, weight)


def terms_kernel(info, grad, first, second, after, later, first_out, second_out):
    first_out[...] = lax.dot_general(grad[...], first[...], NT, preferred_element_type=F32).astype(BF16)
    second_out[...] = lax.dot_general(grad[...], second[...], NT, preferred_element_type=F32).astype(BF16)


def terms(grad, weight, info, at, after, later):
    rows, width = grad.shape
    block = min(width, 512)
    steps = width // block
    shape = jax.ShapeDtypeStruct((rows, width), BF16)
    out_spec = pl.BlockSpec((rows, block), lambda n, info: (0, n))
    return pl.pallas_call(
        terms_kernel,
        grid_spec=pltpu.PrefetchScalarGridSpec(
            num_scalar_prefetch=1,
            grid=(steps,),
            in_specs=[
                pl.BlockSpec((rows, width), lambda n, info: (0, 0)),
                pl.BlockSpec((block, width), lambda n, info: (info[at + 1] * steps + n, 0)),
                pl.BlockSpec((block, width), lambda n, info: (info[at] * steps + n, 0)),
                ANYWHERE,
                ANYWHERE,
            ],
            out_specs=[out_spec, out_spec],
        ),
        out_shape=[shape, shape],
        compiler_params=params(),
        cost_estimate=costs(0, 0),
        name="input_terms",
    )(info, grad, weight, weight, after, later)


def forward_kernel(finish, count, info, *refs):
    pieces, blocks, carry, out = refs[:count], refs[count:2 * count], refs[2 * count], refs[-1]
    total = carry[...]
    for piece, block in zip(pieces, blocks):
        total += jnp.dot(piece[...], block[...], preferred_element_type=F32)
    if finish:
        total = jax.nn.gelu(total)
    out[...] = total.astype(out.dtype)


def forward_step(pieces, ats, weight, info, carry, rows, h, finish, before):
    half, width = pieces[0].shape
    count = len(pieces)
    block = min(width, 512)
    piece = pl.BlockSpec((half, width), lambda n, info: (0, 0))
    out_rows, place = (rows, h * (rows - half)) if finish else (half, 0)
    return pl.pallas_call(
        functools.partial(forward_kernel, finish, count),
        grid_spec=pltpu.PrefetchScalarGridSpec(
            num_scalar_prefetch=1,
            grid=(width // block,),
            in_specs=[piece] * count
            + [pl.BlockSpec((width, block), functools.partial(lambda at, n, info: (info[at], n), at)) for at in ats]
            + [pl.BlockSpec((carry.shape[0], block), lambda n, info: (0, n)), ANYWHERE],
            out_specs=pl.BlockSpec(
                (pl.Element(half), pl.Element(block)), lambda n, info: (place, pl.multiple_of(n * block, block))
            ),
        ),
        out_shape=jax.ShapeDtypeStruct((out_rows, width), BF16 if finish else F32),
        input_output_aliases={2 * count + 2: 0} if finish and h else {},
        compiler_params=params(),
        cost_estimate=costs(2 * count * half * width * width, 2 * count * width * width + 8 * half * width),
        name="forward_step",
    )(info, *pieces, *[weight] * count, carry, before)


def step_down(shard, stride):
    sections = lax.axis_size("section")
    return over("section", shard, [(s, s - stride) for s in range(stride, sections, 2 * stride)])


def local(
    sent_act,
    sent_grad,
    stash_in,
    stash_pre,
    layer_weight,
    layer_bias,
    seg_table,
    seg_index,
    seg_amp,
    field_angle,
    angle_weight,
    target,
    sched,
):
    section = lax.axis_index("section")
    sections = lax.axis_size("section")
    me = lax.axis_index("fsdp")
    count = lax.axis_size("fsdp")
    chips = count // CORES
    rows = sent_act.shape[1]
    halves = 2
    cut = rows // 16 * 9
    weight = layer_weight[0]

    numbers = [section * seg_table.shape[0], section == 0, sched[0], section == sections - 1]
    for by in range(chips):
        base = lax.rem(me // CORES + by, chips) * CORES
        core = lax.rem(me, CORES)
        numbers += [base + core, base + 1 - core]
    info = jnp.stack([jnp.asarray(number, jnp.int32) for number in numbers])
    is_first = section == 0
    stashed_in = lax.dynamic_index_in_dim(stash_in[0], sched[0], 0, keepdims=False)
    stashed_full = lax.all_gather(stashed_in, "fsdp", axis=1, tiled=True)

    from_before = over("section", sent_act[0], [(s, s + 1) for s in range(sections - 1)])
    from_next = over("section", sent_grad[0], [(s, s - 1) for s in range(1, sections)])
    rounded = lookup_sum(seg_table, seg_index, seg_amp, field_angle, angle_weight, info)

    received = []
    for by in range(1, chips):
        at = BLOCKS + 2 * by
        if by == 1:
            slope, closing = slopes(stash_pre, target, info, rounded)
            pre_grad, *terms_out = first_terms(from_next, slope, closing, weight, info, at)
            to_other, kept = terms_out[:2], terms_out[2:]
        else:
            to_other, kept = [
                [term[:cuts(rows)[0]], term[cuts(rows)[0]:]]
                for term in terms(pre_grad, weight, info, at, info, info)
            ]
        both = [
            (mine.astype(F32) + swap_cores(other).astype(F32)).astype(BF16)
            for mine, other in zip(kept, to_other)
        ]
        if by == 1:
            token = both[0]
        received.append([to_chip(piece, by) for piece in both])
    grad_bias = jnp.sum(pre_grad.astype(F32), axis=0)

    early = rows // 4 * 3
    near = step_down(rounded[:early], 1)
    near, token, from_before = lax.optimization_barrier((near, token, from_before))
    late = step_down(rounded[early:], 1)
    leaving = [(rounded[:cut].astype(F32) + near[:cut].astype(F32)).astype(BF16)]
    grad_w = lax.dot_general(
        stashed_full, pre_grad, (((0,), (0,)), ((), ())), preferred_element_type=F32
    ).astype(BF16)
    late, grad_w, kept_back = lax.optimization_barrier((late, grad_w, leaving[0]))
    late = jnp.concatenate([near[cut:], late], axis=0)
    leaving.append((rounded[cut:].astype(F32) + late.astype(F32)).astype(BF16))
    stride = 2
    while 2 * stride < sections:
        kept_back = None
        leaving = [(piece.astype(F32) + step_down(piece, stride).astype(F32)).astype(BF16) for piece in leaving]
        stride *= 2
    last = [step_down(leaving[0], stride)]
    last.append(step_down(leaving[1], stride))
    last[0], received[0], grad_w, leaving[1] = lax.optimization_barrier((last[0], received[0], grad_w, leaving[1]))

    if kept_back is not None:
        leaving[0] = kept_back
    inputs, carries = [], []
    for h in range(halves):
        first_input = (leaving[h].astype(F32) + last[h].astype(F32)).astype(BF16)
        span = slice(cut, rows) if h else slice(0, cut)
        inputs.append(jnp.where(is_first, first_input, from_before[span]))
        carry = forward_step(
            [inputs[h], swap_cores(inputs[h])], [BLOCKS, BLOCKS + 1], weight, info, layer_bias, rows, h, False, info
        )
        if h == 0:
            to_other, kept = terms(pre_grad, weight, info, BLOCKS, inputs[0], token)
            last[1], to_other, grad_bias = lax.optimization_barrier((last[1], to_other, grad_bias))
        carries.append(carry)
    beside = kept.astype(F32) + swap_cores(to_other).astype(F32)
    far = [sum(part[h].astype(F32) for part in received) for h in range(2)]
    grad_in = (beside + jnp.concatenate(far, axis=0)).astype(BF16)
    fwd_out = info
    for h, carry in enumerate(carries):
        for by in range(1, chips):
            at = BLOCKS + 2 * by
            finish = by == chips - 1
            arrived = to_chip(inputs[h], chips - by)
            if h:
                arrived, fwd_out, grad_in = lax.optimization_barrier((arrived, fwd_out, grad_in))
                carry = forward_step([arrived], [at], weight, info, carry, rows, h, False, info)
                carry = forward_step(
                    [swap_cores(arrived)], [at + 1], weight, info, carry, rows, h, finish, fwd_out
                )
            else:
                before = carries[-1] if by == 1 else info
                carry = forward_step(
                    [arrived, swap_cores(arrived)], [at, at + 1], weight, info, carry, rows, h, finish, before
                )
        fwd_out = carry
    return (fwd_out[None], grad_in[None], grad_w[None], grad_bias[None])


def solution(mesh):
    return jax.shard_map(
        local,
        mesh=mesh,
        in_specs=(
            P("section", "groups", "fsdp"),
            P("section", "groups", "fsdp"),
            P("section", None, "groups", "fsdp"),
            P("section", None, "groups", "fsdp"),
            P("section", None, "fsdp"),
            P("section", "fsdp"),
            P("section", "fsdp"),
            P("groups", None),
            P("groups", None),
            P("groups", None),
            P(None, "fsdp"),
            P("groups", "fsdp"),
            P("section"),
        ),
        out_specs=(
            P("section", "groups", "fsdp"),
            P("section", "groups", "fsdp"),
            P("section", "groups", "fsdp"),
            P("section", ("groups", "fsdp")),
        ),
        check_vma=False,
    )
```
